128 devices in a mesh: tile: 32 (over y, x, core), lev: 4 (over z).
Axes of the slice: x: 4, y: 4, z: 4, core: 2. Of those that a mesh axis runs over, the one named last changes fastest.
Arguments:
- final_adjoint: float32 [32, 768, 4096], P('lev', None, 'tile'), may hold values from -6 to 6
- east_coef: float32 [32, 768, 4096], P('lev', None, 'tile'), may hold values from 0.05 to 0.2
- north_coef: float32 [32, 768, 4096], P('lev', None, 'tile'), may hold values from 0.05 to 0.2
- coriolis_coef: float32 [32, 768, 4096], P('lev', None, 'tile'), may hold values from -0.2 to 0.2
- vertical_coef: float32 [32, 768, 4096], P('lev', None, 'tile'), may hold values from 0 to 0.1
- land_sea: int32 [768, 4096], P(None, 'tile'), may hold values 0 or 1
- counts: int32 [32, 2, 32], P('tile'), may hold values from 32 to 256, as said below
- obs_cell: int32 [32, 2, 32, 256], P('tile'), may hold values from 0 to 98174, as said below
- obs_frac: float32 [32, 2, 32, 2, 256], P('tile'), may hold values from 0 to 1
- innovation: float32 [32, 2, 32, 256], P('tile'), may hold values from -6 to 6
- obs_type: int32 [32, 2, 32, 256], P('tile'), may hold values from 0 to 2
- obs_level: int32 [32, 2, 32, 256], P('tile'), may hold values from 0 to 31
- type_weight: float32 [3], replicated, may hold values from 0.5 to 2
Outputs:
- gradient: float32 [32, 768, 4096], P('lev', None, 'tile')
The draws below stay inside these ranges and needn't reach their ends.
Inputs may be any that keep to these rules, and one draw needn't show every extreme that they name: Slots 0 to counts - 1 of a block hold observations; at each time level one tile, drawn from the seed, receives exactly 256 from every owner. `obs_cell`: row * 128 + column, with the row below 767 and the column below 127.
All inputs are finite; a program needn't handle non-finite values. No bound on the sum of `land_sea` on one device may be relied on, other than what follows from the above.
Results may differ from the reference program's by a relative error of at most 0.00002.
Values sent between devices are 32-bit elements; how exact they have to be, the bound alone decides.
No kernel may reach another device: no remote copies, remote signals or barrier semaphores. Data moves between devices by JAX's collectives and lax.ppermute only.
A program may use at most 128 MiB of HBM per device.

```python
import math
import jax
import jax.numpy as jnp

CX = 128
NY = 768
CAP = 256
STEPS = 2
NX = 4096
LEVELS = 32
N_TILE = 32


def draw_counts(key, part):
    key = jax.random.fold_in(key, 11)
    base_load = jax.random.randint(key, (N_TILE, STEPS, N_TILE), CAP // 8, CAP // 2 + 1)
    hottest = jax.random.randint(jax.random.fold_in(key, 1), (STEPS,), 0, N_TILE)
    busy_tile = jnp.arange(N_TILE)[None, None, :] == hottest[None, :, None]
    return jnp.where(busy_tile, CAP, base_load).astype(jnp.int32)


def draw_obs_cell(key, part):
    key = jax.random.fold_in(key, 23)
    row_pick = jax.random.randint(key, (N_TILE, STEPS, N_TILE, CAP), 0, NY - 1)
    column_pick = jax.random.randint(jax.random.fold_in(key, 1), (N_TILE, STEPS, N_TILE, CAP), 0, CX - 1)
    return (row_pick * CX + column_pick).astype(jnp.int32)


def place_ends(entries, rng, smallest, largest):
    longest = entries.shape.index(max(entries.shape))
    spots = []
    for shift in (0, 1):
        where = [jax.random.randint(jax.random.fold_in(rng, axis), (), 0, length) for axis, length in enumerate(entries.shape)]
        where[longest] = (where[longest] + shift) % entries.shape[longest]
        spots.append(tuple(where))
    return entries.at[spots[0]].set(smallest).at[spots[1]].set(largest)


def levels(rng, shape, split, smallest, largest):
    level, own = 1.0, jax.random.fold_in(rng, 6)
    for position, shards_of in split:
        heights = jnp.exp(jax.random.uniform(jax.random.fold_in(own, position), (shards_of,), jnp.float32, smallest / len(split), largest / len(split)))
        level = level * jnp.repeat(heights, shape[position] // shards_of).reshape([-1 if axis == position else 1 for axis in range(len(shape))])
    return level


def bell_draw(key, dims, spread, bound, pieces=(), kind=jnp.bfloat16):
    drawn = spread * jax.random.normal(key, dims, jnp.float32)
    if pieces:
        drawn = drawn * levels(key, dims, pieces, -0.22, 0.18)
    return jnp.clip(drawn, -bound, bound).astype(kind)


def setup_inputs(seed: int = 0) -> dict:
    key_list = jax.random.split(jax.random.key(seed), 14)
    return {
        "final_adjoint": bell_draw(key_list[0], (LEVELS, NY, NX), 1.0, 6.0, ((0, 4), (2, 32)), jnp.float32),
        "east_coef": jnp.clip(0.05 + 0.15 * jax.random.uniform(key_list[1], (LEVELS, NY, NX), jnp.float32) ** levels(key_list[1], (LEVELS, NY, NX), ((0, 4), (2, 32)), -0.2, 0.2), 0.05, 0.2),
        "north_coef": jnp.clip(0.05 + 0.15 * jax.random.uniform(key_list[2], (LEVELS, NY, NX), jnp.float32) ** levels(key_list[2], (LEVELS, NY, NX), ((0, 4), (2, 32)), -0.2, 0.2), 0.05, 0.2),
        "coriolis_coef": jnp.clip(jax.random.uniform(key_list[3], (LEVELS, NY, NX), jnp.float32, -0.2, 0.2) * levels(key_list[3], (LEVELS, NY, NX), ((0, 4), (2, 32)), -0.4, 0.0), -0.2, 0.2),
        "vertical_coef": jnp.clip(0.1 * jax.random.uniform(key_list[4], (LEVELS, NY, NX), jnp.float32) ** levels(key_list[4], (LEVELS, NY, NX), ((0, 4), (2, 32)), -0.2, 0.2), 0.0, 0.1),
        "land_sea": place_ends((jax.random.randint(key_list[5], (NY, NX), 0, 5) < 4).astype(jnp.int32), jax.random.fold_in(key_list[5], 1), 0, 1),
        "counts": draw_counts(jax.random.fold_in(key_list[13], 71), 0),
        "obs_cell": draw_obs_cell(jax.random.fold_in(key_list[13], 71), 0),
        "obs_frac": jnp.clip(1.0 * jax.random.uniform(key_list[8], (N_TILE, STEPS, N_TILE, 2, CAP), jnp.float32) ** levels(key_list[8], (N_TILE, STEPS, N_TILE, 2, CAP), ((0, 32),), -0.2, 0.2), 0.0, 1.0),
        "innovation": bell_draw(key_list[9], (N_TILE, STEPS, N_TILE, CAP), 1.0, 6.0, ((0, 32),), jnp.float32),
        "obs_type": place_ends(jax.random.randint(key_list[10], (N_TILE, STEPS, N_TILE, CAP), 0, 3), jax.random.fold_in(key_list[10], 1), 0, 2).astype(jnp.int32),
        "obs_level": place_ends(jax.random.randint(key_list[11], (N_TILE, STEPS, N_TILE, CAP), 0, LEVELS), jax.random.fold_in(key_list[11], 1), 0, LEVELS - 1).astype(jnp.int32),
        "type_weight": jnp.clip(jnp.exp(jax.random.uniform(key_list[12], (3,), jnp.float32, math.log(0.5), math.log(2.0))), 0.5, 2.0),
    }


ALTIMETRY = 0.25


def forcing(counts, obs_cell, obs_frac, innovation, obs_type, obs_level, type_weight, time_level):
    slots = innovation.shape[-1]
    live_slot = jnp.arange(slots).astype(jnp.int32)[None, None, :] < counts[:, time_level, :, None]
    obs_kinds = obs_type[:, time_level]
    type_scale = jnp.zeros(obs_kinds.shape, jnp.float32)
    for kind_code in range(3):
        type_scale = type_scale + jnp.where(obs_kinds == kind_code, type_weight[kind_code], 0.0)
    residual = type_scale * innovation[:, time_level] * live_slot.astype(jnp.float32)
    east_frac = obs_frac[:, time_level, :, 0]
    north_frac = obs_frac[:, time_level, :, 1]
    values = jnp.stack([(1.0 - east_frac) * (1.0 - north_frac), east_frac * (1.0 - north_frac),
                        (1.0 - east_frac) * north_frac, east_frac * north_frac], 2) * residual[:, :, None]
    base_cells = obs_cell[:, time_level]
    tile_ids = jnp.arange(N_TILE).astype(jnp.int32)[None, :, None]
    base_flat = (base_cells // CX) * NX + tile_ids * CX + base_cells % CX
    target = jnp.where(obs_kinds == 1, obs_level[:, time_level], jnp.where(obs_kinds == 0, LEVELS, LEVELS + 1))
    offsets = jnp.array([0, 1, NX, NX + 1]).astype(jnp.int32)
    flat_index = (target * (NY * NX) + base_flat)[:, :, None, :] + offsets[None, None, :, None]
    flat_sum = jnp.zeros(((LEVELS + 2) * NY * NX,), jnp.float32)
    flat_sum = flat_sum.at[flat_index.reshape(-1).astype(jnp.int32)].add(values.reshape(-1))
    planes = flat_sum.reshape(LEVELS + 2, NY, NX)
    result = planes[:LEVELS] + ALTIMETRY * planes[LEVELS][None]
    return result.at[0].add(planes[LEVELS + 1])


def adjoint_step(adjoint, sea_mask, east_coef, north_coef, coriolis_coef, vertical_coef):
    masked = sea_mask[None] * adjoint
    east_part = east_coef * masked
    east_west = jnp.roll(east_part, -1, axis=2) + jnp.roll(east_part, 1, axis=2) - 2.0 * east_part
    north_part = north_coef * masked
    zero_row = jnp.zeros_like(north_part[:, :1])
    across = (jnp.concatenate([north_part[:, 1:], zero_row], 1)
              + jnp.concatenate([zero_row, north_part[:, :-1]], 1) - 2.0 * north_part)
    coriolis_part = coriolis_coef * masked
    skew_term = jnp.roll(coriolis_part, -1, axis=2) - jnp.roll(coriolis_part, 1, axis=2)
    vertical = vertical_coef * masked
    below_sum = jnp.flip(jnp.cumsum(jnp.flip(vertical, 0), 0), 0)
    return masked + east_west + across - skew_term + below_sum


def reference(final_adjoint, east_coef, north_coef, coriolis_coef, vertical_coef, land_sea, counts,
              obs_cell, obs_frac, innovation, obs_type, obs_level, type_weight):
    sea_mask = land_sea.astype(jnp.float32)
    late = forcing(counts, obs_cell, obs_frac, innovation, obs_type, obs_level, type_weight, 1)
    adjoint = adjoint_step(final_adjoint + late, sea_mask, east_coef, north_coef, coriolis_coef, vertical_coef)
    early = forcing(counts, obs_cell, obs_frac, innovation, obs_type, obs_level, type_weight, 0)
    return adjoint_step(adjoint + early, sea_mask, east_coef, north_coef, coriolis_coef, vertical_coef)
```

```python
import jax
import jax.numpy as jnp
from jax import lax
from jax.experimental import pallas as pl
from jax.experimental.pallas import tpu as pltpu
from jax.sharding import PartitionSpec as P

LANES = 128
ROWS = 768
BAND = 8
CAP = 256
OWNERS = 32
BLOCK = 24
CHUNK = 32
ACCS = 4
PLANES = BAND + 1
LIMIT = 60 << 20
VMEM = pltpu.VMEM
SMEM = pltpu.SMEM
F32 = jnp.float32


def lane_ids():
    return lax.broadcasted_iota(jnp.int32, (8, LANES), 1)


def prepare(band, weight, counts, cell, frac, innovation, kind, level, out):
    z = band[0]
    ids = lax.broadcasted_iota(jnp.int32, (OWNERS, LANES), 1)
    for s in range(2):
        own = lax.broadcasted_iota(jnp.int32, (OWNERS, OWNERS), 0)
        other = lax.broadcasted_iota(jnp.int32, (OWNERS, OWNERS), 1)
        row = jnp.broadcast_to(counts[0, s : s + 1, :].astype(F32), (OWNERS, OWNERS))
        count = jnp.sum(jnp.where(own == other, row, 0.0), 1, keepdims=True)
        out[pl.ds(20 + s, OWNERS, stride=BLOCK), :] = jnp.broadcast_to(count, (OWNERS, LANES))
        for h in range(2):
            part = slice(h * LANES, (h + 1) * LANES)
            t = kind[0, s, :, part]
            at = cell[0, s, :, part]
            scale = jnp.where(t == 0, weight[0], jnp.where(t == 1, weight[1], weight[2]))
            live = (ids + h * LANES).astype(F32) < count
            residual = jnp.where(live, scale * innovation[0, s, :, part], 0.0)
            local = level[0, s, :, part] - z * BAND
            here = (t == 1) & (local >= 0) & (local < BAND)
            keep = (t == 0) | here | ((t == 2) & (z == 0))
            residual = jnp.where(keep, residual, 0.0)
            residual = jnp.where(t == 0, 0.25 * residual, residual)
            target = jnp.where(t == 0, BAND, jnp.where(here, local, 0))
            east = frac[0, s, :, 0, part]
            north = frac[0, s, :, 1, part]
            index = target * ROWS + lax.shift_right_logical(at, 7)
            column = lax.bitwise_and(at, LANES - 1)
            first = s * 8 + h * 4
            values = (column.astype(F32), east, residual * (1.0 - north), residual * north)
            for j, value in enumerate(values):
                out[pl.ds(first + j, OWNERS, stride=BLOCK), :] = value
            out[pl.ds(16 + s * 2 + h, OWNERS, stride=BLOCK), :] = index.astype(F32)
        out[pl.ds(22 + s, OWNERS, stride=BLOCK), :] = jnp.zeros((OWNERS, LANES), F32)


def spread(s, places, slots, table, pairs, bases, accs):
    def turn(o, _):
        block = slots[pl.ds(o * BLOCK, BLOCK), :].T
        for h in range(2):
            first = s * 8 + h * 4
            table[pl.ds(o * CAP + h * LANES, LANES), 0:4] = block[:, first : first + 4]
        return 0

    lax.fori_loop(0, OWNERS, turn, 0)

    def listing(o, total):
        count = places[o, 4 + s, 0]

        def one(c, total):
            bases[total] = o * CAP + c * CHUNK
            return total + 1

        return lax.fori_loop(0, lax.div(count + (CHUNK - 1), CHUNK), one, total)

    total = lax.fori_loop(0, OWNERS, listing, jnp.int32(0))
    bases[total] = 0
    lanes = lane_ids().astype(F32)

    def build(base):
        made = []
        for g in range(CHUNK // 8):
            block = table[pl.ds(base + 8 * g, 8), :]
            weight = jnp.maximum(0.0, 1.0 - jnp.abs((lanes - block[:, 0:1]) - block[:, 1:2]))
            made.append((weight * block[:, 2:3], weight * block[:, 3:4]))
        return made

    def put(made):
        for g, (south, north) in enumerate(made):
            pairs[pl.ds(16 * g, 8, stride=2), :] = south
            pairs[pl.ds(16 * g + 1, 8, stride=2), :] = north

    put(build(pl.multiple_of(bases[0], CHUNK)))

    def step(i, _):
        made = build(pl.multiple_of(bases[i + 1], CHUNK))
        base = bases[i]
        owner = lax.shift_right_logical(base, 8)
        half = lax.bitwise_and(lax.shift_right_logical(base, 7), 1) + 2 * s
        lane = lax.bitwise_and(base, LANES - 1)
        for j in range(CHUNK):
            acc = accs[j % len(accs)]
            r = places[owner, half, lane + j]
            acc[pl.ds(r, 2), :] = acc[pl.ds(r, 2), :] + pairs[pl.ds(2 * j, 2), :]
        put(made)
        return 0

    lax.fori_loop(0, total, step, 0)


def clear(ref, start, rows):
    def one(i, _):
        ref[pl.ds(pl.multiple_of(start + i * 64, 8), 64), :] = jnp.zeros((64, LANES), F32)
        return 0

    lax.fori_loop(0, rows // 64, one, 0)


def total_of(accs, plane, at):
    value = accs[0][pl.ds(plane * ROWS + at, 8), :]
    for acc in accs[1:]:
        value = value + acc[pl.ds(plane * ROWS + at, 8), :]
    return value


def edge_columns(into, lanes, k, value):
    rolled = pltpu.roll(value, 2 * k + 1, 1)
    return jnp.where((lanes == 2 * k) | (lanes == 2 * k + 1), rolled, into)


def send_edges(edges, turned, to_west, to_east):
    for b in range(ROWS // LANES):
        part = slice(b * LANES, (b + 1) * LANES)
        turned[b * 16 : b * 16 + 16, :] = edges[part, :].T[0:16, :]
        to_west[:, part] = turned[pl.ds(b * 16 + 1, BAND, stride=2), :]
        to_east[:, part] = turned[pl.ds(b * 16, BAND, stride=2), :]


def rims(east, coriolis, out):
    lanes = lane_ids()

    def one(i, _):
        at = pl.multiple_of(i * 8, 8)
        value = jnp.zeros((8, LANES), F32)
        for k in range(BAND):
            e = east[k, pl.ds(at, 8), :]
            c = coriolis[k, pl.ds(at, 8), :]
            value = edge_columns(value, lanes, k, jnp.where(lanes == 0, e - c, e + c))
        out[pl.ds(at, 8), :] = value
        return 0

    lax.fori_loop(0, ROWS // 8, one, 0, unroll=2)


def late_kernel(
    places, slots, final, land, vertical, rim, masked, sums, to_west, to_east,
    table, pairs, bases, edges, turned, sem, *accs,
):
    copies = [
        pltpu.make_async_copy(final.at[k], accs[0].at[pl.ds(k * ROWS, ROWS)], sem.at[k])
        for k in range(BAND)
    ]
    for copy in copies:
        copy.start()
    clear(accs[0], BAND * ROWS, ROWS)
    for acc in accs[1:]:
        clear(acc, 0, PLANES * ROWS)
    for copy in copies:
        copy.wait()
    spread(1, places, slots, table, pairs, bases, accs)
    lanes = lane_ids()

    def one(i, _):
        at = pl.multiple_of(i * 8, 8)
        sea = land[pl.ds(at, 8), :].astype(F32)
        shared = total_of(accs, BAND, at)
        total = jnp.zeros((8, LANES), F32)
        edge = jnp.zeros((8, LANES), F32)
        for k in range(BAND):
            m = sea * (total_of(accs, k, at) + shared)
            masked[k, pl.ds(at, 8), :] = m
            total = total + vertical[k, pl.ds(at, 8), :] * m
            edge = edge_columns(edge, lanes, k, m)
        sums[pl.ds(at, 8), :] = total
        edges[pl.ds(at, 8), :] = edge * rim[pl.ds(at, 8), :]
        return 0

    lax.fori_loop(0, ROWS // 8, one, 0)
    send_edges(edges, turned, to_west, to_east)


def stencil(masked, east, north, coriolis, vertical, flow, give):
    for k in range(BAND):
        flow[k, 0:8, :] = jnp.zeros((8, LANES), F32)
        flow[k, ROWS + 8 : ROWS + 16, :] = jnp.zeros((8, LANES), F32)

    def first(i, _):
        at = pl.multiple_of(i * 8, 8)
        for k in range(BAND):
            value = north[k, pl.ds(at, 8), :] * masked[k, pl.ds(at, 8), :]
            flow[k, pl.ds(pl.multiple_of(at + 8, 8), 8), :] = value
        return 0

    lax.fori_loop(0, ROWS // 8, first, 0, unroll=2)
    lanes = lane_ids()

    def second(i, _):
        at = pl.multiple_of(i * 8, 8)
        below = jnp.zeros((8, LANES), F32)
        for k in reversed(range(BAND)):
            m = masked[k, pl.ds(at, 8), :]
            e = east[k, pl.ds(at, 8), :] * m
            c = coriolis[k, pl.ds(at, 8), :] * m
            below = below + vertical[k, pl.ds(at, 8), :] * m
            ahead = jnp.where(lanes == LANES - 1, 0.0, pltpu.roll(e - c, LANES - 1, 1))
            behind = jnp.where(lanes == 0, 0.0, pltpu.roll(e + c, 1, 1))
            across = (
                flow[k, pl.ds(at + 7, 8), :]
                + flow[k, pl.ds(at + 9, 8), :]
                - 2.0 * flow[k, pl.ds(pl.multiple_of(at + 8, 8), 8), :]
            )
            give(k, at, m + (ahead + behind - 2.0 * e) + across + below)
        return 0

    lax.fori_loop(0, ROWS // 8, second, 0)


def early_kernel(
    places, slots, masked, east, north, coriolis, vertical, out,
    flow, table, pairs, bases, m_s, e_s, n_s, c_s, v_s, sem, *accs,
):
    copies = [
        pltpu.make_async_copy(source, target, sem.at[j])
        for j, (source, target) in enumerate(
            ((masked, m_s), (east, e_s), (north, n_s), (coriolis, c_s), (vertical, v_s))
        )
    ]
    for copy in copies:
        copy.start()
    for acc in accs:
        clear(acc, 0, PLANES * ROWS)
    spread(0, places, slots, table, pairs, bases, accs)
    for copy in copies:
        copy.wait()

    def give(k, at, value):
        out[k, pl.ds(at, 8), :] = value + (total_of(accs, k, at) + total_of(accs, BAND, at))

    stencil(m_s, e_s, n_s, c_s, v_s, flow, give)


def local_kernel(masked, east, north, coriolis, vertical, out, flow):
    def give(k, at, value):
        out[k, pl.ds(at, 8), :] = value

    stencil(masked, east, north, coriolis, vertical, flow, give)


def take_edges(from_east, from_west, turned, placed):
    for b in range(ROWS // LANES):
        part = slice(b * LANES, (b + 1) * LANES)
        turned[pl.ds(b * 16, BAND, stride=2), :] = from_east[:, part]
        turned[pl.ds(b * 16 + 1, BAND, stride=2), :] = from_west[:, part]
        placed[part, 0:16] = turned[b * 16 : b * 16 + 16, :].T


def rim_of(placed, lanes, k, at):
    rolled = pltpu.roll(placed[pl.ds(at, 8), :], LANES - 1 - 2 * k, 1)
    return jnp.where((lanes == 0) | (lanes == LANES - 1), rolled, 0.0)


def middle_kernel(
    field, one_up, two_up, three_up, from_east, from_west, land, vertical, rim,
    masked, sums, to_west, to_east, placed, edges, turned,
):
    take_edges(from_east, from_west, turned, placed)
    lanes = lane_ids()

    def one(i, _):
        at = pl.multiple_of(i * 8, 8)
        rows = pl.ds(at, 8)
        sea = land[rows, :].astype(F32)
        higher = one_up[rows, :] + two_up[rows, :] + three_up[rows, :]
        total = jnp.zeros((8, LANES), F32)
        edge = jnp.zeros((8, LANES), F32)
        for k in range(BAND):
            m = sea * (field[k, rows, :] + higher + rim_of(placed, lanes, k, at))
            masked[k, rows, :] = m
            total = total + vertical[k, rows, :] * m
            edge = edge_columns(edge, lanes, k, m)
        sums[rows, :] = total
        edges[rows, :] = edge * rim[rows, :]
        return 0

    lax.fori_loop(0, ROWS // 8, one, 0)
    send_edges(edges, turned, to_west, to_east)


def last_kernel(field, one_up, two_up, three_up, from_east, from_west, out, placed, turned):
    take_edges(from_east, from_west, turned, placed)
    lanes = lane_ids()

    def one(i, _):
        at = pl.multiple_of(i * 8, 8)
        rows = pl.ds(at, 8)
        higher = one_up[rows, :] + two_up[rows, :] + three_up[rows, :]
        for k in range(BAND):
            out[k, rows, :] = field[k, rows, :] + higher + rim_of(placed, lanes, k, at)
        return 0

    lax.fori_loop(0, ROWS // 8, one, 0)


def shape(*dims):
    return jax.ShapeDtypeStruct(dims, F32)


def vm(count):
    return [pl.BlockSpec(memory_space=VMEM)] * count


def sm(count):
    return [pl.BlockSpec(memory_space=SMEM)] * count


def far(count):
    return [pl.BlockSpec(memory_space=pl.ANY)] * count


def call(kernel, ins, outs, scratch, moved, *args):
    return pl.pallas_call(
        kernel,
        in_specs=ins,
        out_specs=tuple(vm(len(outs))) if len(outs) > 1 else vm(1)[0],
        out_shape=tuple(outs) if len(outs) > 1 else outs[0],
        scratch_shapes=scratch,
        compiler_params=pltpu.CompilerParams(vmem_limit_bytes=LIMIT),
        cost_estimate=pl.CostEstimate(flops=moved, bytes_accessed=moved, transcendentals=0),
    )(*args)


def from_deeper(part):
    return (
        lax.ppermute(part, "lev", [(3, 2), (2, 1), (1, 0)]),
        lax.ppermute(part, "lev", [(3, 1), (2, 0)]),
        lax.ppermute(part, "lev", [(3, 0)]),
    )


def from_sides(to_west, to_east):
    count = lax.axis_size("tile")
    return (
        lax.ppermute(to_west, "tile", [((i + 1) % count, i) for i in range(count)]),
        lax.ppermute(to_east, "tile", [(i, (i + 1) % count) for i in range(count)]),
    )


def body(
    final_adjoint,
    east_coef,
    north_coef,
    coriolis_coef,
    vertical_coef,
    land_sea,
    counts,
    obs_cell,
    obs_frac,
    innovation,
    obs_type,
    obs_level,
    type_weight,
):
    band = lax.axis_index("lev").astype(jnp.int32).reshape(1)
    field = shape(BAND, ROWS, LANES)
    plane = shape(ROWS, LANES)
    edge = shape(BAND, ROWS)
    send = call(
        prepare, sm(2) + vm(6), [shape(OWNERS * BLOCK, LANES)], [], 1 << 20,
        band, type_weight, counts, obs_cell, obs_frac, innovation, obs_type, obs_level,
    )
    arrived = lax.all_to_all(
        send.reshape(OWNERS, BLOCK, LANES), "tile", split_axis=0, concat_axis=0, tiled=True
    )
    rim = call(rims, vm(2), [plane], [], 7 << 20, east_coef, coriolis_coef)
    places = arrived[:, 16:22, :].astype(jnp.int32)
    slots = arrived.reshape(OWNERS * BLOCK, LANES)
    acc = VMEM((PLANES * ROWS + 8, LANES), F32)
    spread_scratch = [
        VMEM((OWNERS * CAP, LANES), F32),
        VMEM((2 * CHUNK, LANES), F32),
        SMEM((OWNERS * CAP // CHUNK + 1,), jnp.int32),
    ]
    edge_scratch = [VMEM((ROWS, LANES), F32), VMEM((ROWS // 8, LANES), F32)]
    masked, sums, to_west, to_east = call(
        late_kernel, sm(1) + vm(1) + far(1) + vm(3), [field, plane, edge, edge],
        spread_scratch + edge_scratch + [pltpu.SemaphoreType.DMA((BAND,))] + [acc] * ACCS,
        10 << 20,
        places, slots, final_adjoint, land_sea, vertical_coef, rim,
    )
    ups = from_deeper(sums)
    sides = from_sides(to_west, to_east)
    fields = [VMEM((BAND, ROWS, LANES), F32)]
    flow = [VMEM((BAND, ROWS + 16, LANES), F32)]
    first = call(
        early_kernel, sm(1) + vm(1) + far(5), [field],
        flow + spread_scratch + fields * 5 + [pltpu.SemaphoreType.DMA((5,))] + [acc] * ACCS,
        60 << 20,
        places, slots, masked, east_coef, north_coef, coriolis_coef, vertical_coef,
    )
    masked, sums, to_west, to_east = call(
        middle_kernel, vm(9), [field, plane, edge, edge],
        [VMEM((ROWS, LANES), F32)] + edge_scratch, 12 << 20,
        first, *ups, *sides, land_sea, vertical_coef, rim,
    )
    ups = from_deeper(sums)
    sides = from_sides(to_west, to_east)
    second = call(
        local_kernel, vm(5), [field], flow, 18 << 20,
        masked, east_coef, north_coef, coriolis_coef, vertical_coef,
    )
    return call(
        last_kernel, vm(6), [field],
        [VMEM((ROWS, LANES), F32), VMEM((ROWS // 8, LANES), F32)], 7 << 20,
        second, *ups, *sides,
    )


def solution(mesh):
    return jax.shard_map(
        body,
        mesh=mesh,
        in_specs=(
            P("lev", None, "tile"),
            P("lev", None, "tile"),
            P("lev", None, "tile"),
            P("lev", None, "tile"),
            P("lev", None, "tile"),
            P(None, "tile"),
            P("tile", None, None),
            P("tile", None, None, None),
            P("tile", None, None, None, None),
            P("tile", None, None, None),
            P("tile", None, None, None),
            P("tile", None, None, None),
            P(),
        ),
        out_specs=P("lev", None, "tile"),
        check_vma=False,
    )
```

```python
import jax
import jax.numpy as jnp
from jax import lax
from jax.experimental import pallas as pl
from jax.experimental.pallas import tpu as pltpu
from jax.sharding import PartitionSpec as P

LANES = 128
ROWS = 768
BAND = 8
CAP = 256
OWNERS = 32
BLOCK = 24
CHUNK = 32
LATE_ACCS = 8
EARLY_ACCS = 6
STRIP = 32
PARTS = 4
PART = ROWS // PARTS
PLANES = BAND + 1
LIMIT = 60 << 20
VMEM = pltpu.VMEM
SMEM = pltpu.SMEM
F32 = jnp.float32
BF16 = jnp.bfloat16


def lane_ids():
    return lax.broadcasted_iota(jnp.int32, (STRIP, LANES), 1)


def prepare(band, weight, counts, cell, frac, innovation, kind, level, out):
    z = band[0]
    ids = lax.broadcasted_iota(jnp.int32, (OWNERS, LANES), 1)
    for s in range(2):
        own = lax.broadcasted_iota(jnp.int32, (OWNERS, OWNERS), 0)
        other = lax.broadcasted_iota(jnp.int32, (OWNERS, OWNERS), 1)
        row = jnp.broadcast_to(counts[0, s : s + 1, :].astype(F32), (OWNERS, OWNERS))
        count = jnp.sum(jnp.where(own == other, row, 0.0), 1, keepdims=True)
        out[pl.ds(20 + s, OWNERS, stride=BLOCK), :] = jnp.broadcast_to(count, (OWNERS, LANES))
        for h in range(2):
            part = slice(h * LANES, (h + 1) * LANES)
            t = kind[0, s, :, part]
            at = cell[0, s, :, part]
            scale = jnp.where(t == 0, weight[0], jnp.where(t == 1, weight[1], weight[2]))
            live = (ids + h * LANES).astype(F32) < count
            residual = jnp.where(live, scale * innovation[0, s, :, part], 0.0)
            local = level[0, s, :, part] - z * BAND
            here = (t == 1) & (local >= 0) & (local < BAND)
            keep = (t == 0) | here | ((t == 2) & (z == 0))
            residual = jnp.where(keep, residual, 0.0)
            residual = jnp.where(t == 0, 0.25 * residual, residual)
            target = jnp.where(t == 0, BAND, jnp.where(here, local, 0))
            east = frac[0, s, :, 0, part]
            north = frac[0, s, :, 1, part]
            index = target * ROWS + lax.shift_right_logical(at, 7)
            column = lax.bitwise_and(at, LANES - 1)
            first = s * 8 + h * 4
            values = (column.astype(F32), east, residual * (1.0 - north), residual * north)
            for j, value in enumerate(values):
                out[pl.ds(first + j, OWNERS, stride=BLOCK), :] = value
            out[pl.ds(16 + s * 2 + h, OWNERS, stride=BLOCK), :] = index.astype(F32)
        out[pl.ds(22 + s, OWNERS, stride=BLOCK), :] = jnp.zeros((OWNERS, LANES), F32)


def make_pairs(select, pairs, block, half, at):
    high = block.astype(BF16).astype(F32)
    rest = block - high
    middle = rest.astype(BF16).astype(F32)
    parts = jnp.concatenate([high, middle, rest - middle, jnp.zeros_like(block)], 0)
    spread = lax.dot_general(
        parts.astype(BF16), select[half], (((0,), (0,)), ((), ())), preferred_element_type=F32
    )
    column, east, south, north = (
        spread[:, j * LANES : (j + 1) * LANES] for j in range(4)
    )
    lanes = lax.broadcasted_iota(jnp.int32, (LANES, LANES), 1).astype(F32)
    weight = jnp.maximum(0.0, 1.0 - jnp.abs((lanes - column) - east))
    pairs[pl.ds(at, LANES, stride=2), :] = weight * south
    pairs[pl.ds(at + 1, LANES, stride=2), :] = weight * north


def spread(s, far_places, slots, select, pairs, places, sem, accs, first_cleared, ready):
    fetch = pltpu.make_async_copy(far_places, places, sem)
    fetch.start()
    row = lax.broadcasted_iota(jnp.int32, (32, 4 * LANES), 0)
    group = lax.shift_right_logical(lax.broadcasted_iota(jnp.int32, (32, 4 * LANES), 1), 7)
    for h in range(2):
        hit = (lax.bitwise_and(row, 7) == group + 4 * h) & (row < 24)
        select[h] = jnp.where(hit, 1.0, 0.0).astype(BF16)
    share = PLANES * ROWS // OWNERS

    def west(o, _):
        for acc in accs[first_cleared:]:
            acc[pl.ds(pl.multiple_of(o * share, 8), share), :] = jnp.zeros((share, LANES), F32)
        block = slots[pl.ds(pl.multiple_of(o * BLOCK + s * 8, 8), 8), :]
        make_pairs(select, pairs, block, 0, o * 2 * CAP)
        return 0

    lax.fori_loop(0, OWNERS, west, 0, unroll=4)
    fetch.wait()

    def most(o, value):
        return jnp.maximum(value, places[o * 8 * LANES + (4 + s) * LANES])

    @pl.when(lax.fori_loop(0, OWNERS, most, jnp.int32(0), unroll=8) > LANES)
    def _():
        def east(o, _):
            block = slots[pl.ds(pl.multiple_of(o * BLOCK + s * 8, 8), 8), :]
            make_pairs(select, pairs, block, 1, o * 2 * CAP + 2 * LANES)
            return 0

        lax.fori_loop(0, OWNERS, east, 0, unroll=4)

    for copy in ready:
        copy.wait()

    def owner(o, _):
        count = places[o * 8 * LANES + (4 + s) * LANES]

        def step(c, _):
            at = o * 8 * LANES + s * CAP + c * CHUNK
            pair = o * 2 * CAP + c * 2 * CHUNK
            for j in range(CHUNK):
                acc = accs[j % len(accs)]
                r = places[at + j]
                acc[pl.ds(r, 2), :] = acc[pl.ds(r, 2), :] + pairs[pl.ds(pair + 2 * j, 2), :]
            return 0

        return lax.fori_loop(0, lax.div(count + (CHUNK - 1), CHUNK), step, 0)

    lax.fori_loop(0, OWNERS, owner, 0)


def total_of(accs, plane, at):
    value = accs[0][pl.ds(plane * ROWS + at, STRIP), :]
    for acc in accs[1:]:
        value = value + acc[pl.ds(plane * ROWS + at, STRIP), :]
    return value


def edge_columns(into, lanes, k, value):
    rolled = pltpu.roll(value, 2 * k + 1, 1)
    return jnp.where((lanes == 2 * k) | (lanes == 2 * k + 1), rolled, into)


def send_edges(edges, at, turned, to_west, to_east, part):
    turned[...] = edges[pl.ds(at, LANES), :].T[0:16, :]
    to_west[:, part] = turned[pl.ds(1, BAND, stride=2), :]
    to_east[:, part] = turned[pl.ds(0, BAND, stride=2), :]


def rims(east, coriolis, out):
    lanes = lane_ids()
    for r in range(0, LANES, STRIP):
        rows = slice(r, r + STRIP)
        value = jnp.zeros((STRIP, LANES), F32)
        for k in range(BAND):
            e = east[k, rows, :]
            c = coriolis[k, rows, :]
            value = edge_columns(value, lanes, k, jnp.where(lanes == 0, e - c, e + c))
        out[rows, :] = value


def row_part(ref, c):
    return ref.at[:, pl.ds(c * PART, PART), :]


def late_kernel(
    far_places, slots, final, land, vertical, rim, masked, sums, to_west, to_east,
    select, pairs, places, edges, turned, v_s, sem, in_sem, out_sem, *accs,
):
    copies = [
        pltpu.make_async_copy(final.at[k], accs[0].at[pl.ds(k * ROWS, ROWS)], in_sem.at[k])
        for k in range(BAND)
    ]
    copies.append(pltpu.make_async_copy(vertical, v_s, in_sem.at[BAND]))
    for copy in copies:
        copy.start()
    accs[0][pl.ds(BAND * ROWS, ROWS), :] = jnp.zeros((ROWS, LANES), F32)
    spread(1, far_places, slots, select, pairs, places, sem, accs, 1, copies[:BAND])
    copies[BAND].wait()
    lanes = lane_ids()

    def one(i, _):
        at = pl.multiple_of(i * STRIP, STRIP)
        rows = pl.ds(at, STRIP)
        sea = land[rows, :].astype(F32)
        shared = total_of(accs, BAND, at)
        total = jnp.zeros((STRIP, LANES), F32)
        edge = jnp.zeros((STRIP, LANES), F32)
        for k in range(BAND):
            m = sea * (total_of(accs, k, at) + shared)
            accs[0][pl.ds(k * ROWS + at, STRIP), :] = m
            total = total + v_s[k, rows, :] * m
            edge = edge_columns(edge, lanes, k, m)
        sums[rows, :] = total
        edges[rows, :] = edge * rim[rows, :]
        return 0

    leaving = []
    for c in range(PARTS):
        lax.fori_loop(c * PART // STRIP, (c + 1) * PART // STRIP, one, 0)
        for k in range(BAND):
            copy = pltpu.make_async_copy(
                accs[0].at[pl.ds(k * ROWS + c * PART, PART)],
                masked.at[k, pl.ds(c * PART, PART)],
                out_sem.at[c, k],
            )
            copy.start()
            leaving.append(copy)
    for b in range(ROWS // LANES):
        part = slice(b * LANES, (b + 1) * LANES)
        send_edges(edges, b * LANES, turned, to_west, to_east, part)
    for copy in leaving:
        copy.wait()


def fetch_fields(sources, targets, sem):
    copies = []
    for c in range(PARTS):
        row = []
        for j, (source, target) in enumerate(zip(sources, targets)):
            start = c * PART + (8 if target.shape[1] > ROWS else 0)
            copy = pltpu.make_async_copy(
                row_part(source, c), target.at[:, pl.ds(start, PART), :], sem.at[c, j]
            )
            copy.start()
            row.append(copy)
        copies.append(row)
    return copies


def stencil(copies, masked, east, north, coriolis, vertical, added, out, out_sem):
    for k in range(BAND):
        north[k, 0:8, :] = jnp.zeros((8, LANES), F32)
        north[k, ROWS + 8 : ROWS + 16, :] = jnp.zeros((8, LANES), F32)

    def first(i, _):
        at = pl.multiple_of(i * STRIP, STRIP)
        rows = pl.ds(pl.multiple_of(at + 8, 8), STRIP)
        for k in range(BAND):
            north[k, rows, :] = north[k, rows, :] * masked[k, pl.ds(at, STRIP), :]
        return 0

    lanes = lane_ids()

    def second(i, _):
        at = pl.multiple_of(i * STRIP, STRIP)
        rows = pl.ds(at, STRIP)
        below = added(BAND, at)
        for k in reversed(range(BAND)):
            m = masked[k, rows, :]
            e = east[k, rows, :] * m
            c = coriolis[k, rows, :] * m
            below = below + vertical[k, rows, :] * m
            ahead = jnp.where(lanes == LANES - 1, 0.0, pltpu.roll(e - c, LANES - 1, 1))
            behind = jnp.where(lanes == 0, 0.0, pltpu.roll(e + c, 1, 1))
            across = (
                north[k, pl.ds(at + 7, STRIP), :]
                + north[k, pl.ds(at + 9, STRIP), :]
                - 2.0 * north[k, pl.ds(pl.multiple_of(at + 8, 8), STRIP), :]
            )
            value = m + (ahead + behind - 2.0 * e) + across + below
            masked[k, rows, :] = value + added(k, at)
        return 0

    leaving = []
    for c in range(PARTS + 1):
        if c < PARTS:
            for copy in copies[c]:
                copy.wait()
            lax.fori_loop(c * PART // STRIP, (c + 1) * PART // STRIP, first, 0)
        if c > 0:
            lax.fori_loop((c - 1) * PART // STRIP, c * PART // STRIP, second, 0)
            copy = pltpu.make_async_copy(
                row_part(masked, c - 1), row_part(out, c - 1), out_sem.at[c - 1]
            )
            copy.start()
            leaving.append(copy)
    for copy in leaving:
        copy.wait()


def early_kernel(
    far_places, slots, masked, east, north, coriolis, vertical, out,
    select, pairs, places, m_s, e_s, n_s, c_s, v_s, sem, in_sem, out_sem, *accs,
):
    copies = fetch_fields(
        (masked, east, north, coriolis, vertical), (m_s, e_s, n_s, c_s, v_s), in_sem
    )
    spread(0, far_places, slots, select, pairs, places, sem, accs, 0, ())

    def added(plane, at):
        return total_of(accs, plane, at)

    stencil(copies, m_s, e_s, n_s, c_s, v_s, added, out, out_sem)


def local_kernel(
    masked, east, north, coriolis, vertical, out, m_s, e_s, n_s, c_s, v_s, in_sem, out_sem
):
    copies = fetch_fields(
        (masked, east, north, coriolis, vertical), (m_s, e_s, n_s, c_s, v_s), in_sem
    )

    def added(plane, at):
        return jnp.zeros((STRIP, LANES), F32)

    stencil(copies, m_s, e_s, n_s, c_s, v_s, added, out, out_sem)


def take_edges(from_east, from_west, turned, placed):
    turned[pl.ds(0, BAND, stride=2), :] = from_east[...]
    turned[pl.ds(1, BAND, stride=2), :] = from_west[...]
    placed[:, 0:16] = turned[...].T


def rim_of(placed, rows, lanes, k):
    rolled = pltpu.roll(placed[rows, :], LANES - 1 - 2 * k, 1)
    return jnp.where((lanes == 0) | (lanes == LANES - 1), rolled, 0.0)


def middle_kernel(
    field, one_up, two_up, three_up, from_east, from_west, land, vertical, rim,
    masked, sums, to_west, to_east, placed, edges, turned,
):
    take_edges(from_east, from_west, turned, placed)
    lanes = lane_ids()
    for r in range(0, LANES, STRIP):
        rows = slice(r, r + STRIP)
        sea = land[rows, :].astype(F32)
        higher = one_up[rows, :] + two_up[rows, :] + three_up[rows, :]
        total = jnp.zeros((STRIP, LANES), F32)
        edge = jnp.zeros((STRIP, LANES), F32)
        for k in range(BAND):
            m = sea * (field[k, rows, :] + higher + rim_of(placed, rows, lanes, k))
            masked[k, rows, :] = m
            total = total + vertical[k, rows, :] * m
            edge = edge_columns(edge, lanes, k, m)
        sums[rows, :] = total
        edges[rows, :] = edge * rim[rows, :]
    send_edges(edges, 0, turned, to_west, to_east, slice(None))


def last_kernel(field, one_up, two_up, three_up, from_east, from_west, out, placed, turned):
    take_edges(from_east, from_west, turned, placed)
    lanes = lane_ids()
    for r in range(0, LANES, STRIP):
        rows = slice(r, r + STRIP)
        higher = one_up[rows, :] + two_up[rows, :] + three_up[rows, :]
        for k in range(BAND):
            out[k, rows, :] = field[k, rows, :] + higher + rim_of(placed, rows, lanes, k)


def shape(*dims):
    return jax.ShapeDtypeStruct(dims, F32)


def vm(count):
    return [pl.BlockSpec(memory_space=VMEM)] * count


def sm(count):
    return [pl.BlockSpec(memory_space=SMEM)] * count


def far(count):
    return [pl.BlockSpec(memory_space=pl.ANY)] * count


def fields_by_rows(count):
    return [pl.BlockSpec((BAND, LANES, LANES), lambda i: (0, i, 0))] * count


def planes_by_rows(count):
    return [pl.BlockSpec((LANES, LANES), lambda i: (i, 0))] * count


def edges_by_rows(count):
    return [pl.BlockSpec((BAND, LANES), lambda i: (0, i))] * count


def call(kernel, ins, outs, shapes, scratch, moved, *args, grid=()):
    many = len(outs) > 1
    return pl.pallas_call(
        kernel,
        grid=grid,
        in_specs=ins,
        out_specs=tuple(outs) if many else outs[0],
        out_shape=tuple(shapes) if many else shapes[0],
        scratch_shapes=scratch,
        compiler_params=pltpu.CompilerParams(vmem_limit_bytes=LIMIT),
        cost_estimate=pl.CostEstimate(flops=moved, bytes_accessed=moved, transcendentals=0),
    )(*args)


def from_deeper(part):
    return (
        lax.ppermute(part, "lev", [(3, 2), (2, 1), (1, 0)]),
        lax.ppermute(part, "lev", [(3, 1), (2, 0)]),
        lax.ppermute(part, "lev", [(3, 0)]),
    )


def from_sides(to_west, to_east):
    count = lax.axis_size("tile")
    return (
        lax.ppermute(to_west, "tile", [((i + 1) % count, i) for i in range(count)]),
        lax.ppermute(to_east, "tile", [(i, (i + 1) % count) for i in range(count)]),
    )


def body(
    final_adjoint,
    east_coef,
    north_coef,
    coriolis_coef,
    vertical_coef,
    land_sea,
    counts,
    obs_cell,
    obs_frac,
    innovation,
    obs_type,
    obs_level,
    type_weight,
):
    band = lax.axis_index("lev").astype(jnp.int32).reshape(1)
    field = shape(BAND, ROWS, LANES)
    plane = shape(ROWS, LANES)
    edge = shape(BAND, ROWS)
    strips = (ROWS // LANES,)
    dma = pltpu.SemaphoreType.DMA
    send = call(
        prepare, sm(2) + vm(6), vm(1), [shape(OWNERS * BLOCK, LANES)], [], 1 << 20,
        band, type_weight, counts, obs_cell, obs_frac, innovation, obs_type, obs_level,
    )
    arrived = lax.all_to_all(
        send.reshape(OWNERS, BLOCK, LANES), "tile", split_axis=0, concat_axis=0, tiled=True
    )
    rim = call(
        rims, fields_by_rows(2), planes_by_rows(1), [plane], [], 7 << 20,
        east_coef, coriolis_coef, grid=strips,
    )
    places = arrived[:, 16:24, :].astype(jnp.int32).reshape(-1)
    slots = arrived.reshape(OWNERS * BLOCK, LANES)
    acc = VMEM((PLANES * ROWS + 8, LANES), F32)
    spread_scratch = [
        VMEM((2, 32, 4 * LANES), BF16),
        VMEM((OWNERS * CAP * 2, LANES), F32),
        SMEM((OWNERS * 8 * LANES,), jnp.int32),
    ]
    turned = [VMEM((2 * BAND, LANES), F32)]
    masked, sums, to_west, to_east = call(
        late_kernel, far(1) + vm(1) + far(1) + vm(1) + far(1) + vm(1), far(1) + vm(3),
        [field, plane, edge, edge],
        spread_scratch + [VMEM((ROWS, LANES), F32)] + turned + [VMEM((BAND, ROWS, LANES), F32)]
        + [dma, dma((BAND + 1,)), dma((PARTS, BAND))] + [acc] * LATE_ACCS,
        10 << 20,
        places, slots, final_adjoint, land_sea, vertical_coef, rim,
    )
    ups = from_deeper(sums)
    sides = from_sides(to_west, to_east)
    stored = VMEM((BAND, ROWS, LANES), F32)
    wide = VMEM((BAND, ROWS + 16, LANES), F32)
    stencil_scratch = [stored, stored, wide, stored, stored]
    stencil_sems = [dma((PARTS, 5)), dma((PARTS,))]
    first = call(
        early_kernel, far(1) + vm(1) + far(5), far(1), [field],
        spread_scratch + stencil_scratch + [dma] + stencil_sems + [acc] * EARLY_ACCS,
        40 << 20,
        places, slots, masked, east_coef, north_coef, coriolis_coef, vertical_coef,
    )
    edge_scratch = [VMEM((LANES, LANES), F32)] * 2 + turned
    masked, sums, to_west, to_east = call(
        middle_kernel,
        fields_by_rows(1) + planes_by_rows(3) + edges_by_rows(2) + planes_by_rows(1)
        + fields_by_rows(1) + planes_by_rows(1),
        fields_by_rows(1) + planes_by_rows(1) + edges_by_rows(2),
        [field, plane, edge, edge], edge_scratch, 12 << 20,
        first, *ups, *sides, land_sea, vertical_coef, rim, grid=strips,
    )
    ups = from_deeper(sums)
    sides = from_sides(to_west, to_east)
    second = call(
        local_kernel, far(5), far(1), [field], stencil_scratch + stencil_sems, 18 << 20,
        masked, east_coef, north_coef, coriolis_coef, vertical_coef,
    )
    return call(
        last_kernel, fields_by_rows(1) + planes_by_rows(3) + edges_by_rows(2), fields_by_rows(1),
        [field], [VMEM((LANES, LANES), F32)] + turned, 7 << 20,
        second, *ups, *sides, grid=strips,
    )


def solution(mesh):
    return jax.shard_map(
        body,
        mesh=mesh,
        in_specs=(
            P("lev", None, "tile"),
            P("lev", None, "tile"),
            P("lev", None, "tile"),
            P("lev", None, "tile"),
            P("lev", None, "tile"),
            P(None, "tile"),
            P("tile", None, None),
            P("tile", None, None, None),
            P("tile", None, None, None, None),
            P("tile", None, None, None),
            P("tile", None, None, None),
            P("tile", None, None, None),
            P(),
        ),
        out_specs=P("lev", None, "tile"),
        check_vma=False,
    )
```

```python
import jax
import jax.numpy as jnp
from jax import lax
from jax.experimental import pallas as pl
from jax.experimental.pallas import tpu as pltpu
from jax.sharding import PartitionSpec as P

LANES = 128
ROWS = 768
BAND = 8
CAP = 256
OWNERS = 32
BLOCK = 24
CHUNK = 32
LATE_ACCS = 8
EARLY_ACCS = 6
STRIP = 32
PARTS = 6
PART = ROWS // PARTS
PLANES = BAND + 1
LIMIT = 63 << 20
VMEM = pltpu.VMEM
SMEM = pltpu.SMEM
F32 = jnp.float32
BF16 = jnp.bfloat16


def lane_ids():
    return lax.broadcasted_iota(jnp.int32, (STRIP, LANES), 1)


def prepare(band, weight, counts, cell, frac, innovation, kind, level, out):
    z = band[0]
    ids = lax.broadcasted_iota(jnp.int32, (OWNERS, LANES), 1)
    for s in range(2):
        own = lax.broadcasted_iota(jnp.int32, (OWNERS, OWNERS), 0)
        other = lax.broadcasted_iota(jnp.int32, (OWNERS, OWNERS), 1)
        row = jnp.broadcast_to(counts[0, s : s + 1, :].astype(F32), (OWNERS, OWNERS))
        count = jnp.sum(jnp.where(own == other, row, 0.0), 1, keepdims=True)
        out[pl.ds(20 + s, OWNERS, stride=BLOCK), :] = jnp.broadcast_to(count, (OWNERS, LANES))
        for h in range(2):
            part = slice(h * LANES, (h + 1) * LANES)
            t = kind[0, s, :, part]
            at = cell[0, s, :, part]
            scale = jnp.where(t == 0, weight[0], jnp.where(t == 1, weight[1], weight[2]))
            live = (ids + h * LANES).astype(F32) < count
            residual = jnp.where(live, scale * innovation[0, s, :, part], 0.0)
            local = level[0, s, :, part] - z * BAND
            here = (t == 1) & (local >= 0) & (local < BAND)
            keep = (t == 0) | here | ((t == 2) & (z == 0))
            residual = jnp.where(keep, residual, 0.0)
            residual = jnp.where(t == 0, 0.25 * residual, residual)
            target = jnp.where(t == 0, BAND, jnp.where(here, local, 0))
            east = frac[0, s, :, 0, part]
            north = frac[0, s, :, 1, part]
            index = target * ROWS + lax.shift_right_logical(at, 7)
            column = lax.bitwise_and(at, LANES - 1)
            first = s * 8 + h * 4
            values = (column.astype(F32), east, residual * (1.0 - north), residual * north)
            for j, value in enumerate(values):
                out[pl.ds(first + j, OWNERS, stride=BLOCK), :] = value
            out[pl.ds(16 + s * 2 + h, OWNERS, stride=BLOCK), :] = index.astype(F32)
        out[pl.ds(22 + s, OWNERS, stride=BLOCK), :] = jnp.zeros((OWNERS, LANES), F32)


def make_pairs(select, pairs, block, half, at):
    parts = jnp.concatenate(three_parts(block) + [jnp.zeros_like(block)], 0)
    spread = lax.dot_general(
        parts.astype(BF16), select[half], (((0,), (0,)), ((), ())), preferred_element_type=F32
    )
    column, east, south, north = (
        spread[:, j * LANES : (j + 1) * LANES] for j in range(4)
    )
    lanes = lax.broadcasted_iota(jnp.int32, (LANES, LANES), 1).astype(F32)
    weight = jnp.maximum(0.0, 1.0 - jnp.abs((lanes - column) - east))
    pairs[pl.ds(at, LANES, stride=2), :] = weight * south
    pairs[pl.ds(at + 1, LANES, stride=2), :] = weight * north


def spread(s, far_places, slots, select, pairs, places, sem, accs, first_cleared, ready):
    fetch = pltpu.make_async_copy(far_places, places, sem)
    fetch.start()
    row = lax.broadcasted_iota(jnp.int32, (32, 4 * LANES), 0)
    group = lax.shift_right_logical(lax.broadcasted_iota(jnp.int32, (32, 4 * LANES), 1), 7)
    for h in range(2):
        hit = (lax.bitwise_and(row, 7) == group + 4 * h) & (row < 24)
        select[h] = jnp.where(hit, 1.0, 0.0).astype(BF16)
    share = PLANES * ROWS // OWNERS

    def west(o, _):
        for acc in accs[first_cleared:]:
            acc[pl.ds(pl.multiple_of(o * share, 8), share), :] = jnp.zeros((share, LANES), F32)
        block = slots[pl.ds(pl.multiple_of(o * BLOCK + s * 8, 8), 8), :]
        make_pairs(select, pairs, block, 0, o * 2 * CAP)
        return 0

    lax.fori_loop(0, OWNERS, west, 0, unroll=4)
    fetch.wait()

    def most(o, value):
        return jnp.maximum(value, places[o * 8 * LANES + (4 + s) * LANES])

    @pl.when(lax.fori_loop(0, OWNERS, most, jnp.int32(0), unroll=8) > LANES)
    def _():
        def east(o, _):
            block = slots[pl.ds(pl.multiple_of(o * BLOCK + s * 8, 8), 8), :]
            make_pairs(select, pairs, block, 1, o * 2 * CAP + 2 * LANES)
            return 0

        lax.fori_loop(0, OWNERS, east, 0, unroll=4)

    for copy in ready:
        copy.wait()

    def owner(o, _):
        count = places[o * 8 * LANES + (4 + s) * LANES]

        def step(c, _):
            at = o * 8 * LANES + s * CAP + c * CHUNK
            pair = o * 2 * CAP + c * 2 * CHUNK
            for j in range(CHUNK):
                acc = accs[j % len(accs)]
                r = places[at + j]
                acc[pl.ds(r, 2), :] = acc[pl.ds(r, 2), :] + pairs[pl.ds(pair + 2 * j, 2), :]
            return 0

        return lax.fori_loop(0, lax.div(count + (CHUNK - 1), CHUNK), step, 0)

    lax.fori_loop(0, OWNERS, owner, 0)


def total_of(accs, plane, at):
    value = accs[0][pl.ds(plane * ROWS + at, STRIP), :]
    for acc in accs[1:]:
        value = value + acc[pl.ds(plane * ROWS + at, STRIP), :]
    return value


def edge_columns(into, lanes, k, value):
    rolled = pltpu.roll(value, 2 * k + 1, 1)
    return jnp.where((lanes == 2 * k) | (lanes == 2 * k + 1), rolled, into)


def send_edges(edges, at, turned, to_west, to_east, part):
    turned[...] = edges[pl.ds(at, LANES), :].T[0:16, :]
    to_west[:, part] = turned[pl.ds(1, BAND, stride=2), :]
    to_east[:, part] = turned[pl.ds(0, BAND, stride=2), :]


def rims(east, coriolis, vertical, land, out, columns):
    lanes = lane_ids()
    for r in range(0, LANES, STRIP):
        rows = slice(r, r + STRIP)
        value = jnp.zeros((STRIP, LANES), F32)
        total = vertical[0, rows, :]
        for k in range(BAND):
            e = east[k, rows, :]
            c = coriolis[k, rows, :]
            value = edge_columns(value, lanes, k, jnp.where(lanes == 0, e - c, e + c))
            if k:
                total = total + vertical[k, rows, :]
        out[rows, :] = value
        columns[rows, :] = total * land[rows, :].astype(F32)


def row_part(ref, c):
    return ref.at[:, pl.ds(c * PART, PART), :]


def late_kernel(
    far_places, slots, final, land, vertical, rim, masked, sums, to_west, to_east,
    select, pairs, places, edges, turned, v_s, sem, in_sem, out_sem, *accs,
):
    copies = [
        pltpu.make_async_copy(final.at[k], accs[0].at[pl.ds(k * ROWS, ROWS)], in_sem.at[k])
        for k in range(BAND)
    ]
    copies.append(pltpu.make_async_copy(vertical, v_s, in_sem.at[BAND]))
    for copy in copies:
        copy.start()
    accs[0][pl.ds(BAND * ROWS, ROWS), :] = jnp.zeros((ROWS, LANES), F32)
    spread(1, far_places, slots, select, pairs, places, sem, accs, 1, copies[:BAND])
    copies[BAND].wait()
    lanes = lane_ids()

    def one(i, _):
        at = pl.multiple_of(i * STRIP, STRIP)
        rows = pl.ds(at, STRIP)
        sea = land[rows, :].astype(F32)
        shared = total_of(accs, BAND, at)
        total = jnp.zeros((STRIP, LANES), F32)
        edge = jnp.zeros((STRIP, LANES), F32)
        for k in range(BAND):
            m = sea * (total_of(accs, k, at) + shared)
            accs[0][pl.ds(k * ROWS + at, STRIP), :] = m
            total = total + v_s[k, rows, :] * m
            edge = edge_columns(edge, lanes, k, m)
        sums[rows, :] = total
        edges[rows, :] = edge * rim[rows, :]
        return 0

    leaving = []
    for c in range(PARTS):
        lax.fori_loop(c * PART // STRIP, (c + 1) * PART // STRIP, one, 0)
        for k in range(BAND):
            copy = pltpu.make_async_copy(
                accs[0].at[pl.ds(k * ROWS + c * PART, PART)],
                masked.at[k, pl.ds(c * PART, PART)],
                out_sem.at[c, k],
            )
            copy.start()
            leaving.append(copy)
    for b in range(ROWS // LANES):
        part = slice(b * LANES, (b + 1) * LANES)
        send_edges(edges, b * LANES, turned, to_west, to_east, part)
    for copy in leaving:
        copy.wait()


def fetch_fields(sources, targets, sem):
    copies = []
    for c in range(PARTS):
        row = []
        for j, (source, target) in enumerate(zip(sources, targets)):
            start = c * PART + (8 if target.shape[1] > ROWS else 0)
            copy = pltpu.make_async_copy(
                row_part(source, c), target.at[:, pl.ds(start, PART), :], sem.at[c, j]
            )
            copy.start()
            row.append(copy)
        copies.append(row)
    return copies


def rim_select(select):
    row = lax.broadcasted_iota(jnp.int32, (8 * BAND, BAND * LANES), 0)
    column = lax.broadcasted_iota(jnp.int32, (8 * BAND, BAND * LANES), 1)
    level = lax.shift_right_logical(column, 7)
    lane = lax.bitwise_and(column, LANES - 1)
    side = jnp.where(row < 3 * BAND, LANES - 1, 0)
    hit = (lax.bitwise_and(row, BAND - 1) == level) & (lane == side) & (row < 6 * BAND)
    select[...] = jnp.where(hit, 1.0, 0.0).astype(BF16)


def three_parts(value):
    high = value.astype(BF16).astype(F32)
    rest = value - high
    middle = rest.astype(BF16).astype(F32)
    return [high, middle, rest - middle]


def place_rims(from_east, from_west, select, placed):
    rim_select(select)
    for b in range(ROWS // LANES):
        part = slice(b * LANES, (b + 1) * LANES)
        east, west = from_east[:, part], from_west[:, part]
        empty = jnp.zeros((2 * BAND, LANES), F32)
        parts = jnp.concatenate(three_parts(east) + three_parts(west) + [empty], 0)
        placed[part, :] = lax.dot_general(
            parts.astype(BF16), select[...], (((0,), (0,)), ((), ())), preferred_element_type=F32
        )


def stencil(copies, masked, east, north, coriolis, vertical, prepare_rows, start, added, finish,
            out, out_sem):
    for k in range(BAND):
        north[k, 0:8, :] = jnp.zeros((8, LANES), F32)
        north[k, ROWS + 8 : ROWS + 16, :] = jnp.zeros((8, LANES), F32)

    def first(i, _):
        at = pl.multiple_of(i * STRIP, STRIP)
        rows = pl.ds(pl.multiple_of(at + 8, 8), STRIP)
        prepare_rows(at)
        for k in range(BAND):
            north[k, rows, :] = north[k, rows, :] * masked[k, pl.ds(at, STRIP), :]
        return 0

    lanes = lane_ids()

    def second(i, _):
        at = pl.multiple_of(i * STRIP, STRIP)
        rows = pl.ds(at, STRIP)
        below = start(at)
        total = jnp.zeros((STRIP, LANES), F32)
        for k in reversed(range(BAND)):
            m = masked[k, rows, :]
            e = east[k, rows, :] * m
            c = coriolis[k, rows, :] * m
            v = vertical[k, rows, :]
            below = below + v * m
            ahead = jnp.where(lanes == LANES - 1, 0.0, pltpu.roll(e - c, LANES - 1, 1))
            behind = jnp.where(lanes == 0, 0.0, pltpu.roll(e + c, 1, 1))
            across = (
                north[k, pl.ds(at + 7, STRIP), :]
                + north[k, pl.ds(at + 9, STRIP), :]
                - 2.0 * north[k, pl.ds(pl.multiple_of(at + 8, 8), STRIP), :]
            )
            value = m + (ahead + behind - 2.0 * e) + across + below + added(k, at)
            masked[k, rows, :] = value
            total = total + v * value
        finish(at, total)
        return 0

    leaving = []
    for c in range(PARTS + 1):
        if c < PARTS:
            for copy in copies[c]:
                copy.wait()
            lax.fori_loop(c * PART // STRIP, (c + 1) * PART // STRIP, first, 0)
        if c > 0:
            lax.fori_loop((c - 1) * PART // STRIP, c * PART // STRIP, second, 0)
            copy = pltpu.make_async_copy(
                row_part(masked, c - 1), row_part(out, c - 1), out_sem.at[c - 1]
            )
            copy.start()
            leaving.append(copy)
    return leaving


def early_kernel(
    far_places, slots, land, from_east, from_west, masked, east, north, coriolis, vertical,
    out, sums,
    select, pairs, places, rim_picks, placed, m_s, e_s, n_s, c_s, v_s,
    sem, in_sem, out_sem, *accs,
):
    copies = fetch_fields(
        (masked, east, north, coriolis, vertical), (m_s, e_s, n_s, c_s, v_s), in_sem
    )
    place_rims(from_east, from_west, rim_picks, placed)
    spread(0, far_places, slots, select, pairs, places, sem, accs, 0, ())

    def start(at):
        return total_of(accs, BAND, at)

    def added(k, at):
        rows = pl.ds(at, STRIP)
        return total_of(accs, k, at) + placed[rows, k * LANES : (k + 1) * LANES]

    def finish(at, total):
        rows = pl.ds(at, STRIP)
        sums[rows, :] = total * land[rows, :].astype(F32)

    leaving = stencil(
        copies, m_s, e_s, n_s, c_s, v_s, lambda at: None, start, added, finish, out, out_sem
    )
    for copy in leaving:
        copy.wait()


def middle_kernel(
    one_up, two_up, three_up, one_column, two_column, land, rim,
    field, east, north, coriolis, vertical, out, to_west, to_east,
    edges, turned, m_s, e_s, n_s, c_s, v_s, in_sem, out_sem,
):
    copies = fetch_fields(
        (field, east, north, coriolis, vertical), (m_s, e_s, n_s, c_s, v_s), in_sem
    )
    lanes = lane_ids()

    def prepare_rows(at):
        rows = pl.ds(at, STRIP)
        sea = land[rows, :].astype(F32)
        higher = one_up[rows, :] + two_up[rows, :] + three_up[rows, :]
        edge = jnp.zeros((STRIP, LANES), F32)
        for k in range(BAND):
            m = sea * (m_s[k, rows, :] + higher)
            m_s[k, rows, :] = m
            edge = edge_columns(edge, lanes, k, m)
        edges[rows, :] = edge * rim[rows, :]

    def start(at):
        rows = pl.ds(at, STRIP)
        near = one_column[rows, :]
        return two_up[rows, :] * near + three_up[rows, :] * (near + two_column[rows, :])

    leaving = stencil(
        copies, m_s, e_s, n_s, c_s, v_s, prepare_rows, start, lambda k, at: 0.0,
        lambda at, total: None, out, out_sem,
    )
    for b in range(ROWS // LANES):
        part = slice(b * LANES, (b + 1) * LANES)
        send_edges(edges, b * LANES, turned, to_west, to_east, part)
    for copy in leaving:
        copy.wait()


def last_kernel(field, one_up, two_up, three_up, from_east, from_west, out, select, placed):
    step = pl.program_id(0)

    @pl.when(step == 0)
    def _():
        place_rims(from_east, from_west, select, placed)

    for r in range(0, LANES, STRIP):
        rows = slice(r, r + STRIP)
        at = pl.multiple_of(step * LANES + r, STRIP)
        higher = one_up[rows, :] + two_up[rows, :] + three_up[rows, :]
        for k in range(BAND):
            rim = placed[pl.ds(at, STRIP), k * LANES : (k + 1) * LANES]
            out[k, rows, :] = field[k, rows, :] + higher + rim


def shape(*dims):
    return jax.ShapeDtypeStruct(dims, F32)


def vm(count):
    return [pl.BlockSpec(memory_space=VMEM)] * count


def sm(count):
    return [pl.BlockSpec(memory_space=SMEM)] * count


def far(count):
    return [pl.BlockSpec(memory_space=pl.ANY)] * count


def fields_by_rows(count):
    return [pl.BlockSpec((BAND, LANES, LANES), lambda i: (0, i, 0))] * count


def planes_by_rows(count):
    return [pl.BlockSpec((LANES, LANES), lambda i: (i, 0))] * count


def call(kernel, ins, outs, shapes, scratch, moved, *args, grid=()):
    many = len(outs) > 1
    return pl.pallas_call(
        kernel,
        grid=grid,
        in_specs=ins,
        out_specs=tuple(outs) if many else outs[0],
        out_shape=tuple(shapes) if many else shapes[0],
        scratch_shapes=scratch,
        compiler_params=pltpu.CompilerParams(vmem_limit_bytes=LIMIT),
        cost_estimate=pl.CostEstimate(flops=moved, bytes_accessed=moved, transcendentals=0),
    )(*args)


def from_deeper(part):
    return (
        lax.ppermute(part, "lev", [(3, 2), (2, 1), (1, 0)]),
        lax.ppermute(part, "lev", [(3, 1), (2, 0)]),
        lax.ppermute(part, "lev", [(3, 0)]),
    )


def from_sides(to_west, to_east):
    count = lax.axis_size("tile")
    return (
        lax.ppermute(to_west, "tile", [((i + 1) % count, i) for i in range(count)]),
        lax.ppermute(to_east, "tile", [(i, (i + 1) % count) for i in range(count)]),
    )


def body(
    final_adjoint,
    east_coef,
    north_coef,
    coriolis_coef,
    vertical_coef,
    land_sea,
    counts,
    obs_cell,
    obs_frac,
    innovation,
    obs_type,
    obs_level,
    type_weight,
):
    band = lax.axis_index("lev").astype(jnp.int32).reshape(1)
    field = shape(BAND, ROWS, LANES)
    plane = shape(ROWS, LANES)
    edge = shape(BAND, ROWS)
    strips = (ROWS // LANES,)
    dma = pltpu.SemaphoreType.DMA
    send = call(
        prepare, sm(2) + vm(6), vm(1), [shape(OWNERS * BLOCK, LANES)], [], 1 << 20,
        band, type_weight, counts, obs_cell, obs_frac, innovation, obs_type, obs_level,
    )
    arrived = lax.all_to_all(
        send.reshape(OWNERS, BLOCK, LANES), "tile", split_axis=0, concat_axis=0, tiled=True
    )
    rim, columns = call(
        rims, fields_by_rows(3) + planes_by_rows(1), planes_by_rows(2), [plane, plane], [],
        10 << 20, east_coef, coriolis_coef, vertical_coef, land_sea, grid=strips,
    )
    one_column = lax.ppermute(columns, "lev", [(2, 1), (1, 0)])
    two_column = lax.ppermute(columns, "lev", [(2, 0)])
    places = arrived[:, 16:24, :].astype(jnp.int32).reshape(-1)
    slots = arrived.reshape(OWNERS * BLOCK, LANES)
    acc = VMEM((PLANES * ROWS + 8, LANES), F32)
    spread_scratch = [
        VMEM((2, 32, 4 * LANES), BF16),
        VMEM((OWNERS * CAP * 2, LANES), F32),
        SMEM((OWNERS * 8 * LANES,), jnp.int32),
    ]
    turned = [VMEM((2 * BAND, LANES), F32)]
    masked, sums, to_west, to_east = call(
        late_kernel, far(1) + vm(1) + far(1) + vm(1) + far(1) + vm(1), far(1) + vm(3),
        [field, plane, edge, edge],
        spread_scratch + [VMEM((ROWS, LANES), F32)] + turned + [VMEM((BAND, ROWS, LANES), F32)]
        + [dma, dma((BAND + 1,)), dma((PARTS, BAND))] + [acc] * LATE_ACCS,
        10 << 20,
        places, slots, final_adjoint, land_sea, vertical_coef, rim,
    )
    sides = from_sides(to_west, to_east)
    ups = from_deeper(sums)
    stored = VMEM((BAND, ROWS, LANES), F32)
    wide = VMEM((BAND, ROWS + 16, LANES), F32)
    stencil_scratch = [stored, stored, wide, stored, stored]
    stencil_sems = [dma((PARTS, 5)), dma((PARTS,))]
    rim_scratch = [VMEM((8 * BAND, BAND * LANES), BF16), VMEM((ROWS, BAND * LANES), F32)]
    first, sums = call(
        early_kernel, far(1) + vm(4) + far(5), far(1) + vm(1), [field, plane],
        spread_scratch + rim_scratch + stencil_scratch + [dma] + stencil_sems
        + [acc] * EARLY_ACCS,
        40 << 20,
        places, slots, land_sea, *sides,
        masked, east_coef, north_coef, coriolis_coef, vertical_coef,
    )
    later_ups = from_deeper(sums)
    second, to_west, to_east = call(
        middle_kernel, vm(7) + far(5), far(1) + vm(2), [field, edge, edge],
        [VMEM((ROWS, LANES), F32)] + turned + stencil_scratch + stencil_sems, 24 << 20,
        *ups, one_column, two_column, land_sea, rim,
        first, east_coef, north_coef, coriolis_coef, vertical_coef,
    )
    sides = from_sides(to_west, to_east)
    whole_edge = [pl.BlockSpec((BAND, ROWS), lambda i: (0, 0))] * 2
    return call(
        last_kernel, fields_by_rows(1) + planes_by_rows(3) + whole_edge, fields_by_rows(1),
        [field], rim_scratch, 7 << 20,
        second, *later_ups, *sides, grid=strips,
    )


def solution(mesh):
    return jax.shard_map(
        body,
        mesh=mesh,
        in_specs=(
            P("lev", None, "tile"),
            P("lev", None, "tile"),
            P("lev", None, "tile"),
            P("lev", None, "tile"),
            P("lev", None, "tile"),
            P(None, "tile"),
            P("tile", None, None),
            P("tile", None, None, None),
            P("tile", None, None, None, None),
            P("tile", None, None, None),
            P("tile", None, None, None),
            P("tile", None, None, None),
            P(),
        ),
        out_specs=P("lev", None, "tile"),
        check_vma=False,
    )
```

```python
import jax
import jax.numpy as jnp
from jax import lax
from jax.experimental import pallas as pl
from jax.experimental.pallas import tpu as pltpu
from jax.sharding import PartitionSpec as P

LANES = 128
ROWS = 768
BAND = 8
CAP = 256
OWNERS = 32
BLOCK = 24
CHUNK = 32
LATE_ACCS = 6
EARLY_ACCS = 6
STRIP = 32
UNROLL = 4
PARTS = 6
PART = ROWS // PARTS
PLANES = BAND + 1
LIMIT = 63 << 20
VMEM = pltpu.VMEM
SMEM = pltpu.SMEM
F32 = jnp.float32
BF16 = jnp.bfloat16


def lane_ids():
    return lax.broadcasted_iota(jnp.int32, (STRIP, LANES), 1)


def prepare(band, weight, counts, cell, frac, innovation, kind, level, out):
    z = band[0]
    ids = lax.broadcasted_iota(jnp.int32, (OWNERS, LANES), 1)
    for s in range(2):
        own = lax.broadcasted_iota(jnp.int32, (OWNERS, OWNERS), 0)
        other = lax.broadcasted_iota(jnp.int32, (OWNERS, OWNERS), 1)
        row = jnp.broadcast_to(counts[0, s : s + 1, :].astype(F32), (OWNERS, OWNERS))
        count = jnp.sum(jnp.where(own == other, row, 0.0), 1, keepdims=True)
        out[pl.ds(20 + s, OWNERS, stride=BLOCK), :] = jnp.broadcast_to(count, (OWNERS, LANES))
        for h in range(2):
            part = slice(h * LANES, (h + 1) * LANES)
            t = kind[0, s, :, part]
            at = cell[0, s, :, part]
            scale = jnp.where(t == 0, weight[0], jnp.where(t == 1, weight[1], weight[2]))
            live = (ids + h * LANES).astype(F32) < count
            residual = jnp.where(live, scale * innovation[0, s, :, part], 0.0)
            local = level[0, s, :, part] - z * BAND
            here = (t == 1) & (local >= 0) & (local < BAND)
            keep = (t == 0) | here | ((t == 2) & (z == 0))
            residual = jnp.where(keep, residual, 0.0)
            residual = jnp.where(t == 0, 0.25 * residual, residual)
            target = jnp.where(t == 0, BAND, jnp.where(here, local, 0))
            east = frac[0, s, :, 0, part]
            north = frac[0, s, :, 1, part]
            index = target * ROWS + lax.shift_right_logical(at, 7)
            column = lax.bitwise_and(at, LANES - 1)
            first = s * 8 + h * 4
            values = (column.astype(F32), east, residual * (1.0 - north), residual * north)
            for j, value in enumerate(values):
                out[pl.ds(first + j, OWNERS, stride=BLOCK), :] = value
            out[pl.ds(16 + s * 2 + h, OWNERS, stride=BLOCK), :] = index.astype(F32)
        out[pl.ds(22 + s, OWNERS, stride=BLOCK), :] = jnp.zeros((OWNERS, LANES), F32)


def make_pairs(select, pairs, block, half, at):
    parts = jnp.concatenate(three_parts(block) + [jnp.zeros_like(block)], 0)
    spread = lax.dot_general(
        parts.astype(BF16), select[half], (((0,), (0,)), ((), ())), preferred_element_type=F32
    )
    column, east, south, north = (
        spread[:, j * LANES : (j + 1) * LANES] for j in range(4)
    )
    lanes = lax.broadcasted_iota(jnp.int32, (LANES, LANES), 1).astype(F32)
    weight = jnp.maximum(0.0, 1.0 - jnp.abs((lanes - column) - east))
    pairs[pl.ds(at, LANES, stride=2), :] = weight * south
    pairs[pl.ds(at + 1, LANES, stride=2), :] = weight * north


def spread(s, far_places, slots, select, pairs, places, sem, accs, first_cleared, ready):
    fetch = pltpu.make_async_copy(far_places, places, sem)
    fetch.start()
    row = lax.broadcasted_iota(jnp.int32, (32, 4 * LANES), 0)
    group = lax.shift_right_logical(lax.broadcasted_iota(jnp.int32, (32, 4 * LANES), 1), 7)
    for h in range(2):
        hit = (lax.bitwise_and(row, 7) == group + 4 * h) & (row < 24)
        select[h] = jnp.where(hit, 1.0, 0.0).astype(BF16)
    share = PLANES * ROWS // OWNERS

    def west(o, _):
        for acc in accs[first_cleared:]:
            acc[pl.ds(pl.multiple_of(o * share, 8), share), :] = jnp.zeros((share, LANES), F32)
        block = slots[pl.ds(pl.multiple_of(o * BLOCK + s * 8, 8), 8), :]
        make_pairs(select, pairs, block, 0, o * 2 * CAP)
        return 0

    lax.fori_loop(0, OWNERS, west, 0, unroll=4)
    fetch.wait()

    def most(o, value):
        return jnp.maximum(value, places[o * 8 * LANES + (4 + s) * LANES])

    @pl.when(lax.fori_loop(0, OWNERS, most, jnp.int32(0), unroll=8) > LANES)
    def _():
        def east(o, _):
            block = slots[pl.ds(pl.multiple_of(o * BLOCK + s * 8, 8), 8), :]
            make_pairs(select, pairs, block, 1, o * 2 * CAP + 2 * LANES)
            return 0

        lax.fori_loop(0, OWNERS, east, 0, unroll=4)

    for copy in ready:
        copy.wait()

    def owner(o, _):
        count = places[o * 8 * LANES + (4 + s) * LANES]

        def step(c, _):
            at = o * 8 * LANES + s * CAP + c * CHUNK
            pair = o * 2 * CAP + c * 2 * CHUNK
            for j in range(CHUNK):
                acc = accs[j % len(accs)]
                r = places[at + j]
                acc[pl.ds(r, 2), :] = acc[pl.ds(r, 2), :] + pairs[pl.ds(pair + 2 * j, 2), :]
            return 0

        return lax.fori_loop(0, lax.div(count + (CHUNK - 1), CHUNK), step, 0)

    lax.fori_loop(0, OWNERS, owner, 0)


def total_of(accs, plane, at):
    value = accs[0][pl.ds(plane * ROWS + at, STRIP), :]
    for acc in accs[1:]:
        value = value + acc[pl.ds(plane * ROWS + at, STRIP), :]
    return value


def edge_columns(into, lanes, k, value):
    rolled = pltpu.roll(value, 2 * k + 1, 1)
    return jnp.where((lanes == 2 * k) | (lanes == 2 * k + 1), rolled, into)


def send_edges(edges, at, turned, to_west, to_east, part):
    turned[...] = edges[pl.ds(at, LANES), :].T[0:16, :]
    to_west[:, part] = turned[pl.ds(1, BAND, stride=2), :]
    to_east[:, part] = turned[pl.ds(0, BAND, stride=2), :]


def rims(east, coriolis, vertical, land, out, columns):
    lanes = lane_ids()
    for r in range(0, LANES, STRIP):
        rows = slice(r, r + STRIP)
        value = jnp.zeros((STRIP, LANES), F32)
        total = vertical[0, rows, :]
        for k in range(BAND):
            e = east[k, rows, :]
            c = coriolis[k, rows, :]
            value = edge_columns(value, lanes, k, jnp.where(lanes == 0, e - c, e + c))
            if k:
                total = total + vertical[k, rows, :]
        out[rows, :] = value
        columns[rows, :] = total * land[rows, :].astype(F32)


def row_part(ref, c):
    return ref.at[:, pl.ds(c * PART, PART), :]


def late_kernel(
    far_places, slots, final, land, vertical, rim, masked, sums, to_west, to_east,
    select, pairs, places, edges, turned, v_s, o_s, sem, in_sem, out_sem, *accs,
):
    copies = [
        pltpu.make_async_copy(final.at[k], accs[0].at[pl.ds(k * ROWS, ROWS)], in_sem.at[k])
        for k in range(BAND)
    ]
    copies.append(pltpu.make_async_copy(vertical, v_s, in_sem.at[BAND]))
    for copy in copies:
        copy.start()
    accs[0][pl.ds(BAND * ROWS, ROWS), :] = jnp.zeros((ROWS, LANES), F32)
    spread(1, far_places, slots, select, pairs, places, sem, accs, 1, copies[:BAND])
    copies[BAND].wait()
    lanes = lane_ids()

    def one(i, _):
        at = pl.multiple_of(i * STRIP, STRIP)
        rows = pl.ds(at, STRIP)
        sea = land[rows, :].astype(F32)
        shared = total_of(accs, BAND, at)
        total = jnp.zeros((STRIP, LANES), F32)
        edge = jnp.zeros((STRIP, LANES), F32)
        for k in range(BAND):
            m = sea * (total_of(accs, k, at) + shared)
            o_s[k, rows, :] = m
            total = total + v_s[k, rows, :] * m
            edge = edge_columns(edge, lanes, k, m)
        sums[rows, :] = total
        edges[rows, :] = edge * rim[rows, :]
        return 0

    leaving = []
    for c in range(PARTS):
        lax.fori_loop(c * PART // STRIP, (c + 1) * PART // STRIP, one, 0, unroll=UNROLL)
        copy = pltpu.make_async_copy(row_part(o_s, c), row_part(masked, c), out_sem.at[c])
        copy.start()
        leaving.append(copy)
    for b in range(ROWS // LANES):
        part = slice(b * LANES, (b + 1) * LANES)
        send_edges(edges, b * LANES, turned, to_west, to_east, part)
    for copy in leaving:
        copy.wait()


def fetch_fields(sources, targets, sem):
    copies = []
    for c in range(PARTS):
        row = []
        for j, (source, target) in enumerate(zip(sources, targets)):
            copy = pltpu.make_async_copy(row_part(source, c), row_part(target, c), sem.at[c, j])
            copy.start()
            row.append(copy)
        copies.append(row)
    return copies


def rim_select(select):
    row = lax.broadcasted_iota(jnp.int32, (8 * BAND, BAND * LANES), 0)
    column = lax.broadcasted_iota(jnp.int32, (8 * BAND, BAND * LANES), 1)
    level = lax.shift_right_logical(column, 7)
    lane = lax.bitwise_and(column, LANES - 1)
    side = jnp.where(row < 3 * BAND, LANES - 1, 0)
    hit = (lax.bitwise_and(row, BAND - 1) == level) & (lane == side) & (row < 6 * BAND)
    select[...] = jnp.where(hit, 1.0, 0.0).astype(BF16)


def three_parts(value):
    high = value.astype(BF16).astype(F32)
    rest = value - high
    middle = rest.astype(BF16).astype(F32)
    return [high, middle, rest - middle]


def place_rims(from_east, from_west, select, placed):
    rim_select(select)
    for b in range(ROWS // LANES):
        part = slice(b * LANES, (b + 1) * LANES)
        east, west = from_east[:, part], from_west[:, part]
        empty = jnp.zeros((2 * BAND, LANES), F32)
        parts = jnp.concatenate(three_parts(east) + three_parts(west) + [empty], 0)
        placed[part, :] = lax.dot_general(
            parts.astype(BF16), select[...], (((0,), (0,)), ((), ())), preferred_element_type=F32
        )


def stencil(copies, masked, east, north, coriolis, vertical, flow, made, prepare_rows, start, added,
            finish, out, out_sem):
    for k in range(BAND):
        flow[k, 0:8, :] = jnp.zeros((8, LANES), F32)
        flow[k, ROWS + 8 : ROWS + 16, :] = jnp.zeros((8, LANES), F32)

    def first(i, _):
        at = pl.multiple_of(i * STRIP, STRIP)
        prepare_rows(at)
        rows = pl.ds(at, STRIP)
        for k in range(BAND):
            value = north[k, rows, :] * masked[k, rows, :]
            flow[k, pl.ds(pl.multiple_of(at + 8, 8), STRIP), :] = value
        return 0

    lanes = lane_ids()

    def second(i, _):
        at = pl.multiple_of(i * STRIP, STRIP)
        rows = pl.ds(at, STRIP)
        below = start(at)
        total = jnp.zeros((STRIP, LANES), F32)
        for k in reversed(range(BAND)):
            m = masked[k, rows, :]
            e = east[k, rows, :] * m
            c = coriolis[k, rows, :] * m
            v = vertical[k, rows, :]
            below = below + v * m
            ahead = jnp.where(lanes == LANES - 1, 0.0, pltpu.roll(e - c, LANES - 1, 1))
            behind = jnp.where(lanes == 0, 0.0, pltpu.roll(e + c, 1, 1))
            across = (
                flow[k, pl.ds(at + 7, STRIP), :]
                + flow[k, pl.ds(at + 9, STRIP), :]
                - 2.0 * flow[k, pl.ds(pl.multiple_of(at + 8, 8), STRIP), :]
            )
            value = m + (ahead + behind - 2.0 * e) + across + below + added(k, at)
            made[k, rows, :] = value
            total = total + v * value
        finish(at, total)
        return 0

    leaving = []
    for c in range(PARTS + 1):
        if c < PARTS:
            for copy in copies[c]:
                copy.wait()
            lax.fori_loop(c * PART // STRIP, (c + 1) * PART // STRIP, first, 0, unroll=UNROLL)
        if c > 0:
            lax.fori_loop((c - 1) * PART // STRIP, c * PART // STRIP, second, 0, unroll=UNROLL)
            copy = pltpu.make_async_copy(
                row_part(made, c - 1), row_part(out, c - 1), out_sem.at[c - 1]
            )
            copy.start()
            leaving.append(copy)
    return leaving


def early_kernel(
    far_places, slots, land, from_east, from_west, masked, east, north, coriolis, vertical,
    out, sums,
    select, pairs, places, rim_picks, placed, m_s, e_s, n_s, c_s, v_s, flow, made,
    sem, in_sem, out_sem, *accs,
):
    copies = fetch_fields(
        (masked, east, north, coriolis, vertical), (m_s, e_s, n_s, c_s, v_s), in_sem
    )
    place_rims(from_east, from_west, rim_picks, placed)
    spread(0, far_places, slots, select, pairs, places, sem, accs, 0, ())

    def start(at):
        return total_of(accs, BAND, at)

    def added(k, at):
        rows = pl.ds(at, STRIP)
        return total_of(accs, k, at) + placed[rows, k * LANES : (k + 1) * LANES]

    def finish(at, total):
        rows = pl.ds(at, STRIP)
        sums[rows, :] = total * land[rows, :].astype(F32)

    leaving = stencil(
        copies, m_s, e_s, n_s, c_s, v_s, flow, made, lambda at: None, start, added, finish, out, out_sem
    )
    for copy in leaving:
        copy.wait()


def middle_kernel(
    one_up, two_up, three_up, one_column, two_column, land, rim,
    field, east, north, coriolis, vertical, out, to_west, to_east,
    edges, turned, m_s, e_s, n_s, c_s, v_s, flow, made, in_sem, out_sem,
):
    copies = fetch_fields(
        (field, east, north, coriolis, vertical), (m_s, e_s, n_s, c_s, v_s), in_sem
    )
    lanes = lane_ids()

    def prepare_rows(at):
        rows = pl.ds(at, STRIP)
        sea = land[rows, :].astype(F32)
        higher = one_up[rows, :] + two_up[rows, :] + three_up[rows, :]
        edge = jnp.zeros((STRIP, LANES), F32)
        for k in range(BAND):
            m = sea * (m_s[k, rows, :] + higher)
            m_s[k, rows, :] = m
            edge = edge_columns(edge, lanes, k, m)
        edges[rows, :] = edge * rim[rows, :]

    def start(at):
        rows = pl.ds(at, STRIP)
        near = one_column[rows, :]
        return two_up[rows, :] * near + three_up[rows, :] * (near + two_column[rows, :])

    leaving = stencil(
        copies, m_s, e_s, n_s, c_s, v_s, flow, made, prepare_rows, start, lambda k, at: 0.0,
        lambda at, total: None, out, out_sem,
    )
    for b in range(ROWS // LANES):
        part = slice(b * LANES, (b + 1) * LANES)
        send_edges(edges, b * LANES, turned, to_west, to_east, part)
    for copy in leaving:
        copy.wait()


def rim_kernel(field, from_east, from_west, out, select, placed):
    step = pl.program_id(0)

    @pl.when(step == 0)
    def _():
        place_rims(from_east, from_west, select, placed)

    for r in range(0, LANES, STRIP):
        rows = slice(r, r + STRIP)
        at = pl.multiple_of(step * LANES + r, STRIP)
        for k in range(BAND):
            rim = placed[pl.ds(at, STRIP), k * LANES : (k + 1) * LANES]
            out[k, rows, :] = field[k, rows, :] + rim


def shape(*dims):
    return jax.ShapeDtypeStruct(dims, F32)


def vm(count):
    return [pl.BlockSpec(memory_space=VMEM)] * count


def sm(count):
    return [pl.BlockSpec(memory_space=SMEM)] * count


def far(count):
    return [pl.BlockSpec(memory_space=pl.ANY)] * count


def fields_by_rows(count):
    return [pl.BlockSpec((BAND, LANES, LANES), lambda i: (0, i, 0))] * count


def planes_by_rows(count):
    return [pl.BlockSpec((LANES, LANES), lambda i: (i, 0))] * count


def call(kernel, ins, outs, shapes, scratch, moved, *args, grid=()):
    many = len(outs) > 1
    return pl.pallas_call(
        kernel,
        grid=grid,
        in_specs=ins,
        out_specs=tuple(outs) if many else outs[0],
        out_shape=tuple(shapes) if many else shapes[0],
        scratch_shapes=scratch,
        compiler_params=pltpu.CompilerParams(vmem_limit_bytes=LIMIT),
        cost_estimate=pl.CostEstimate(flops=moved, bytes_accessed=moved, transcendentals=0),
    )(*args)


def from_deeper(part):
    return (
        lax.ppermute(part, "lev", [(3, 2), (2, 1), (1, 0)]),
        lax.ppermute(part, "lev", [(3, 1), (2, 0)]),
        lax.ppermute(part, "lev", [(3, 0)]),
    )


def from_sides(to_west, to_east):
    count = lax.axis_size("tile")
    return (
        lax.ppermute(to_west, "tile", [((i + 1) % count, i) for i in range(count)]),
        lax.ppermute(to_east, "tile", [(i, (i + 1) % count) for i in range(count)]),
    )


def body(
    final_adjoint,
    east_coef,
    north_coef,
    coriolis_coef,
    vertical_coef,
    land_sea,
    counts,
    obs_cell,
    obs_frac,
    innovation,
    obs_type,
    obs_level,
    type_weight,
):
    band = lax.axis_index("lev").astype(jnp.int32).reshape(1)
    field = shape(BAND, ROWS, LANES)
    plane = shape(ROWS, LANES)
    edge = shape(BAND, ROWS)
    strips = (ROWS // LANES,)
    dma = pltpu.SemaphoreType.DMA
    send = call(
        prepare, sm(2) + vm(6), vm(1), [shape(OWNERS * BLOCK, LANES)], [], 1 << 20,
        band, type_weight, counts, obs_cell, obs_frac, innovation, obs_type, obs_level,
    )
    arrived = lax.all_to_all(
        send.reshape(OWNERS, BLOCK, LANES), "tile", split_axis=0, concat_axis=0, tiled=True
    )
    rim, columns = call(
        rims, fields_by_rows(3) + planes_by_rows(1), planes_by_rows(2), [plane, plane], [],
        10 << 20, east_coef, coriolis_coef, vertical_coef, land_sea, grid=strips,
    )
    one_column = lax.ppermute(columns, "lev", [(2, 1), (1, 0)])
    two_column = lax.ppermute(columns, "lev", [(2, 0)])
    places = arrived[:, 16:24, :].astype(jnp.int32).reshape(-1)
    slots = arrived.reshape(OWNERS * BLOCK, LANES)
    acc = VMEM((PLANES * ROWS + 8, LANES), F32)
    spread_scratch = [
        VMEM((2, 32, 4 * LANES), BF16),
        VMEM((OWNERS * CAP * 2, LANES), F32),
        SMEM((OWNERS * 8 * LANES,), jnp.int32),
    ]
    turned = [VMEM((2 * BAND, LANES), F32)]
    masked, sums, to_west, to_east = call(
        late_kernel, far(1) + vm(1) + far(1) + vm(1) + far(1) + vm(1), far(1) + vm(3),
        [field, plane, edge, edge],
        spread_scratch + [VMEM((ROWS, LANES), F32)] + turned + [VMEM((BAND, ROWS, LANES), F32)] * 2
        + [dma, dma((BAND + 1,)), dma((PARTS,))] + [acc] * LATE_ACCS,
        10 << 20,
        places, slots, final_adjoint, land_sea, vertical_coef, rim,
    )
    sides = from_sides(to_west, to_east)
    ups = from_deeper(sums)
    stored = VMEM((BAND, ROWS, LANES), F32)
    wide = VMEM((BAND, ROWS + 16, LANES), F32)
    stencil_scratch = [stored] * 5 + [wide, stored]
    stencil_sems = [dma((PARTS, 5)), dma((PARTS,))]
    rim_scratch = [VMEM((8 * BAND, BAND * LANES), BF16), VMEM((ROWS, BAND * LANES), F32)]
    first, sums = call(
        early_kernel, far(1) + vm(4) + far(5), far(1) + vm(1), [field, plane],
        spread_scratch + rim_scratch + stencil_scratch + [dma] + stencil_sems
        + [acc] * EARLY_ACCS,
        40 << 20,
        places, slots, land_sea, *sides,
        masked, east_coef, north_coef, coriolis_coef, vertical_coef,
    )
    later_ups = from_deeper(sums)
    second, to_west, to_east = call(
        middle_kernel, vm(7) + far(5), far(1) + vm(2), [field, edge, edge],
        [VMEM((ROWS, LANES), F32)] + turned + stencil_scratch + stencil_sems, 24 << 20,
        *ups, one_column, two_column, land_sea, rim,
        first, east_coef, north_coef, coriolis_coef, vertical_coef,
    )
    sides = from_sides(to_west, to_east)
    whole_edge = [pl.BlockSpec((BAND, ROWS), lambda i: (0, 0))] * 2
    third = call(
        rim_kernel, fields_by_rows(1) + whole_edge, fields_by_rows(1),
        [field], rim_scratch, 7 << 20, second, *sides, grid=strips,
    )
    return third + (later_ups[0] + later_ups[1] + later_ups[2])[None]


def solution(mesh):
    return jax.shard_map(
        body,
        mesh=mesh,
        in_specs=(
            P("lev", None, "tile"),
            P("lev", None, "tile"),
            P("lev", None, "tile"),
            P("lev", None, "tile"),
            P("lev", None, "tile"),
            P(None, "tile"),
            P("tile", None, None),
            P("tile", None, None, None),
            P("tile", None, None, None, None),
            P("tile", None, None, None),
            P("tile", None, None, None),
            P("tile", None, None, None),
            P(),
        ),
        out_specs=P("lev", None, "tile"),
        check_vma=False,
    )
```

```python
import jax
import jax.numpy as jnp
from jax import lax
from jax.experimental import pallas as pl
from jax.experimental.pallas import tpu as pltpu
from jax.sharding import PartitionSpec as P

LANES = 128
ROWS = 768
BAND = 8
CAP = 256
OWNERS = 32
BLOCK = 24
CHUNK = 32
LATE_ACCS = 6
EARLY_ACCS = 6
STRIP = 32
UNROLL = 4
PARTS = 6
PART = ROWS // PARTS
PLANES = BAND + 1
LIMIT = 63 << 20
VMEM = pltpu.VMEM
SMEM = pltpu.SMEM
F32 = jnp.float32
BF16 = jnp.bfloat16


def lane_ids():
    return lax.broadcasted_iota(jnp.int32, (STRIP, LANES), 1)


def prepare(band, weight, counts, cell, frac, innovation, kind, level, out):
    z = band[0]
    ids = lax.broadcasted_iota(jnp.int32, (OWNERS, LANES), 1)
    for s in range(2):
        own = lax.broadcasted_iota(jnp.int32, (OWNERS, OWNERS), 0)
        other = lax.broadcasted_iota(jnp.int32, (OWNERS, OWNERS), 1)
        row = jnp.broadcast_to(counts[0, s : s + 1, :].astype(F32), (OWNERS, OWNERS))
        count = jnp.sum(jnp.where(own == other, row, 0.0), 1, keepdims=True)
        out[pl.ds(20 + s, OWNERS, stride=BLOCK), :] = jnp.broadcast_to(count, (OWNERS, LANES))
        for h in range(2):
            part = slice(h * LANES, (h + 1) * LANES)
            t = kind[0, s, :, part]
            at = cell[0, s, :, part]
            scale = jnp.where(t == 0, weight[0], jnp.where(t == 1, weight[1], weight[2]))
            live = (ids + h * LANES).astype(F32) < count
            residual = jnp.where(live, scale * innovation[0, s, :, part], 0.0)
            local = level[0, s, :, part] - z * BAND
            here = (t == 1) & (local >= 0) & (local < BAND)
            keep = (t == 0) | here | ((t == 2) & (z == 0))
            residual = jnp.where(keep, residual, 0.0)
            residual = jnp.where(t == 0, 0.25 * residual, residual)
            target = jnp.where(t == 0, BAND, jnp.where(here, local, 0))
            east = frac[0, s, :, 0, part]
            north = frac[0, s, :, 1, part]
            index = target * ROWS + lax.shift_right_logical(at, 7)
            column = lax.bitwise_and(at, LANES - 1)
            first = s * 8 + h * 4
            values = (column.astype(F32), east, residual * (1.0 - north), residual * north)
            for j, value in enumerate(values):
                out[pl.ds(first + j, OWNERS, stride=BLOCK), :] = value
            out[pl.ds(16 + s * 2 + h, OWNERS, stride=BLOCK), :] = index.astype(F32)
        out[pl.ds(22 + s, OWNERS, stride=BLOCK), :] = jnp.zeros((OWNERS, LANES), F32)


def make_pairs(select, pairs, block, half, at):
    parts = jnp.concatenate(three_parts(block) + [jnp.zeros_like(block)], 0)
    spread = lax.dot_general(
        parts.astype(BF16), select[half], (((0,), (0,)), ((), ())), preferred_element_type=F32
    )
    column, east, south, north = (
        spread[:, j * LANES : (j + 1) * LANES] for j in range(4)
    )
    lanes = lax.broadcasted_iota(jnp.int32, (LANES, LANES), 1).astype(F32)
    weight = jnp.maximum(0.0, 1.0 - jnp.abs((lanes - column) - east))
    pairs[pl.ds(at, LANES, stride=2), :] = weight * south
    pairs[pl.ds(at + 1, LANES, stride=2), :] = weight * north


def spread(s, far_places, slots, select, pairs, places, sem, accs, first_cleared, ready):
    fetch = pltpu.make_async_copy(far_places, places, sem)
    fetch.start()
    row = lax.broadcasted_iota(jnp.int32, (32, 4 * LANES), 0)
    group = lax.shift_right_logical(lax.broadcasted_iota(jnp.int32, (32, 4 * LANES), 1), 7)
    for h in range(2):
        hit = (lax.bitwise_and(row, 7) == group + 4 * h) & (row < 24)
        select[h] = jnp.where(hit, 1.0, 0.0).astype(BF16)
    share = PLANES * ROWS // OWNERS

    def west(o, _):
        for acc in accs[first_cleared:]:
            acc[pl.ds(pl.multiple_of(o * share, 8), share), :] = jnp.zeros((share, LANES), F32)
        block = slots[pl.ds(pl.multiple_of(o * BLOCK + s * 8, 8), 8), :]
        make_pairs(select, pairs, block, 0, o * 2 * CAP)
        return 0

    lax.fori_loop(0, OWNERS, west, 0, unroll=4)
    fetch.wait()

    def most(o, value):
        return jnp.maximum(value, places[o * 8 * LANES + (4 + s) * LANES])

    @pl.when(lax.fori_loop(0, OWNERS, most, jnp.int32(0), unroll=8) > LANES)
    def _():
        def east(o, _):
            block = slots[pl.ds(pl.multiple_of(o * BLOCK + s * 8, 8), 8), :]
            make_pairs(select, pairs, block, 1, o * 2 * CAP + 2 * LANES)
            return 0

        lax.fori_loop(0, OWNERS, east, 0, unroll=4)

    for copy in ready:
        copy.wait()

    def owner(o, _):
        count = places[o * 8 * LANES + (4 + s) * LANES]

        def step(c, _):
            at = o * 8 * LANES + s * CAP + c * CHUNK
            pair = o * 2 * CAP + c * 2 * CHUNK
            for j in range(CHUNK):
                acc = accs[j % len(accs)]
                r = places[at + j]
                acc[pl.ds(r, 2), :] = acc[pl.ds(r, 2), :] + pairs[pl.ds(pair + 2 * j, 2), :]
            return 0

        return lax.fori_loop(0, lax.div(count + (CHUNK - 1), CHUNK), step, 0)

    lax.fori_loop(0, OWNERS, owner, 0)


def total_of(accs, plane, at):
    value = accs[0][pl.ds(plane * ROWS + at, STRIP), :]
    for acc in accs[1:]:
        value = value + acc[pl.ds(plane * ROWS + at, STRIP), :]
    return value


def edge_columns(into, lanes, k, value):
    rolled = pltpu.roll(value, 2 * k + 1, 1)
    return jnp.where((lanes == 2 * k) | (lanes == 2 * k + 1), rolled, into)


def send_edges(edges, at, turned, to_west, to_east, part):
    turned[...] = edges[pl.ds(at, LANES), :].T[0:16, :]
    to_west[:, part] = turned[pl.ds(1, BAND, stride=2), :]
    to_east[:, part] = turned[pl.ds(0, BAND, stride=2), :]


def rims(east, coriolis, vertical, land, out, columns):
    lanes = lane_ids()
    for r in range(0, LANES, STRIP):
        rows = slice(r, r + STRIP)
        value = jnp.zeros((STRIP, LANES), F32)
        total = vertical[0, rows, :]
        for k in range(BAND):
            e = east[k, rows, :]
            c = coriolis[k, rows, :]
            value = edge_columns(value, lanes, k, jnp.where(lanes == 0, e - c, e + c))
            if k:
                total = total + vertical[k, rows, :]
        out[rows, :] = value
        columns[rows, :] = total * land[rows, :].astype(F32)


def row_part(ref, c):
    return ref.at[:, pl.ds(c * PART, PART), :]


def late_kernel(
    far_places, slots, final, land, vertical, rim, masked, sums, to_west, to_east,
    select, pairs, places, edges, turned, v_s, o_s, sem, in_sem, out_sem, *accs,
):
    copies = [
        pltpu.make_async_copy(final.at[k], accs[0].at[pl.ds(k * ROWS, ROWS)], in_sem.at[k])
        for k in range(BAND)
    ]
    copies.append(pltpu.make_async_copy(vertical, v_s, in_sem.at[BAND]))
    for copy in copies:
        copy.start()
    accs[0][pl.ds(BAND * ROWS, ROWS), :] = jnp.zeros((ROWS, LANES), F32)
    spread(1, far_places, slots, select, pairs, places, sem, accs, 1, copies[:BAND])
    copies[BAND].wait()
    lanes = lane_ids()

    def one(i, _):
        at = pl.multiple_of(i * STRIP, STRIP)
        rows = pl.ds(at, STRIP)
        sea = land[rows, :].astype(F32)
        shared = total_of(accs, BAND, at)
        total = jnp.zeros((STRIP, LANES), F32)
        edge = jnp.zeros((STRIP, LANES), F32)
        for k in range(BAND):
            m = sea * (total_of(accs, k, at) + shared)
            o_s[k, rows, :] = m
            total = total + v_s[k, rows, :] * m
            edge = edge_columns(edge, lanes, k, m)
        sums[rows, :] = total
        edges[rows, :] = edge * rim[rows, :]
        return 0

    leaving = []
    for c in range(PARTS):
        lax.fori_loop(c * PART // STRIP, (c + 1) * PART // STRIP, one, 0, unroll=UNROLL)
        copy = pltpu.make_async_copy(row_part(o_s, c), row_part(masked, c), out_sem.at[c])
        copy.start()
        leaving.append(copy)
    for b in range(ROWS // LANES):
        part = slice(b * LANES, (b + 1) * LANES)
        send_edges(edges, b * LANES, turned, to_west, to_east, part)
    for copy in leaving:
        copy.wait()


def fetch_fields(sources, targets, sem):
    copies = []
    for c in range(PARTS):
        row = []
        for j, (source, target) in enumerate(zip(sources, targets)):
            copy = pltpu.make_async_copy(row_part(source, c), row_part(target, c), sem.at[c, j])
            copy.start()
            row.append(copy)
        copies.append(row)
    return copies


def rim_select(select):
    row = lax.broadcasted_iota(jnp.int32, (8 * BAND, BAND * LANES), 0)
    column = lax.broadcasted_iota(jnp.int32, (8 * BAND, BAND * LANES), 1)
    level = lax.shift_right_logical(column, 7)
    lane = lax.bitwise_and(column, LANES - 1)
    side = jnp.where(row < 3 * BAND, LANES - 1, 0)
    hit = (lax.bitwise_and(row, BAND - 1) == level) & (lane == side) & (row < 6 * BAND)
    select[...] = jnp.where(hit, 1.0, 0.0).astype(BF16)


def three_parts(value):
    high = value.astype(BF16).astype(F32)
    rest = value - high
    middle = rest.astype(BF16).astype(F32)
    return [high, middle, rest - middle]


def place_rims(from_east, from_west, select, placed):
    rim_select(select)
    for b in range(ROWS // LANES):
        part = slice(b * LANES, (b + 1) * LANES)
        east, west = from_east[:, part], from_west[:, part]
        empty = jnp.zeros((2 * BAND, LANES), F32)
        parts = jnp.concatenate(three_parts(east) + three_parts(west) + [empty], 0)
        placed[part, :] = lax.dot_general(
            parts.astype(BF16), select[...], (((0,), (0,)), ((), ())), preferred_element_type=F32
        )


def stencil(copies, masked, east, north, coriolis, vertical, flow, made, prepare_rows, start, added,
            finish, out, out_sem):
    for k in range(BAND):
        flow[k, 0:8, :] = jnp.zeros((8, LANES), F32)
        flow[k, ROWS + 8 : ROWS + 16, :] = jnp.zeros((8, LANES), F32)

    def first(i, _):
        at = pl.multiple_of(i * STRIP, STRIP)
        prepare_rows(at)
        rows = pl.ds(at, STRIP)
        for k in range(BAND):
            value = north[k, rows, :] * masked[k, rows, :]
            flow[k, pl.ds(pl.multiple_of(at + 8, 8), STRIP), :] = value
        return 0

    lanes = lane_ids()

    def second(i, _):
        at = pl.multiple_of(i * STRIP, STRIP)
        rows = pl.ds(at, STRIP)
        below = start(at)
        total = jnp.zeros((STRIP, LANES), F32)
        for k in reversed(range(BAND)):
            m = masked[k, rows, :]
            e = east[k, rows, :] * m
            c = coriolis[k, rows, :] * m
            v = vertical[k, rows, :]
            below = below + v * m
            ahead = jnp.where(lanes == LANES - 1, 0.0, pltpu.roll(e - c, LANES - 1, 1))
            behind = jnp.where(lanes == 0, 0.0, pltpu.roll(e + c, 1, 1))
            across = (
                flow[k, pl.ds(at + 7, STRIP), :]
                + flow[k, pl.ds(at + 9, STRIP), :]
                - 2.0 * flow[k, pl.ds(pl.multiple_of(at + 8, 8), STRIP), :]
            )
            value = m + (ahead + behind - 2.0 * e) + across + below + added(k, at)
            made[k, rows, :] = value
            total = total + v * value
        finish(at, total)
        return 0

    leaving = []
    for c in range(PARTS + 1):
        if c < PARTS:
            for copy in copies[c]:
                copy.wait()
            lax.fori_loop(c * PART // STRIP, (c + 1) * PART // STRIP, first, 0, unroll=UNROLL)
        if c > 0:
            lax.fori_loop((c - 1) * PART // STRIP, c * PART // STRIP, second, 0, unroll=UNROLL)
            copy = pltpu.make_async_copy(
                row_part(made, c - 1), row_part(out, c - 1), out_sem.at[c - 1]
            )
            copy.start()
            leaving.append(copy)
    return leaving


def early_kernel(
    far_places, slots, land, from_east, from_west, masked, east, north, coriolis, vertical,
    out, sums,
    select, pairs, places, rim_picks, placed, m_s, e_s, n_s, c_s, v_s, flow, made,
    sem, in_sem, out_sem, *accs,
):
    copies = fetch_fields(
        (masked, east, north, coriolis, vertical), (m_s, e_s, n_s, c_s, v_s), in_sem
    )
    place_rims(from_east, from_west, rim_picks, placed)
    spread(0, far_places, slots, select, pairs, places, sem, accs, 0, ())

    def start(at):
        return total_of(accs, BAND, at)

    def added(k, at):
        rows = pl.ds(at, STRIP)
        return total_of(accs, k, at) + placed[rows, k * LANES : (k + 1) * LANES]

    def finish(at, total):
        rows = pl.ds(at, STRIP)
        sums[rows, :] = total * land[rows, :].astype(F32)

    leaving = stencil(
        copies, m_s, e_s, n_s, c_s, v_s, flow, made, lambda at: None, start, added, finish, out, out_sem
    )
    for copy in leaving:
        copy.wait()


def middle_kernel(
    picks, one_up, two_up, three_up, columns, far_columns, own, later, land, rim,
    field, east, north, coriolis, vertical, out, to_west, to_east, onward,
    edges, turned, m_s, e_s, n_s, c_s, v_s, flow, made, in_sem, out_sem,
):
    copies = fetch_fields(
        (field, east, north, coriolis, vertical), (m_s, e_s, n_s, c_s, v_s), in_sem
    )
    lanes = lane_ids()

    def prepare_rows(at):
        rows = pl.ds(at, STRIP)
        sea = land[rows, :].astype(F32)
        higher = one_up[rows, :] + two_up[rows, :] + three_up[rows, :]
        edge = jnp.zeros((STRIP, LANES), F32)
        for k in range(BAND):
            m = sea * (m_s[k, rows, :] + higher)
            m_s[k, rows, :] = m
            edge = edge_columns(edge, lanes, k, m)
        edges[rows, :] = edge * rim[rows, :]

    def start(at):
        rows = pl.ds(at, STRIP)
        one, two, three = one_up[rows, :], two_up[rows, :], three_up[rows, :]
        near, other = columns[rows, :], far_columns[rows, :]
        onward[rows, :] = (
            picks[0] * later[rows, :]
            + near * (picks[1] * one + picks[2] * two)
            + other * (picks[3] * own[rows, :] + picks[4] * two)
        )
        return other * (picks[5] * two + picks[6] * three)

    leaving = stencil(
        copies, m_s, e_s, n_s, c_s, v_s, flow, made, prepare_rows, start, lambda k, at: 0.0,
        lambda at, total: None, out, out_sem,
    )
    for b in range(ROWS // LANES):
        part = slice(b * LANES, (b + 1) * LANES)
        send_edges(edges, b * LANES, turned, to_west, to_east, part)
    for copy in leaving:
        copy.wait()


def rim_kernel(field, from_east, from_west, out, select, placed):
    step = pl.program_id(0)

    @pl.when(step == 0)
    def _():
        place_rims(from_east, from_west, select, placed)

    for r in range(0, LANES, STRIP):
        rows = slice(r, r + STRIP)
        at = pl.multiple_of(step * LANES + r, STRIP)
        for k in range(BAND):
            rim = placed[pl.ds(at, STRIP), k * LANES : (k + 1) * LANES]
            out[k, rows, :] = field[k, rows, :] + rim


def shape(*dims):
    return jax.ShapeDtypeStruct(dims, F32)


def vm(count):
    return [pl.BlockSpec(memory_space=VMEM)] * count


def sm(count):
    return [pl.BlockSpec(memory_space=SMEM)] * count


def far(count):
    return [pl.BlockSpec(memory_space=pl.ANY)] * count


def fields_by_rows(count):
    return [pl.BlockSpec((BAND, LANES, LANES), lambda i: (0, i, 0))] * count


def planes_by_rows(count):
    return [pl.BlockSpec((LANES, LANES), lambda i: (i, 0))] * count


def call(kernel, ins, outs, shapes, scratch, moved, *args, grid=()):
    many = len(outs) > 1
    return pl.pallas_call(
        kernel,
        grid=grid,
        in_specs=ins,
        out_specs=tuple(outs) if many else outs[0],
        out_shape=tuple(shapes) if many else shapes[0],
        scratch_shapes=scratch,
        compiler_params=pltpu.CompilerParams(vmem_limit_bytes=LIMIT),
        cost_estimate=pl.CostEstimate(flops=moved, bytes_accessed=moved, transcendentals=0),
    )(*args)


def from_deeper(part):
    return (
        lax.ppermute(part, "lev", [(3, 2), (2, 1), (1, 0)]),
        lax.ppermute(part, "lev", [(3, 1), (2, 0)]),
        lax.ppermute(part, "lev", [(3, 0)]),
    )


def by_core(part, first_core, second_core):
    bands = lax.axis_size("lev")
    pairs = [
        (tile * bands + source, tile * bands + target)
        for tile in range(lax.axis_size("tile"))
        for source, target in (second_core if tile % 2 else first_core)
    ]
    return lax.ppermute(part, ("tile", "lev"), pairs)


PICKS = (
    ((0, 0, 0, 0, 0, 1, 1, 0, 1), (0,) * 9, (1, 1, 0, 0, 0, 0, 0, 1, 1), (1, 0, 0, 1, 0, 0, 0, 1, 0)),
    ((0, 0, 0, 0, 0, 0, 0, 1, 1), (1, 1, 1, 0, 1, 1, 0, 1, 1), (0,) * 9, (1, 0, 0, 0, 0, 0, 0, 0, 0)),
)


def core_picks():
    core = lax.rem(lax.axis_index("tile"), 2)
    at = core * 4 + lax.axis_index("lev")
    table = jnp.array(PICKS, F32).reshape(8, 9)
    return lax.dynamic_index_in_dim(table, at, 0, False)


def from_sides(to_west, to_east):
    count = lax.axis_size("tile")
    return (
        lax.ppermute(to_west, "tile", [((i + 1) % count, i) for i in range(count)]),
        lax.ppermute(to_east, "tile", [(i, (i + 1) % count) for i in range(count)]),
    )


def body(
    final_adjoint,
    east_coef,
    north_coef,
    coriolis_coef,
    vertical_coef,
    land_sea,
    counts,
    obs_cell,
    obs_frac,
    innovation,
    obs_type,
    obs_level,
    type_weight,
):
    band = lax.axis_index("lev").astype(jnp.int32).reshape(1)
    picks = core_picks()
    field = shape(BAND, ROWS, LANES)
    plane = shape(ROWS, LANES)
    edge = shape(BAND, ROWS)
    strips = (ROWS // LANES,)
    dma = pltpu.SemaphoreType.DMA
    send = call(
        prepare, sm(2) + vm(6), vm(1), [shape(OWNERS * BLOCK, LANES)], [], 1 << 20,
        band, type_weight, counts, obs_cell, obs_frac, innovation, obs_type, obs_level,
    )
    arrived = lax.all_to_all(
        send.reshape(OWNERS, BLOCK, LANES), "tile", split_axis=0, concat_axis=0, tiled=True
    )
    rim, columns = call(
        rims, fields_by_rows(3) + planes_by_rows(1), planes_by_rows(2), [plane, plane], [],
        10 << 20, east_coef, coriolis_coef, vertical_coef, land_sea, grid=strips,
    )
    far_columns = by_core(columns, ((1, 0), (2, 3)), ((2, 1),))
    places = arrived[:, 16:24, :].astype(jnp.int32).reshape(-1)
    slots = arrived.reshape(OWNERS * BLOCK, LANES)
    acc = VMEM((PLANES * ROWS + 8, LANES), F32)
    spread_scratch = [
        VMEM((2, 32, 4 * LANES), BF16),
        VMEM((OWNERS * CAP * 2, LANES), F32),
        SMEM((OWNERS * 8 * LANES,), jnp.int32),
    ]
    turned = [VMEM((2 * BAND, LANES), F32)]
    masked, sums, to_west, to_east = call(
        late_kernel, far(1) + vm(1) + far(1) + vm(1) + far(1) + vm(1), far(1) + vm(3),
        [field, plane, edge, edge],
        spread_scratch + [VMEM((ROWS, LANES), F32)] + turned + [VMEM((BAND, ROWS, LANES), F32)] * 2
        + [dma, dma((BAND + 1,)), dma((PARTS,))] + [acc] * LATE_ACCS,
        10 << 20,
        places, slots, final_adjoint, land_sea, vertical_coef, rim,
    )
    sides = from_sides(to_west, to_east)
    ups = from_deeper(sums)
    stored = VMEM((BAND, ROWS, LANES), F32)
    wide = VMEM((BAND, ROWS + 16, LANES), F32)
    stencil_scratch = [stored] * 5 + [wide, stored]
    stencil_sems = [dma((PARTS, 5)), dma((PARTS,))]
    rim_scratch = [VMEM((8 * BAND, BAND * LANES), BF16), VMEM((ROWS, BAND * LANES), F32)]
    first, later = call(
        early_kernel, far(1) + vm(4) + far(5), far(1) + vm(1), [field, plane],
        spread_scratch + rim_scratch + stencil_scratch + [dma] + stencil_sems
        + [acc] * EARLY_ACCS,
        40 << 20,
        places, slots, land_sea, *sides,
        masked, east_coef, north_coef, coriolis_coef, vertical_coef,
    )
    near_sums = by_core(later, ((3, 2), (2, 3), (1, 0)), ((2, 1), (3, 0)))
    second, to_west, to_east, onward = call(
        middle_kernel, sm(1) + vm(9) + far(5), far(1) + vm(3), [field, edge, edge, plane],
        [VMEM((ROWS, LANES), F32)] + turned + stencil_scratch + stencil_sems, 24 << 20,
        picks, *ups, columns, far_columns, sums, later, land_sea, rim,
        first, east_coef, north_coef, coriolis_coef, vertical_coef,
    )
    rest_sums = by_core(
        onward + picks[7] * near_sums, ((2, 1), (3, 0)), ((0, 1), (1, 0), (3, 2))
    )
    sides = from_sides(to_west, to_east)
    whole_edge = [pl.BlockSpec((BAND, ROWS), lambda i: (0, 0))] * 2
    third = call(
        rim_kernel, fields_by_rows(1) + whole_edge, fields_by_rows(1),
        [field], rim_scratch, 7 << 20, second, *sides, grid=strips,
    )
    return third + (picks[8] * near_sums + rest_sums)[None]


def solution(mesh):
    return jax.shard_map(
        body,
        mesh=mesh,
        in_specs=(
            P("lev", None, "tile"),
            P("lev", None, "tile"),
            P("lev", None, "tile"),
            P("lev", None, "tile"),
            P("lev", None, "tile"),
            P(None, "tile"),
            P("tile", None, None),
            P("tile", None, None, None),
            P("tile", None, None, None, None),
            P("tile", None, None, None),
            P("tile", None, None, None),
            P("tile", None, None, None),
            P(),
        ),
        out_specs=P("lev", None, "tile"),
        check_vma=False,
    )
```

```python
import jax
import jax.numpy as jnp
from jax import lax
from jax.experimental import pallas as pl
from jax.experimental.pallas import tpu as pltpu
from jax.sharding import PartitionSpec as P

LANES = 128
ROWS = 768
BAND = 8
CAP = 256
OWNERS = 32
BLOCK = 24
CHUNK = 32
LATE_ACCS = 6
EARLY_ACCS = 6
STRIP = 32
UNROLL = 4
PARTS = 6
PART = ROWS // PARTS
PLANES = BAND + 1
LIMIT = 63 << 20
VMEM = pltpu.VMEM
SMEM = pltpu.SMEM
F32 = jnp.float32
BF16 = jnp.bfloat16


def lane_ids():
    return lax.broadcasted_iota(jnp.int32, (STRIP, LANES), 1)


def prepare(band, weight, counts, cell, frac, innovation, kind, level, out):
    z = band[0]
    ids = lax.broadcasted_iota(jnp.int32, (OWNERS, LANES), 1)
    for s in range(2):
        own = lax.broadcasted_iota(jnp.int32, (OWNERS, OWNERS), 0)
        other = lax.broadcasted_iota(jnp.int32, (OWNERS, OWNERS), 1)
        row = jnp.broadcast_to(counts[0, s : s + 1, :].astype(F32), (OWNERS, OWNERS))
        count = jnp.sum(jnp.where(own == other, row, 0.0), 1, keepdims=True)
        out[pl.ds(20 + s, OWNERS, stride=BLOCK), :] = jnp.broadcast_to(count, (OWNERS, LANES))
        for h in range(2):
            part = slice(h * LANES, (h + 1) * LANES)
            t = kind[0, s, :, part]
            at = cell[0, s, :, part]
            scale = jnp.where(t == 0, weight[0], jnp.where(t == 1, weight[1], weight[2]))
            live = (ids + h * LANES).astype(F32) < count
            residual = jnp.where(live, scale * innovation[0, s, :, part], 0.0)
            local = level[0, s, :, part] - z * BAND
            here = (t == 1) & (local >= 0) & (local < BAND)
            keep = (t == 0) | here | ((t == 2) & (z == 0))
            residual = jnp.where(keep, residual, 0.0)
            residual = jnp.where(t == 0, 0.25 * residual, residual)
            target = jnp.where(t == 0, BAND, jnp.where(here, local, 0))
            east = frac[0, s, :, 0, part]
            north = frac[0, s, :, 1, part]
            index = target * ROWS + lax.shift_right_logical(at, 7)
            column = lax.bitwise_and(at, LANES - 1)
            first = s * 8 + h * 4
            values = (column.astype(F32), east, residual * (1.0 - north), residual * north)
            for j, value in enumerate(values):
                out[pl.ds(first + j, OWNERS, stride=BLOCK), :] = value
            out[pl.ds(16 + s * 2 + h, OWNERS, stride=BLOCK), :] = index.astype(F32)
        out[pl.ds(22 + s, OWNERS, stride=BLOCK), :] = jnp.zeros((OWNERS, LANES), F32)


def make_pairs(select, pairs, block, half, at):
    parts = jnp.concatenate(three_parts(block) + [jnp.zeros_like(block)], 0)
    spread = lax.dot_general(
        parts.astype(BF16), select[half], (((0,), (0,)), ((), ())), preferred_element_type=F32
    )
    column, east, south, north = (
        spread[:, j * LANES : (j + 1) * LANES] for j in range(4)
    )
    lanes = lax.broadcasted_iota(jnp.int32, (LANES, LANES), 1).astype(F32)
    weight = jnp.maximum(0.0, 1.0 - jnp.abs((lanes - column) - east))
    pairs[pl.ds(at, LANES, stride=2), :] = weight * south
    pairs[pl.ds(at + 1, LANES, stride=2), :] = weight * north


def spread(s, far_places, slots, select, pairs, places, sem, accs, first_cleared, ready):
    fetch = pltpu.make_async_copy(far_places, places, sem)
    fetch.start()
    row = lax.broadcasted_iota(jnp.int32, (32, 4 * LANES), 0)
    group = lax.shift_right_logical(lax.broadcasted_iota(jnp.int32, (32, 4 * LANES), 1), 7)
    for h in range(2):
        hit = (lax.bitwise_and(row, 7) == group + 4 * h) & (row < 24)
        select[h] = jnp.where(hit, 1.0, 0.0).astype(BF16)
    share = PLANES * ROWS // OWNERS

    def west(o, _):
        for acc in accs[first_cleared:]:
            acc[pl.ds(pl.multiple_of(o * share, 8), share), :] = jnp.zeros((share, LANES), F32)
        block = slots[pl.ds(pl.multiple_of(o * BLOCK + s * 8, 8), 8), :]
        make_pairs(select, pairs, block, 0, o * 2 * CAP)
        return 0

    lax.fori_loop(0, OWNERS, west, 0, unroll=4)
    fetch.wait()

    def most(o, value):
        return jnp.maximum(value, places[o * 8 * LANES + (4 + s) * LANES])

    @pl.when(lax.fori_loop(0, OWNERS, most, jnp.int32(0), unroll=8) > LANES)
    def _():
        def east(o, _):
            block = slots[pl.ds(pl.multiple_of(o * BLOCK + s * 8, 8), 8), :]
            make_pairs(select, pairs, block, 1, o * 2 * CAP + 2 * LANES)
            return 0

        lax.fori_loop(0, OWNERS, east, 0, unroll=4)

    for copy in ready:
        copy.wait()

    def owner(o, _):
        count = places[o * 8 * LANES + (4 + s) * LANES]

        def step(c, _):
            at = o * 8 * LANES + s * CAP + c * CHUNK
            pair = o * 2 * CAP + c * 2 * CHUNK
            for j in range(CHUNK):
                acc = accs[j % len(accs)]
                r = places[at + j]
                acc[pl.ds(r, 2), :] = acc[pl.ds(r, 2), :] + pairs[pl.ds(pair + 2 * j, 2), :]
            return 0

        return lax.fori_loop(0, lax.div(count + (CHUNK - 1), CHUNK), step, 0)

    lax.fori_loop(0, OWNERS, owner, 0)


def total_of(accs, plane, at):
    value = accs[0][pl.ds(plane * ROWS + at, STRIP), :]
    for acc in accs[1:]:
        value = value + acc[pl.ds(plane * ROWS + at, STRIP), :]
    return value


def edge_columns(into, lanes, k, value):
    rolled = pltpu.roll(value, 2 * k + 1, 1)
    return jnp.where((lanes == 2 * k) | (lanes == 2 * k + 1), rolled, into)


def send_edges(edges, at, turned, to_west, to_east, part):
    turned[...] = edges[pl.ds(at, LANES), :].T[0:16, :]
    to_west[:, part] = turned[pl.ds(1, BAND, stride=2), :]
    to_east[:, part] = turned[pl.ds(0, BAND, stride=2), :]


def rims(east, coriolis, vertical, land, out, columns):
    lanes = lane_ids()
    for r in range(0, LANES, STRIP):
        rows = slice(r, r + STRIP)
        value = jnp.zeros((STRIP, LANES), F32)
        total = vertical[0, rows, :]
        for k in range(BAND):
            e = east[k, rows, :]
            c = coriolis[k, rows, :]
            value = edge_columns(value, lanes, k, jnp.where(lanes == 0, e - c, e + c))
            if k:
                total = total + vertical[k, rows, :]
        out[rows, :] = value
        columns[rows, :] = total * land[rows, :].astype(F32)


def row_part(ref, c):
    return ref.at[:, pl.ds(c * PART, PART), :]


def late_kernel(
    far_places, slots, final, land, vertical, rim, masked, sums, to_west, to_east,
    select, pairs, places, edges, turned, v_s, o_s, sem, in_sem, out_sem, *accs,
):
    copies = [
        pltpu.make_async_copy(final.at[k], accs[0].at[pl.ds(k * ROWS, ROWS)], in_sem.at[k])
        for k in range(BAND)
    ]
    copies.append(pltpu.make_async_copy(vertical, v_s, in_sem.at[BAND]))
    for copy in copies:
        copy.start()
    accs[0][pl.ds(BAND * ROWS, ROWS), :] = jnp.zeros((ROWS, LANES), F32)
    spread(1, far_places, slots, select, pairs, places, sem, accs, 1, copies[:BAND])
    copies[BAND].wait()
    lanes = lane_ids()

    def one(i, _):
        at = pl.multiple_of(i * STRIP, STRIP)
        rows = pl.ds(at, STRIP)
        sea = land[rows, :].astype(F32)
        shared = total_of(accs, BAND, at)
        total = jnp.zeros((STRIP, LANES), F32)
        edge = jnp.zeros((STRIP, LANES), F32)
        for k in range(BAND):
            m = sea * (total_of(accs, k, at) + shared)
            o_s[k, rows, :] = m
            total = total + v_s[k, rows, :] * m
            edge = edge_columns(edge, lanes, k, m)
        sums[rows, :] = total
        edges[rows, :] = edge * rim[rows, :]
        return 0

    leaving = []
    for c in range(PARTS):
        lax.fori_loop(c * PART // STRIP, (c + 1) * PART // STRIP, one, 0, unroll=UNROLL)
        copy = pltpu.make_async_copy(row_part(o_s, c), row_part(masked, c), out_sem.at[c])
        copy.start()
        leaving.append(copy)
    for b in range(ROWS // LANES):
        part = slice(b * LANES, (b + 1) * LANES)
        send_edges(edges, b * LANES, turned, to_west, to_east, part)
    for copy in leaving:
        copy.wait()


def fetch_fields(sources, targets, sem):
    copies = []
    for c in range(PARTS):
        row = []
        for j, (source, target) in enumerate(zip(sources, targets)):
            copy = pltpu.make_async_copy(row_part(source, c), row_part(target, c), sem.at[c, j])
            copy.start()
            row.append(copy)
        copies.append(row)
    return copies


def rim_select(select):
    row = lax.broadcasted_iota(jnp.int32, (8 * BAND, BAND * LANES), 0)
    column = lax.broadcasted_iota(jnp.int32, (8 * BAND, BAND * LANES), 1)
    level = lax.shift_right_logical(column, 7)
    lane = lax.bitwise_and(column, LANES - 1)
    side = jnp.where(row < 3 * BAND, LANES - 1, 0)
    hit = (lax.bitwise_and(row, BAND - 1) == level) & (lane == side) & (row < 6 * BAND)
    select[...] = jnp.where(hit, 1.0, 0.0).astype(BF16)


def three_parts(value):
    high = value.astype(BF16).astype(F32)
    rest = value - high
    middle = rest.astype(BF16).astype(F32)
    return [high, middle, rest - middle]


def place_rims(from_east, from_west, select, placed):
    rim_select(select)
    for b in range(ROWS // LANES):
        part = slice(b * LANES, (b + 1) * LANES)
        east, west = from_east[:, part], from_west[:, part]
        empty = jnp.zeros((2 * BAND, LANES), F32)
        parts = jnp.concatenate(three_parts(east) + three_parts(west) + [empty], 0)
        placed[part, :] = lax.dot_general(
            parts.astype(BF16), select[...], (((0,), (0,)), ((), ())), preferred_element_type=F32
        )


def stencil(copies, masked, east, north, coriolis, vertical, flow, made, prepare_rows, start, added,
            finish, out, out_sem):
    for k in range(BAND):
        flow[k, 0:8, :] = jnp.zeros((8, LANES), F32)
        flow[k, ROWS + 8 : ROWS + 16, :] = jnp.zeros((8, LANES), F32)

    def first(i, _):
        at = pl.multiple_of(i * STRIP, STRIP)
        prepare_rows(at)
        rows = pl.ds(at, STRIP)
        for k in range(BAND):
            value = north[k, rows, :] * masked[k, rows, :]
            flow[k, pl.ds(pl.multiple_of(at + 8, 8), STRIP), :] = value
        return 0

    lanes = lane_ids()

    def second(i, _):
        at = pl.multiple_of(i * STRIP, STRIP)
        rows = pl.ds(at, STRIP)
        below = start(at)
        total = jnp.zeros((STRIP, LANES), F32)
        for k in reversed(range(BAND)):
            m = masked[k, rows, :]
            e = east[k, rows, :] * m
            c = coriolis[k, rows, :] * m
            v = vertical[k, rows, :]
            below = below + v * m
            ahead = jnp.where(lanes == LANES - 1, 0.0, pltpu.roll(e - c, LANES - 1, 1))
            behind = jnp.where(lanes == 0, 0.0, pltpu.roll(e + c, 1, 1))
            across = (
                flow[k, pl.ds(at + 7, STRIP), :]
                + flow[k, pl.ds(at + 9, STRIP), :]
                - 2.0 * flow[k, pl.ds(pl.multiple_of(at + 8, 8), STRIP), :]
            )
            value = m + (ahead + behind - 2.0 * e) + across + below + added(k, at)
            made[k, rows, :] = value
            total = total + v * value
        finish(at, total)
        return 0

    leaving = []
    for c in range(PARTS + 1):
        if c < PARTS:
            for copy in copies[c]:
                copy.wait()
            lax.fori_loop(c * PART // STRIP, (c + 1) * PART // STRIP, first, 0, unroll=UNROLL)
        if c > 0:
            lax.fori_loop((c - 1) * PART // STRIP, c * PART // STRIP, second, 0, unroll=UNROLL)
            copy = pltpu.make_async_copy(
                row_part(made, c - 1), row_part(out, c - 1), out_sem.at[c - 1]
            )
            copy.start()
            leaving.append(copy)
    return leaving


def early_kernel(
    far_places, slots, land, from_east, from_west, masked, east, north, coriolis, vertical,
    out, sums,
    select, pairs, places, rim_picks, placed, m_s, e_s, n_s, c_s, v_s, flow, made,
    sem, in_sem, out_sem, *accs,
):
    copies = fetch_fields(
        (masked, east, north, coriolis, vertical), (m_s, e_s, n_s, c_s, v_s), in_sem
    )
    place_rims(from_east, from_west, rim_picks, placed)
    spread(0, far_places, slots, select, pairs, places, sem, accs, 0, ())

    def start(at):
        return total_of(accs, BAND, at)

    def added(k, at):
        rows = pl.ds(at, STRIP)
        return total_of(accs, k, at) + placed[rows, k * LANES : (k + 1) * LANES]

    def finish(at, total):
        rows = pl.ds(at, STRIP)
        sums[rows, :] = total * land[rows, :].astype(F32)

    leaving = stencil(
        copies, m_s, e_s, n_s, c_s, v_s, flow, made, lambda at: None, start, added, finish, out, out_sem
    )
    for copy in leaving:
        copy.wait()


def pass_on(band, own, arrived, out):
    out[...] = jnp.where(band[0] == 0, 0.0, 1.0) * own[...] + arrived[...]


def middle_kernel(
    band, near, rest, columns, far_columns, own, later, land, rim,
    field, east, north, coriolis, vertical, out, to_west, to_east, onward,
    edges, turned, m_s, e_s, n_s, c_s, v_s, flow, made, in_sem, out_sem,
):
    z = band[0]
    inner = jnp.where(z == 3, 0.0, 1.0)

    copies = fetch_fields(
        (field, east, north, coriolis, vertical), (m_s, e_s, n_s, c_s, v_s), in_sem
    )
    lanes = lane_ids()

    def prepare_rows(at):
        rows = pl.ds(at, STRIP)
        sea = land[rows, :].astype(F32)
        higher = inner * near[rows, :] + rest[rows, :]
        edge = jnp.zeros((STRIP, LANES), F32)
        for k in range(BAND):
            m = sea * (m_s[k, rows, :] + higher)
            m_s[k, rows, :] = m
            edge = edge_columns(edge, lanes, k, m)
        edges[rows, :] = edge * rim[rows, :]

    def start(at):
        rows = pl.ds(at, STRIP)
        higher = inner * near[rows, :] + rest[rows, :]
        other = far_columns[rows, :]
        onward[rows, :] = later[rows, :] + columns[rows, :] * higher + other * jnp.where(
            z == 3, own[rows, :], rest[rows, :]
        )
        return other * rest[rows, :]

    leaving = stencil(
        copies, m_s, e_s, n_s, c_s, v_s, flow, made, prepare_rows, start, lambda k, at: 0.0,
        lambda at, total: None, out, out_sem,
    )
    for b in range(ROWS // LANES):
        part = slice(b * LANES, (b + 1) * LANES)
        send_edges(edges, b * LANES, turned, to_west, to_east, part)
    for copy in leaving:
        copy.wait()


def rim_kernel(from_east, from_west, placed, select):
    place_rims(from_east, from_west, select, placed)


def last_kernel(band, field, placed, near, rest, out):
    inner = jnp.where(band[0] == 3, 0.0, 1.0)
    for r in range(0, LANES, STRIP):
        rows = slice(r, r + STRIP)
        higher = inner * near[rows, :] + rest[rows, :]
        for k in range(BAND):
            rim = placed[rows, k * LANES : (k + 1) * LANES]
            out[k, rows, :] = field[k, rows, :] + higher + rim


def shape(*dims):
    return jax.ShapeDtypeStruct(dims, F32)


def vm(count):
    return [pl.BlockSpec(memory_space=VMEM)] * count


def sm(count):
    return [pl.BlockSpec(memory_space=SMEM)] * count


def far(count):
    return [pl.BlockSpec(memory_space=pl.ANY)] * count


def fields_by_rows(count):
    return [pl.BlockSpec((BAND, LANES, LANES), lambda i: (0, i, 0))] * count


def planes_by_rows(count):
    return [pl.BlockSpec((LANES, LANES), lambda i: (i, 0))] * count


def call(kernel, ins, outs, shapes, scratch, moved, *args, grid=()):
    many = len(outs) > 1
    return pl.pallas_call(
        kernel,
        grid=grid,
        in_specs=ins,
        out_specs=tuple(outs) if many else outs[0],
        out_shape=tuple(shapes) if many else shapes[0],
        scratch_shapes=scratch,
        compiler_params=pltpu.CompilerParams(vmem_limit_bytes=LIMIT),
        cost_estimate=pl.CostEstimate(flops=moved, bytes_accessed=moved, transcendentals=0),
    )(*args)


def by_core(part, first_core, second_core):
    bands = lax.axis_size("lev")
    pairs = [
        (tile * bands + source, tile * bands + target)
        for tile in range(lax.axis_size("tile"))
        for source, target in (second_core if tile % 2 else first_core)
    ]
    return lax.ppermute(part, ("tile", "lev"), pairs)


def step_one(part):
    return by_core(part, ((3, 2), (2, 3), (1, 0)), ((2, 1), (3, 0)))


def step_two(part):
    return by_core(part, ((2, 1), (3, 0)), ((0, 1), (1, 0), (3, 2)))


def from_sides(to_west, to_east):
    count = lax.axis_size("tile")
    return (
        lax.ppermute(to_west, "tile", [((i + 1) % count, i) for i in range(count)]),
        lax.ppermute(to_east, "tile", [(i, (i + 1) % count) for i in range(count)]),
    )


def body(
    final_adjoint,
    east_coef,
    north_coef,
    coriolis_coef,
    vertical_coef,
    land_sea,
    counts,
    obs_cell,
    obs_frac,
    innovation,
    obs_type,
    obs_level,
    type_weight,
):
    band = lax.axis_index("lev").astype(jnp.int32).reshape(1)
    field = shape(BAND, ROWS, LANES)
    plane = shape(ROWS, LANES)
    edge = shape(BAND, ROWS)
    strips = (ROWS // LANES,)
    dma = pltpu.SemaphoreType.DMA
    send = call(
        prepare, sm(2) + vm(6), vm(1), [shape(OWNERS * BLOCK, LANES)], [], 1 << 20,
        band, type_weight, counts, obs_cell, obs_frac, innovation, obs_type, obs_level,
    )
    arrived = lax.all_to_all(
        send.reshape(OWNERS, BLOCK, LANES), "tile", split_axis=0, concat_axis=0, tiled=True
    )
    rim, columns = call(
        rims, fields_by_rows(3) + planes_by_rows(1), planes_by_rows(2), [plane, plane], [],
        10 << 20, east_coef, coriolis_coef, vertical_coef, land_sea, grid=strips,
    )
    far_columns = by_core(columns, ((1, 0), (2, 3)), ((2, 1),))
    places = arrived[:, 16:24, :].astype(jnp.int32).reshape(-1)
    slots = arrived.reshape(OWNERS * BLOCK, LANES)
    acc = VMEM((PLANES * ROWS + 8, LANES), F32)
    spread_scratch = [
        VMEM((2, 32, 4 * LANES), BF16),
        VMEM((OWNERS * CAP * 2, LANES), F32),
        SMEM((OWNERS * 8 * LANES,), jnp.int32),
    ]
    turned = [VMEM((2 * BAND, LANES), F32)]
    masked, sums, to_west, to_east = call(
        late_kernel, far(1) + vm(1) + far(1) + vm(1) + far(1) + vm(1), far(1) + vm(3),
        [field, plane, edge, edge],
        spread_scratch + [VMEM((ROWS, LANES), F32)] + turned + [VMEM((BAND, ROWS, LANES), F32)] * 2
        + [dma, dma((BAND + 1,)), dma((PARTS,))] + [acc] * LATE_ACCS,
        10 << 20,
        places, slots, final_adjoint, land_sea, vertical_coef, rim,
    )
    sides = from_sides(to_west, to_east)
    near = step_one(sums)
    rest = step_two(call(pass_on, sm(1) + vm(2), vm(1), [plane], [], 1 << 20, band, sums, near))
    stored = VMEM((BAND, ROWS, LANES), F32)
    wide = VMEM((BAND, ROWS + 16, LANES), F32)
    stencil_scratch = [stored] * 5 + [wide, stored]
    stencil_sems = [dma((PARTS, 5)), dma((PARTS,))]
    rim_scratch = [VMEM((8 * BAND, BAND * LANES), BF16), VMEM((ROWS, BAND * LANES), F32)]
    first, later = call(
        early_kernel, far(1) + vm(4) + far(5), far(1) + vm(1), [field, plane],
        spread_scratch + rim_scratch + stencil_scratch + [dma] + stencil_sems
        + [acc] * EARLY_ACCS,
        40 << 20,
        places, slots, land_sea, *sides,
        masked, east_coef, north_coef, coriolis_coef, vertical_coef,
    )
    later_near = step_one(later)
    second, to_west, to_east, onward = call(
        middle_kernel, sm(1) + vm(8) + far(5), far(1) + vm(3), [field, edge, edge, plane],
        [VMEM((ROWS, LANES), F32)] + turned + stencil_scratch + stencil_sems, 24 << 20,
        band, near, rest, columns, far_columns, sums, later, land_sea, rim,
        first, east_coef, north_coef, coriolis_coef, vertical_coef,
    )
    later_rest = step_two(
        call(pass_on, sm(1) + vm(2), vm(1), [plane], [], 1 << 20, band, onward, later_near)
    )
    placed = call(
        rim_kernel, vm(2), vm(1), [shape(ROWS, BAND * LANES)], rim_scratch[:1], 6 << 20,
        *from_sides(to_west, to_east),
    )
    return call(
        last_kernel,
        sm(1) + fields_by_rows(1) + [pl.BlockSpec((LANES, BAND * LANES), lambda i: (i, 0))]
        + planes_by_rows(2),
        fields_by_rows(1), [field], [], 11 << 20,
        band, second, placed, later_near, later_rest, grid=strips,
    )


def solution(mesh):
    return jax.shard_map(
        body,
        mesh=mesh,
        in_specs=(
            P("lev", None, "tile"),
            P("lev", None, "tile"),
            P("lev", None, "tile"),
            P("lev", None, "tile"),
            P("lev", None, "tile"),
            P(None, "tile"),
            P("tile", None, None),
            P("tile", None, None, None),
            P("tile", None, None, None, None),
            P("tile", None, None, None),
            P("tile", None, None, None),
            P("tile", None, None, None),
            P(),
        ),
        out_specs=P("lev", None, "tile"),
        check_vma=False,
    )
```

```python
import jax
import jax.numpy as jnp
from jax import lax
from jax.experimental import pallas as pl
from jax.experimental.pallas import tpu as pltpu
from jax.sharding import PartitionSpec as P

LANES = 128
ROWS = 768
BAND = 8
CAP = 256
OWNERS = 32
BLOCK = 24
CHUNK = 32
LATE_ACCS = 6
EARLY_ACCS = 6
STRIP = 32
UNROLL = 4
PARTS = 6
PART = ROWS // PARTS
PLANES = BAND + 1
LIMIT = 64 << 20
VMEM = pltpu.VMEM
SMEM = pltpu.SMEM
F32 = jnp.float32
BF16 = jnp.bfloat16


def lane_ids():
    return lax.broadcasted_iota(jnp.int32, (STRIP, LANES), 1)


def prepare(band, weight, counts, cell, frac, innovation, kind, level, out):
    z = band[0]
    ids = lax.broadcasted_iota(jnp.int32, (OWNERS, LANES), 1)
    for s in range(2):
        own = lax.broadcasted_iota(jnp.int32, (OWNERS, OWNERS), 0)
        other = lax.broadcasted_iota(jnp.int32, (OWNERS, OWNERS), 1)
        row = jnp.broadcast_to(counts[0, s : s + 1, :].astype(F32), (OWNERS, OWNERS))
        count = jnp.sum(jnp.where(own == other, row, 0.0), 1, keepdims=True)
        out[pl.ds(20 + s, OWNERS, stride=BLOCK), :] = jnp.broadcast_to(count, (OWNERS, LANES))
        for h in range(2):
            part = slice(h * LANES, (h + 1) * LANES)
            t = kind[0, s, :, part]
            at = cell[0, s, :, part]
            scale = jnp.where(t == 0, weight[0], jnp.where(t == 1, weight[1], weight[2]))
            live = (ids + h * LANES).astype(F32) < count
            residual = jnp.where(live, scale * innovation[0, s, :, part], 0.0)
            local = level[0, s, :, part] - z * BAND
            here = (t == 1) & (local >= 0) & (local < BAND)
            keep = (t == 0) | here | ((t == 2) & (z == 0))
            residual = jnp.where(keep, residual, 0.0)
            residual = jnp.where(t == 0, 0.25 * residual, residual)
            target = jnp.where(t == 0, BAND, jnp.where(here, local, 0))
            east = frac[0, s, :, 0, part]
            north = frac[0, s, :, 1, part]
            index = target * ROWS + lax.shift_right_logical(at, 7)
            column = lax.bitwise_and(at, LANES - 1)
            first = s * 8 + h * 4
            values = (column.astype(F32), east, residual * (1.0 - north), residual * north)
            for j, value in enumerate(values):
                out[pl.ds(first + j, OWNERS, stride=BLOCK), :] = value
            out[pl.ds(16 + s * 2 + h, OWNERS, stride=BLOCK), :] = index.astype(F32)
        out[pl.ds(22 + s, OWNERS, stride=BLOCK), :] = jnp.zeros((OWNERS, LANES), F32)


def make_pairs(select, pairs, block, half, at):
    parts = jnp.concatenate(three_parts(block) + [jnp.zeros_like(block)], 0)
    spread = lax.dot_general(
        parts.astype(BF16), select[half], (((0,), (0,)), ((), ())), preferred_element_type=F32
    )
    column, east, south, north = (
        spread[:, j * LANES : (j + 1) * LANES] for j in range(4)
    )
    lanes = lax.broadcasted_iota(jnp.int32, (LANES, LANES), 1).astype(F32)
    weight = jnp.maximum(0.0, 1.0 - jnp.abs((lanes - column) - east))
    pairs[pl.ds(at, LANES, stride=2), :] = weight * south
    pairs[pl.ds(at + 1, LANES, stride=2), :] = weight * north


def spread(s, far_places, slots, select, pairs, places, sem, accs, first_cleared, ready):
    fetch = pltpu.make_async_copy(far_places, places, sem)
    fetch.start()
    row = lax.broadcasted_iota(jnp.int32, (32, 4 * LANES), 0)
    group = lax.shift_right_logical(lax.broadcasted_iota(jnp.int32, (32, 4 * LANES), 1), 7)
    for h in range(2):
        hit = (lax.bitwise_and(row, 7) == group + 4 * h) & (row < 24)
        select[h] = jnp.where(hit, 1.0, 0.0).astype(BF16)
    share = PLANES * ROWS // OWNERS

    def west(o, _):
        for acc in accs[first_cleared:]:
            acc[pl.ds(pl.multiple_of(o * share, 8), share), :] = jnp.zeros((share, LANES), F32)
        block = slots[pl.ds(pl.multiple_of(o * BLOCK + s * 8, 8), 8), :]
        make_pairs(select, pairs, block, 0, o * 2 * CAP)
        return 0

    lax.fori_loop(0, OWNERS, west, 0, unroll=4)
    fetch.wait()

    def most(o, value):
        return jnp.maximum(value, places[o * 8 * LANES + (4 + s) * LANES])

    @pl.when(lax.fori_loop(0, OWNERS, most, jnp.int32(0), unroll=8) > LANES)
    def _():
        def east(o, _):
            block = slots[pl.ds(pl.multiple_of(o * BLOCK + s * 8, 8), 8), :]
            make_pairs(select, pairs, block, 1, o * 2 * CAP + 2 * LANES)
            return 0

        lax.fori_loop(0, OWNERS, east, 0, unroll=4)

    for copy in ready:
        copy.wait()

    def owner(o, _):
        count = places[o * 8 * LANES + (4 + s) * LANES]

        def step(c, _):
            at = o * 8 * LANES + s * CAP + c * CHUNK
            pair = o * 2 * CAP + c * 2 * CHUNK
            for j in range(CHUNK):
                acc = accs[j % len(accs)]
                r = places[at + j]
                acc[pl.ds(r, 2), :] = acc[pl.ds(r, 2), :] + pairs[pl.ds(pair + 2 * j, 2), :]
            return 0

        return lax.fori_loop(0, lax.div(count + (CHUNK - 1), CHUNK), step, 0)

    lax.fori_loop(0, OWNERS, owner, 0)


def total_of(accs, plane, at):
    value = accs[0][pl.ds(plane * ROWS + at, STRIP), :]
    for acc in accs[1:]:
        value = value + acc[pl.ds(plane * ROWS + at, STRIP), :]
    return value


def edge_columns(into, lanes, k, value):
    rolled = pltpu.roll(value, 2 * k + 1, 1)
    return jnp.where((lanes == 2 * k) | (lanes == 2 * k + 1), rolled, into)


def send_edges(edges, at, turned, to_west, to_east, part):
    turned[...] = edges[pl.ds(at, LANES), :].T[0:16, :]
    to_west[:, part] = turned[pl.ds(1, BAND, stride=2), :]
    to_east[:, part] = turned[pl.ds(0, BAND, stride=2), :]


def sum_columns(unused, vertical, land, columns, sent):
    for r in range(0, LANES, STRIP):
        rows = slice(r, r + STRIP)
        total = vertical[0, rows, :]
        for k in range(1, BAND):
            total = total + vertical[k, rows, :]
        total = total * land[rows, :].astype(F32)
        columns[rows, :] = total
        sent[rows, :] = total


def rims(east, coriolis, out):
    lanes = lane_ids()
    for r in range(0, LANES, STRIP):
        rows = slice(r, r + STRIP)
        value = jnp.zeros((STRIP, LANES), F32)
        for k in range(BAND):
            e = east[k, rows, :]
            c = coriolis[k, rows, :]
            value = edge_columns(value, lanes, k, jnp.where(lanes == 0, e - c, e + c))
        out[rows, :] = value


def row_part(ref, c):
    return ref.at[:, pl.ds(c * PART, PART), :]


def late_kernel(
    unused, far_places, slots, final, land, vertical, rim, masked, sums, to_west, to_east,
    select, pairs, places, edges, turned, v_s, o_s, sem, in_sem, out_sem, *accs,
):
    copies = [
        pltpu.make_async_copy(final.at[k], accs[0].at[pl.ds(k * ROWS, ROWS)], in_sem.at[k])
        for k in range(BAND)
    ]
    copies.append(pltpu.make_async_copy(vertical, v_s, in_sem.at[BAND]))
    for copy in copies:
        copy.start()
    accs[0][pl.ds(BAND * ROWS, ROWS), :] = jnp.zeros((ROWS, LANES), F32)
    spread(1, far_places, slots, select, pairs, places, sem, accs, 1, copies[:BAND])
    copies[BAND].wait()
    lanes = lane_ids()

    def one(i, _):
        at = pl.multiple_of(i * STRIP, STRIP)
        rows = pl.ds(at, STRIP)
        sea = land[rows, :].astype(F32)
        shared = total_of(accs, BAND, at)
        total = jnp.zeros((STRIP, LANES), F32)
        edge = jnp.zeros((STRIP, LANES), F32)
        for k in range(BAND):
            m = sea * (total_of(accs, k, at) + shared)
            o_s[k, rows, :] = m
            total = total + v_s[k, rows, :] * m
            edge = edge_columns(edge, lanes, k, m)
        sums[rows, :] = total
        edges[rows, :] = edge * rim[rows, :]
        return 0

    leaving = []
    for c in range(PARTS):
        lax.fori_loop(c * PART // STRIP, (c + 1) * PART // STRIP, one, 0, unroll=UNROLL)
        copy = pltpu.make_async_copy(row_part(o_s, c), row_part(masked, c), out_sem.at[c])
        copy.start()
        leaving.append(copy)
    for b in range(ROWS // LANES):
        part = slice(b * LANES, (b + 1) * LANES)
        send_edges(edges, b * LANES, turned, to_west, to_east, part)
    for copy in leaving:
        copy.wait()


def fetch_fields(sources, targets, sem):
    copies = []
    for c in range(PARTS):
        row = []
        for j, (source, target) in enumerate(zip(sources, targets)):
            copy = pltpu.make_async_copy(row_part(source, c), row_part(target, c), sem.at[c, j])
            copy.start()
            row.append(copy)
        copies.append(row)
    return copies


def rim_select(select):
    row = lax.broadcasted_iota(jnp.int32, (8 * BAND, BAND * LANES), 0)
    column = lax.broadcasted_iota(jnp.int32, (8 * BAND, BAND * LANES), 1)
    level = lax.shift_right_logical(column, 7)
    lane = lax.bitwise_and(column, LANES - 1)
    side = jnp.where(row < 3 * BAND, LANES - 1, 0)
    hit = (lax.bitwise_and(row, BAND - 1) == level) & (lane == side) & (row < 6 * BAND)
    select[...] = jnp.where(hit, 1.0, 0.0).astype(BF16)


def three_parts(value):
    high = value.astype(BF16).astype(F32)
    rest = value - high
    middle = rest.astype(BF16).astype(F32)
    return [high, middle, rest - middle]


def place_rims(from_east, from_west, select, placed):
    for b in range(placed.shape[0] // LANES):
        part = slice(b * LANES, (b + 1) * LANES)
        east, west = from_east[:, part], from_west[:, part]
        empty = jnp.zeros((2 * BAND, LANES), F32)
        parts = jnp.concatenate(three_parts(east) + three_parts(west) + [empty], 0)
        placed[part, :] = lax.dot_general(
            parts.astype(BF16), select[...], (((0,), (0,)), ((), ())), preferred_element_type=F32
        )


def stencil(copies, masked, east, north, coriolis, vertical, flow, made, prepare_rows, start, added,
            finish, out, out_sem):
    for k in range(BAND):
        flow[k, 0:8, :] = jnp.zeros((8, LANES), F32)
        flow[k, ROWS + 8 : ROWS + 16, :] = jnp.zeros((8, LANES), F32)

    def first(i, _):
        at = pl.multiple_of(i * STRIP, STRIP)
        prepare_rows(at)
        rows = pl.ds(at, STRIP)
        for k in range(BAND):
            value = north[k, rows, :] * masked[k, rows, :]
            flow[k, pl.ds(pl.multiple_of(at + 8, 8), STRIP), :] = value
        return 0

    lanes = lane_ids()

    def second(i, _):
        at = pl.multiple_of(i * STRIP, STRIP)
        rows = pl.ds(at, STRIP)
        below = start(at)
        total = jnp.zeros((STRIP, LANES), F32)
        for k in reversed(range(BAND)):
            m = masked[k, rows, :]
            e = east[k, rows, :] * m
            c = coriolis[k, rows, :] * m
            v = vertical[k, rows, :]
            below = below + v * m
            ahead = jnp.where(lanes == LANES - 1, 0.0, pltpu.roll(e - c, LANES - 1, 1))
            behind = jnp.where(lanes == 0, 0.0, pltpu.roll(e + c, 1, 1))
            across = (
                flow[k, pl.ds(at + 7, STRIP), :]
                + flow[k, pl.ds(at + 9, STRIP), :]
                - 2.0 * flow[k, pl.ds(pl.multiple_of(at + 8, 8), STRIP), :]
            )
            value = m + (ahead + behind - 2.0 * e) + across + below + added(k, at)
            made[k, rows, :] = value
            total = total + v * value
        finish(at, total)
        return 0

    leaving = []
    for c in range(PARTS + 1):
        if c < PARTS:
            for copy in copies[c]:
                copy.wait()
            lax.fori_loop(c * PART // STRIP, (c + 1) * PART // STRIP, first, 0, unroll=UNROLL)
        if c > 0:
            lax.fori_loop((c - 1) * PART // STRIP, c * PART // STRIP, second, 0, unroll=UNROLL)
            copy = pltpu.make_async_copy(
                row_part(made, c - 1), row_part(out, c - 1), out_sem.at[c - 1]
            )
            copy.start()
            leaving.append(copy)
    return leaving


def early_kernel(
    far_places, slots, land, from_east, from_west, masked, east, north, coriolis, vertical,
    out, sums,
    select, pairs, places, rim_picks, placed, m_s, e_s, n_s, c_s, v_s, flow, made,
    sem, in_sem, out_sem, *accs,
):
    copies = fetch_fields(
        (masked, east, north, coriolis, vertical), (m_s, e_s, n_s, c_s, v_s), in_sem
    )
    rim_select(rim_picks)
    place_rims(from_east, from_west, rim_picks, placed)
    spread(0, far_places, slots, select, pairs, places, sem, accs, 0, ())

    def start(at):
        return total_of(accs, BAND, at)

    def added(k, at):
        rows = pl.ds(at, STRIP)
        return total_of(accs, k, at) + placed[rows, k * LANES : (k + 1) * LANES]

    def finish(at, total):
        rows = pl.ds(at, STRIP)
        sums[rows, :] = total * land[rows, :].astype(F32)

    leaving = stencil(
        copies, m_s, e_s, n_s, c_s, v_s, flow, made, lambda at: None, start, added, finish, out, out_sem
    )
    for copy in leaving:
        copy.wait()


def middle_kernel(
    band, one_up, two_up, three_up, columns, far_columns, own, later, land, rim,
    field, east, north, coriolis, vertical, out, to_west, to_east, onward,
    edges, turned, m_s, e_s, n_s, c_s, v_s, flow, made, in_sem, out_sem,
):
    z = band[0]
    sends = jnp.where(z == 0, 0.0, 1.0)

    copies = fetch_fields(
        (field, east, north, coriolis, vertical), (m_s, e_s, n_s, c_s, v_s), in_sem
    )
    lanes = lane_ids()

    def prepare_rows(at):
        rows = pl.ds(at, STRIP)
        sea = land[rows, :].astype(F32)
        higher = one_up[rows, :] + two_up[rows, :] + three_up[rows, :]
        edge = jnp.zeros((STRIP, LANES), F32)
        for k in range(BAND):
            m = sea * (m_s[k, rows, :] + higher)
            m_s[k, rows, :] = m
            edge = edge_columns(edge, lanes, k, m)
        edges[rows, :] = edge * rim[rows, :]

    def start(at):
        rows = pl.ds(at, STRIP)
        two, three = two_up[rows, :], three_up[rows, :]
        higher = one_up[rows, :] + two + three
        other = far_columns[rows, :]
        onward[rows, :] = sends * (
            later[rows, :]
            + columns[rows, :] * higher
            + other * jnp.where(z == 3, own[rows, :], two)
        )
        return other * (two + three)

    leaving = stencil(
        copies, m_s, e_s, n_s, c_s, v_s, flow, made, prepare_rows, start, lambda k, at: 0.0,
        lambda at, total: None, out, out_sem,
    )
    for b in range(ROWS // LANES):
        part = slice(b * LANES, (b + 1) * LANES)
        send_edges(edges, b * LANES, turned, to_west, to_east, part)
    for copy in leaving:
        copy.wait()


def last_kernel(band, field, near, rest, from_east, from_west, out, select, placed):
    @pl.when(pl.program_id(0) == 0)
    def _():
        rim_select(select)

    place_rims(from_east, from_west, select, placed)
    inner = jnp.where(band[0] == 3, 0.0, 1.0)
    for r in range(0, LANES, STRIP):
        rows = slice(r, r + STRIP)
        higher = inner * near[rows, :] + rest[rows, :]
        for k in range(BAND):
            rim = placed[rows, k * LANES : (k + 1) * LANES]
            out[k, rows, :] = field[k, rows, :] + higher + rim


def shape(*dims):
    return jax.ShapeDtypeStruct(dims, F32)


def vm(count):
    return [pl.BlockSpec(memory_space=VMEM)] * count


def sm(count):
    return [pl.BlockSpec(memory_space=SMEM)] * count


def far(count):
    return [pl.BlockSpec(memory_space=pl.ANY)] * count


def fields_by_rows(count):
    return [pl.BlockSpec((BAND, LANES, LANES), lambda i: (0, i, 0))] * count


def planes_by_rows(count):
    return [pl.BlockSpec((LANES, LANES), lambda i: (i, 0))] * count


def call(kernel, ins, outs, shapes, scratch, moved, *args, grid=()):
    many = len(outs) > 1
    return pl.pallas_call(
        kernel,
        grid=grid,
        in_specs=ins,
        out_specs=tuple(outs) if many else outs[0],
        out_shape=tuple(shapes) if many else shapes[0],
        scratch_shapes=scratch,
        compiler_params=pltpu.CompilerParams(vmem_limit_bytes=LIMIT),
        cost_estimate=pl.CostEstimate(flops=moved, bytes_accessed=moved, transcendentals=0),
    )(*args)


def by_core(part, first_core, second_core):
    bands = lax.axis_size("lev")
    pairs = [
        (tile * bands + source, tile * bands + target)
        for tile in range(lax.axis_size("tile"))
        for source, target in (second_core if tile % 2 else first_core)
    ]
    return lax.ppermute(part, ("tile", "lev"), pairs)


def from_deeper(part):
    return (
        lax.ppermute(part, "lev", [(3, 2), (2, 1), (1, 0)]),
        lax.ppermute(part, "lev", [(3, 1), (2, 0)]),
        lax.ppermute(part, "lev", [(3, 0)]),
    )


def step_one(part):
    return by_core(part, ((3, 2), (2, 3), (1, 0)), ((2, 1), (3, 0)))


def step_two(part):
    return by_core(part, ((2, 1), (3, 0)), ((0, 1), (1, 0), (3, 2)))


def from_sides(to_west, to_east):
    count = lax.axis_size("tile")
    return (
        lax.ppermute(to_west, "tile", [((i + 1) % count, i) for i in range(count)]),
        lax.ppermute(to_east, "tile", [(i, (i + 1) % count) for i in range(count)]),
    )


def body(
    final_adjoint,
    east_coef,
    north_coef,
    coriolis_coef,
    vertical_coef,
    land_sea,
    counts,
    obs_cell,
    obs_frac,
    innovation,
    obs_type,
    obs_level,
    type_weight,
):
    band = lax.axis_index("lev").astype(jnp.int32).reshape(1)
    field = shape(BAND, ROWS, LANES)
    plane = shape(ROWS, LANES)
    edge = shape(BAND, ROWS)
    strips = (ROWS // LANES,)
    dma = pltpu.SemaphoreType.DMA
    send = call(
        prepare, sm(2) + vm(6), vm(1), [shape(OWNERS * BLOCK, LANES)], [], 1 << 20,
        band, type_weight, counts, obs_cell, obs_frac, innovation, obs_type, obs_level,
    )
    arrived = lax.all_to_all(
        send.reshape(OWNERS, BLOCK, LANES), "tile", split_axis=0, concat_axis=0, tiled=True
    )
    columns, sent = call(
        sum_columns, far(1) + fields_by_rows(1) + planes_by_rows(1), planes_by_rows(2),
        [plane] * 2, [], 4 << 20, send, vertical_coef, land_sea, grid=strips,
    )
    far_columns = by_core(sent, ((1, 0), (2, 3)), ((2, 1),))
    rim = call(
        rims, fields_by_rows(2), planes_by_rows(1), [plane], [], 7 << 20,
        east_coef, coriolis_coef, grid=strips,
    )
    places = arrived[:, 16:24, :].astype(jnp.int32).reshape(-1)
    slots = arrived.reshape(OWNERS * BLOCK, LANES)
    acc = VMEM((PLANES * ROWS + 8, LANES), F32)
    spread_scratch = [
        VMEM((2, 32, 4 * LANES), BF16),
        VMEM((OWNERS * CAP * 2, LANES), F32),
        SMEM((OWNERS * 8 * LANES,), jnp.int32),
    ]
    turned = [VMEM((2 * BAND, LANES), F32)]
    masked, sums, to_west, to_east = call(
        late_kernel, far(2) + vm(1) + far(1) + vm(1) + far(1) + vm(1), far(1) + vm(3),
        [field, plane, edge, edge],
        spread_scratch + [VMEM((ROWS, LANES), F32)] + turned + [VMEM((BAND, ROWS, LANES), F32)] * 2
        + [dma, dma((BAND + 1,)), dma((PARTS,))] + [acc] * LATE_ACCS,
        10 << 20,
        far_columns, places, slots, final_adjoint, land_sea, vertical_coef, rim,
    )
    sides = from_sides(to_west, to_east)
    ups = from_deeper(sums)
    stored = VMEM((BAND, ROWS, LANES), F32)
    wide = VMEM((BAND, ROWS + 16, LANES), F32)
    stencil_scratch = [stored] * 5 + [wide, stored]
    stencil_sems = [dma((PARTS, 5)), dma((PARTS,))]
    rim_scratch = [VMEM((8 * BAND, BAND * LANES), BF16), VMEM((ROWS, BAND * LANES), F32)]
    first, later = call(
        early_kernel, far(1) + vm(4) + far(5), far(1) + vm(1), [field, plane],
        spread_scratch + rim_scratch + stencil_scratch + [dma] + stencil_sems
        + [acc] * EARLY_ACCS,
        40 << 20,
        places, slots, land_sea, *sides,
        masked, east_coef, north_coef, coriolis_coef, vertical_coef,
    )
    later_near = step_one(later)
    second, to_west, to_east, onward = call(
        middle_kernel, sm(1) + vm(9) + far(5), far(1) + vm(3), [field, edge, edge, plane],
        [VMEM((ROWS, LANES), F32)] + turned + stencil_scratch + stencil_sems, 24 << 20,
        band, *ups, columns, far_columns, sums, later, land_sea, rim,
        first, east_coef, north_coef, coriolis_coef, vertical_coef,
    )
    later_rest = step_two(onward + later_near)
    sides = from_sides(to_west, to_east)
    edge_blocks = [pl.BlockSpec((BAND, LANES), lambda i: (0, i))] * 2
    return call(
        last_kernel, sm(1) + fields_by_rows(1) + planes_by_rows(2) + edge_blocks,
        fields_by_rows(1), [field],
        [rim_scratch[0], VMEM((LANES, BAND * LANES), F32)], 8 << 20,
        band, second, later_near, later_rest, *sides, grid=strips,
    )


def solution(mesh):
    return jax.shard_map(
        body,
        mesh=mesh,
        in_specs=(
            P("lev", None, "tile"),
            P("lev", None, "tile"),
            P("lev", None, "tile"),
            P("lev", None, "tile"),
            P("lev", None, "tile"),
            P(None, "tile"),
            P("tile", None, None),
            P("tile", None, None, None),
            P("tile", None, None, None, None),
            P("tile", None, None, None),
            P("tile", None, None, None),
            P("tile", None, None, None),
            P(),
        ),
        out_specs=P("lev", None, "tile"),
        check_vma=False,
    )
```

```python
import jax
import jax.numpy as jnp
from jax import lax
from jax.experimental import pallas as pl
from jax.experimental.pallas import tpu as pltpu
from jax.sharding import PartitionSpec as P

LANES = 128
ROWS = 768
BAND = 8
CAP = 256
OWNERS = 32
BLOCK = 24
CHUNK = 32
LATE_ACCS = 6
EARLY_ACCS = 6
STRIP = 32
UNROLL = 4
PARTS = 6
PART = ROWS // PARTS
PLANES = BAND + 1
LIMIT = 64 << 20
VMEM = pltpu.VMEM
SMEM = pltpu.SMEM
F32 = jnp.float32
BF16 = jnp.bfloat16


def lane_ids():
    return lax.broadcasted_iota(jnp.int32, (STRIP, LANES), 1)


def prepare(band, weight, counts, cell, frac, innovation, kind, level, out):
    z = band[0]
    ids = lax.broadcasted_iota(jnp.int32, (OWNERS, LANES), 1)
    for s in range(2):
        own = lax.broadcasted_iota(jnp.int32, (OWNERS, OWNERS), 0)
        other = lax.broadcasted_iota(jnp.int32, (OWNERS, OWNERS), 1)
        row = jnp.broadcast_to(counts[0, s : s + 1, :].astype(F32), (OWNERS, OWNERS))
        count = jnp.sum(jnp.where(own == other, row, 0.0), 1, keepdims=True)
        out[pl.ds(20 + s, OWNERS, stride=BLOCK), :] = jnp.broadcast_to(count, (OWNERS, LANES))
        for h in range(2):
            part = slice(h * LANES, (h + 1) * LANES)
            t = kind[0, s, :, part]
            at = cell[0, s, :, part]
            scale = jnp.where(t == 0, weight[0], jnp.where(t == 1, weight[1], weight[2]))
            live = (ids + h * LANES).astype(F32) < count
            residual = jnp.where(live, scale * innovation[0, s, :, part], 0.0)
            local = level[0, s, :, part] - z * BAND
            here = (t == 1) & (local >= 0) & (local < BAND)
            keep = (t == 0) | here | ((t == 2) & (z == 0))
            residual = jnp.where(keep, residual, 0.0)
            residual = jnp.where(t == 0, 0.25 * residual, residual)
            target = jnp.where(t == 0, BAND, jnp.where(here, local, 0))
            east = frac[0, s, :, 0, part]
            north = frac[0, s, :, 1, part]
            index = target * ROWS + lax.shift_right_logical(at, 7)
            column = lax.bitwise_and(at, LANES - 1)
            first = s * 8 + h * 4
            values = (column.astype(F32), east, residual * (1.0 - north), residual * north)
            for j, value in enumerate(values):
                out[pl.ds(first + j, OWNERS, stride=BLOCK), :] = value
            out[pl.ds(16 + s * 2 + h, OWNERS, stride=BLOCK), :] = index.astype(F32)
        out[pl.ds(22 + s, OWNERS, stride=BLOCK), :] = jnp.zeros((OWNERS, LANES), F32)


def make_pairs(select, pairs, block, half, at):
    parts = jnp.concatenate(three_parts(block) + [jnp.zeros_like(block)], 0)
    spread = lax.dot_general(
        parts.astype(BF16), select[half], (((0,), (0,)), ((), ())), preferred_element_type=F32
    )
    column, east, south, north = (
        spread[:, j * LANES : (j + 1) * LANES] for j in range(4)
    )
    lanes = lax.broadcasted_iota(jnp.int32, (LANES, LANES), 1).astype(F32)
    weight = jnp.maximum(0.0, 1.0 - jnp.abs((lanes - column) - east))
    pairs[pl.ds(at, LANES, stride=2), :] = weight * south
    pairs[pl.ds(at + 1, LANES, stride=2), :] = weight * north


def spread(s, far_places, slots, select, pairs, places, sem, accs, first_cleared, ready):
    fetch = pltpu.make_async_copy(far_places, places, sem)
    fetch.start()
    row = lax.broadcasted_iota(jnp.int32, (32, 4 * LANES), 0)
    group = lax.shift_right_logical(lax.broadcasted_iota(jnp.int32, (32, 4 * LANES), 1), 7)
    for h in range(2):
        hit = (lax.bitwise_and(row, 7) == group + 4 * h) & (row < 24)
        select[h] = jnp.where(hit, 1.0, 0.0).astype(BF16)
    share = PLANES * ROWS // OWNERS

    def west(o, _):
        for acc in accs[first_cleared:]:
            acc[pl.ds(pl.multiple_of(o * share, 8), share), :] = jnp.zeros((share, LANES), F32)
        block = slots[pl.ds(pl.multiple_of(o * BLOCK + s * 8, 8), 8), :]
        make_pairs(select, pairs, block, 0, o * 2 * CAP)
        return 0

    lax.fori_loop(0, OWNERS, west, 0, unroll=4)
    fetch.wait()

    def most(o, value):
        return jnp.maximum(value, places[o * 8 * LANES + (4 + s) * LANES])

    @pl.when(lax.fori_loop(0, OWNERS, most, jnp.int32(0), unroll=8) > LANES)
    def _():
        def east(o, _):
            block = slots[pl.ds(pl.multiple_of(o * BLOCK + s * 8, 8), 8), :]
            make_pairs(select, pairs, block, 1, o * 2 * CAP + 2 * LANES)
            return 0

        lax.fori_loop(0, OWNERS, east, 0, unroll=4)

    for copy in ready:
        copy.wait()

    def owner(o, _):
        count = places[o * 8 * LANES + (4 + s) * LANES]

        def step(c, _):
            at = o * 8 * LANES + s * CAP + c * CHUNK
            pair = o * 2 * CAP + c * 2 * CHUNK
            for j in range(CHUNK):
                acc = accs[j % len(accs)]
                r = places[at + j]
                acc[pl.ds(r, 2), :] = acc[pl.ds(r, 2), :] + pairs[pl.ds(pair + 2 * j, 2), :]
            return 0

        return lax.fori_loop(0, lax.div(count + (CHUNK - 1), CHUNK), step, 0)

    lax.fori_loop(0, OWNERS, owner, 0)


def total_of(accs, plane, at):
    value = accs[0][pl.ds(plane * ROWS + at, STRIP), :]
    for acc in accs[1:]:
        value = value + acc[pl.ds(plane * ROWS + at, STRIP), :]
    return value


def edge_columns(into, lanes, k, value):
    rolled = pltpu.roll(value, 2 * k + 1, 1)
    return jnp.where((lanes == 2 * k) | (lanes == 2 * k + 1), rolled, into)


def send_edges(edges, at, turned, to_west, to_east, part):
    turned[...] = edges[pl.ds(at, LANES), :].T[0:16, :]
    to_west[:, part] = turned[pl.ds(1, BAND, stride=2), :]
    to_east[:, part] = turned[pl.ds(0, BAND, stride=2), :]


def rims(east, coriolis, vertical, land, out, columns):
    lanes = lane_ids()
    for r in range(0, LANES, STRIP):
        rows = slice(r, r + STRIP)
        value = jnp.zeros((STRIP, LANES), F32)
        total = jnp.zeros((STRIP, LANES), F32)
        for k in range(BAND):
            e = east[k, rows, :]
            c = coriolis[k, rows, :]
            value = edge_columns(value, lanes, k, jnp.where(lanes == 0, e - c, e + c))
            total = total + vertical[k, rows, :]
        out[rows, :] = value
        columns[rows, :] = total * land[rows, :].astype(F32)


def row_part(ref, c):
    return ref.at[:, pl.ds(c * PART, PART), :]


def late_kernel(
    far_places, slots, final, land, vertical, rim, masked, sums, to_west, to_east,
    select, pairs, places, edges, turned, v_s, o_s, sem, in_sem, out_sem, *accs,
):
    copies = [
        pltpu.make_async_copy(final.at[k], accs[0].at[pl.ds(k * ROWS, ROWS)], in_sem.at[k])
        for k in range(BAND)
    ]
    copies.append(pltpu.make_async_copy(vertical, v_s, in_sem.at[BAND]))
    for copy in copies:
        copy.start()
    accs[0][pl.ds(BAND * ROWS, ROWS), :] = jnp.zeros((ROWS, LANES), F32)
    spread(1, far_places, slots, select, pairs, places, sem, accs, 1, copies[:BAND])
    copies[BAND].wait()
    lanes = lane_ids()

    def one(i, _):
        at = pl.multiple_of(i * STRIP, STRIP)
        rows = pl.ds(at, STRIP)
        sea = land[rows, :].astype(F32)
        shared = total_of(accs, BAND, at)
        total = jnp.zeros((STRIP, LANES), F32)
        edge = jnp.zeros((STRIP, LANES), F32)
        for k in range(BAND):
            m = sea * (total_of(accs, k, at) + shared)
            o_s[k, rows, :] = m
            total = total + v_s[k, rows, :] * m
            edge = edge_columns(edge, lanes, k, m)
        sums[rows, :] = total
        edges[rows, :] = edge * rim[rows, :]
        return 0

    leaving = []
    for c in range(PARTS):
        lax.fori_loop(c * PART // STRIP, (c + 1) * PART // STRIP, one, 0, unroll=UNROLL)
        copy = pltpu.make_async_copy(row_part(o_s, c), row_part(masked, c), out_sem.at[c])
        copy.start()
        leaving.append(copy)
    for b in range(ROWS // LANES):
        part = slice(b * LANES, (b + 1) * LANES)
        send_edges(edges, b * LANES, turned, to_west, to_east, part)
    for copy in leaving:
        copy.wait()


def fetch_fields(sources, targets, sem):
    copies = []
    for c in range(PARTS):
        row = []
        for j, (source, target) in enumerate(zip(sources, targets)):
            copy = pltpu.make_async_copy(row_part(source, c), row_part(target, c), sem.at[c, j])
            copy.start()
            row.append(copy)
        copies.append(row)
    return copies


def rim_select(select):
    row = lax.broadcasted_iota(jnp.int32, (8 * BAND, BAND * LANES), 0)
    column = lax.broadcasted_iota(jnp.int32, (8 * BAND, BAND * LANES), 1)
    level = lax.shift_right_logical(column, 7)
    lane = lax.bitwise_and(column, LANES - 1)
    side = jnp.where(row < 3 * BAND, LANES - 1, 0)
    hit = (lax.bitwise_and(row, BAND - 1) == level) & (lane == side) & (row < 6 * BAND)
    select[...] = jnp.where(hit, 1.0, 0.0).astype(BF16)


def three_parts(value):
    high = value.astype(BF16).astype(F32)
    rest = value - high
    middle = rest.astype(BF16).astype(F32)
    return [high, middle, rest - middle]


def place_rims(from_east, from_west, select, placed):
    for b in range(placed.shape[0] // LANES):
        part = slice(b * LANES, (b + 1) * LANES)
        east, west = from_east[:, part], from_west[:, part]
        empty = jnp.zeros((2 * BAND, LANES), F32)
        parts = jnp.concatenate(three_parts(east) + three_parts(west) + [empty], 0)
        placed[part, :] = lax.dot_general(
            parts.astype(BF16), select[...], (((0,), (0,)), ((), ())), preferred_element_type=F32
        )


def stencil(copies, masked, east, north, coriolis, vertical, flow, made, prepare_rows, start, added,
            finish, out, out_sem):
    for k in range(BAND):
        flow[k, 0:8, :] = jnp.zeros((8, LANES), F32)
        flow[k, ROWS + 8 : ROWS + 16, :] = jnp.zeros((8, LANES), F32)

    def first(i, _):
        at = pl.multiple_of(i * STRIP, STRIP)
        prepare_rows(at)
        rows = pl.ds(at, STRIP)
        for k in range(BAND):
            value = north[k, rows, :] * masked[k, rows, :]
            flow[k, pl.ds(pl.multiple_of(at + 8, 8), STRIP), :] = value
        return 0

    lanes = lane_ids()

    def second(i, _):
        at = pl.multiple_of(i * STRIP, STRIP)
        rows = pl.ds(at, STRIP)
        below = start(at)
        total = jnp.zeros((STRIP, LANES), F32)
        for k in reversed(range(BAND)):
            m = masked[k, rows, :]
            e = east[k, rows, :] * m
            c = coriolis[k, rows, :] * m
            v = vertical[k, rows, :]
            below = below + v * m
            ahead = jnp.where(lanes == LANES - 1, 0.0, pltpu.roll(e - c, LANES - 1, 1))
            behind = jnp.where(lanes == 0, 0.0, pltpu.roll(e + c, 1, 1))
            across = (
                flow[k, pl.ds(at + 7, STRIP), :]
                + flow[k, pl.ds(at + 9, STRIP), :]
                - 2.0 * flow[k, pl.ds(pl.multiple_of(at + 8, 8), STRIP), :]
            )
            value = m + (ahead + behind - 2.0 * e) + across + below + added(k, at)
            made[k, rows, :] = value
            total = total + v * value
        finish(at, total)
        return 0

    leaving = []
    for c in range(PARTS + 1):
        if c < PARTS:
            for copy in copies[c]:
                copy.wait()
            lax.fori_loop(c * PART // STRIP, (c + 1) * PART // STRIP, first, 0, unroll=UNROLL)
        if c > 0:
            lax.fori_loop((c - 1) * PART // STRIP, c * PART // STRIP, second, 0, unroll=UNROLL)
            copy = pltpu.make_async_copy(
                row_part(made, c - 1), row_part(out, c - 1), out_sem.at[c - 1]
            )
            copy.start()
            leaving.append(copy)
    return leaving


def early_kernel(
    far_places, slots, land, from_east, from_west, masked, east, north, coriolis, vertical,
    out, sums,
    select, pairs, places, rim_picks, placed, m_s, e_s, n_s, c_s, v_s, flow, made,
    sem, in_sem, out_sem, *accs,
):
    copies = fetch_fields(
        (masked, east, north, coriolis, vertical), (m_s, e_s, n_s, c_s, v_s), in_sem
    )
    rim_select(rim_picks)
    place_rims(from_east, from_west, rim_picks, placed)
    spread(0, far_places, slots, select, pairs, places, sem, accs, 0, ())

    def start(at):
        return total_of(accs, BAND, at)

    def added(k, at):
        rows = pl.ds(at, STRIP)
        return total_of(accs, k, at) + placed[rows, k * LANES : (k + 1) * LANES]

    def finish(at, total):
        rows = pl.ds(at, STRIP)
        sums[rows, :] = total * land[rows, :].astype(F32)

    leaving = stencil(
        copies, m_s, e_s, n_s, c_s, v_s, flow, made, lambda at: None, start, added, finish, out, out_sem
    )
    for copy in leaving:
        copy.wait()


def middle_kernel(
    band, one_up, two_up, three_up, complete, land, rim,
    field, east, north, coriolis, vertical, out, to_west, to_east, onward,
    edges, turned, m_s, e_s, n_s, c_s, v_s, flow, made, in_sem, out_sem,
):
    sends = jnp.where(band[0] == 0, 0.0, 1.0)

    copies = fetch_fields(
        (field, east, north, coriolis, vertical), (m_s, e_s, n_s, c_s, v_s), in_sem
    )
    lanes = lane_ids()

    def prepare_rows(at):
        rows = pl.ds(at, STRIP)
        sea = land[rows, :].astype(F32)
        higher = one_up[rows, :] + two_up[rows, :] + three_up[rows, :]
        edge = jnp.zeros((STRIP, LANES), F32)
        for k in range(BAND):
            m = sea * (m_s[k, rows, :] + higher)
            m_s[k, rows, :] = m
            edge = edge_columns(edge, lanes, k, m)
        edges[rows, :] = edge * rim[rows, :]

    def start(at):
        rows = pl.ds(at, STRIP)
        onward[rows, :] = sends * complete[rows, :]
        return jnp.zeros((STRIP, LANES), F32)

    leaving = stencil(
        copies, m_s, e_s, n_s, c_s, v_s, flow, made, prepare_rows, start, lambda k, at: 0.0,
        lambda at, total: None, out, out_sem,
    )
    for b in range(ROWS // LANES):
        part = slice(b * LANES, (b + 1) * LANES)
        send_edges(edges, b * LANES, turned, to_west, to_east, part)
    for copy in leaving:
        copy.wait()


def last_kernel(
    band, near, rest, from_east, from_west, field, out, select, placed, f_s, o_s, in_sem, out_sem
):
    copies = []
    for c in range(PARTS):
        copy = pltpu.make_async_copy(row_part(field, c), row_part(f_s, c), in_sem.at[c])
        copy.start()
        copies.append(copy)
    rim_select(select)
    place_rims(from_east, from_west, select, placed)
    inner = jnp.where(band[0] == 3, 0.0, 1.0)

    def one(i, _):
        rows = pl.ds(pl.multiple_of(i * STRIP, STRIP), STRIP)
        higher = inner * near[rows, :] + rest[rows, :]
        for k in range(BAND):
            rim = placed[rows, k * LANES : (k + 1) * LANES]
            o_s[k, rows, :] = f_s[k, rows, :] + higher + rim
        return 0

    leaving = []
    for c in range(PARTS):
        copies[c].wait()
        lax.fori_loop(c * PART // STRIP, (c + 1) * PART // STRIP, one, 0, unroll=UNROLL)
        copy = pltpu.make_async_copy(row_part(o_s, c), row_part(out, c), out_sem.at[c])
        copy.start()
        leaving.append(copy)
    for copy in leaving:
        copy.wait()


def shape(*dims):
    return jax.ShapeDtypeStruct(dims, F32)


def vm(count):
    return [pl.BlockSpec(memory_space=VMEM)] * count


def sm(count):
    return [pl.BlockSpec(memory_space=SMEM)] * count


def far(count):
    return [pl.BlockSpec(memory_space=pl.ANY)] * count


def fields_by_rows(count):
    return [pl.BlockSpec((BAND, LANES, LANES), lambda i: (0, i, 0))] * count


def planes_by_rows(count):
    return [pl.BlockSpec((LANES, LANES), lambda i: (i, 0))] * count


def call(kernel, ins, outs, shapes, scratch, moved, *args, grid=()):
    many = len(outs) > 1
    return pl.pallas_call(
        kernel,
        grid=grid,
        in_specs=ins,
        out_specs=tuple(outs) if many else outs[0],
        out_shape=tuple(shapes) if many else shapes[0],
        scratch_shapes=scratch,
        compiler_params=pltpu.CompilerParams(vmem_limit_bytes=LIMIT),
        cost_estimate=pl.CostEstimate(flops=moved, bytes_accessed=moved, transcendentals=0),
    )(*args)


def by_core(part, first_core, second_core):
    bands = lax.axis_size("lev")
    pairs = [
        (tile * bands + source, tile * bands + target)
        for tile in range(lax.axis_size("tile"))
        for source, target in (second_core if tile % 2 else first_core)
    ]
    return lax.ppermute(part, ("tile", "lev"), pairs)


def from_deeper(part):
    return (
        lax.ppermute(part, "lev", [(3, 2), (2, 1), (1, 0)]),
        lax.ppermute(part, "lev", [(3, 1), (2, 0)]),
        lax.ppermute(part, "lev", [(3, 0)]),
    )


def step_one(part):
    return by_core(part, ((3, 2), (2, 3), (1, 0)), ((2, 1), (3, 0)))


def step_two(part):
    return by_core(part, ((2, 1), (3, 0)), ((0, 1), (1, 0), (3, 2)))


def from_sides(to_west, to_east):
    count = lax.axis_size("tile")
    return (
        lax.ppermute(to_west, "tile", [((i + 1) % count, i) for i in range(count)]),
        lax.ppermute(to_east, "tile", [(i, (i + 1) % count) for i in range(count)]),
    )


def body(
    final_adjoint,
    east_coef,
    north_coef,
    coriolis_coef,
    vertical_coef,
    land_sea,
    counts,
    obs_cell,
    obs_frac,
    innovation,
    obs_type,
    obs_level,
    type_weight,
):
    band = lax.axis_index("lev").astype(jnp.int32).reshape(1)
    field = shape(BAND, ROWS, LANES)
    plane = shape(ROWS, LANES)
    edge = shape(BAND, ROWS)
    strips = (ROWS // LANES,)
    dma = pltpu.SemaphoreType.DMA
    send = call(
        prepare, sm(2) + vm(6), vm(1), [shape(OWNERS * BLOCK, LANES)], [], 1 << 20,
        band, type_weight, counts, obs_cell, obs_frac, innovation, obs_type, obs_level,
    )
    arrived = lax.all_to_all(
        send.reshape(OWNERS, BLOCK, LANES), "tile", split_axis=0, concat_axis=0, tiled=True
    )
    rim, columns = call(
        rims, fields_by_rows(3) + planes_by_rows(1), planes_by_rows(2), [plane] * 2, [],
        10 << 20, east_coef, coriolis_coef, vertical_coef, land_sea, grid=strips,
    )
    places = arrived[:, 16:24, :].astype(jnp.int32).reshape(-1)
    slots = arrived.reshape(OWNERS * BLOCK, LANES)
    acc = VMEM((PLANES * ROWS + 8, LANES), F32)
    spread_scratch = [
        VMEM((2, 32, 4 * LANES), BF16),
        VMEM((OWNERS * CAP * 2, LANES), F32),
        SMEM((OWNERS * 8 * LANES,), jnp.int32),
    ]
    turned = [VMEM((2 * BAND, LANES), F32)]
    masked, sums, to_west, to_east = call(
        late_kernel, far(1) + vm(1) + far(1) + vm(1) + far(1) + vm(1), far(1) + vm(3),
        [field, plane, edge, edge],
        spread_scratch + [VMEM((ROWS, LANES), F32)] + turned + [VMEM((BAND, ROWS, LANES), F32)] * 2
        + [dma, dma((BAND + 1,)), dma((PARTS,))] + [acc] * LATE_ACCS,
        10 << 20,
        places, slots, final_adjoint, land_sea, vertical_coef, rim,
    )
    sides = from_sides(to_west, to_east)
    ups = from_deeper(sums)
    stored = VMEM((BAND, ROWS, LANES), F32)
    wide = VMEM((BAND, ROWS + 16, LANES), F32)
    stencil_scratch = [stored] * 5 + [wide, stored]
    stencil_sems = [dma((PARTS, 5)), dma((PARTS,))]
    rim_scratch = [VMEM((8 * BAND, BAND * LANES), BF16), VMEM((ROWS, BAND * LANES), F32)]
    first, later = call(
        early_kernel, far(1) + vm(4) + far(5), far(1) + vm(1), [field, plane],
        spread_scratch + rim_scratch + stencil_scratch + [dma] + stencil_sems
        + [acc] * EARLY_ACCS,
        40 << 20,
        places, slots, land_sea, *sides,
        masked, east_coef, north_coef, coriolis_coef, vertical_coef,
    )
    complete = later + columns * (ups[0] + ups[1] + ups[2])
    later_near = step_one(complete)
    second, to_west, to_east, onward = call(
        middle_kernel, sm(1) + vm(6) + far(5), far(1) + vm(3), [field, edge, edge, plane],
        [VMEM((ROWS, LANES), F32)] + turned + stencil_scratch + stencil_sems, 24 << 20,
        band, *ups, complete, land_sea, rim,
        first, east_coef, north_coef, coriolis_coef, vertical_coef,
    )
    later_rest = step_two(onward + later_near)
    sides = from_sides(to_west, to_east)
    return call(
        last_kernel, sm(1) + vm(4) + far(1), far(1), [field],
        rim_scratch + [stored] * 2 + [dma((PARTS,))] * 2, 8 << 20,
        band, later_near, later_rest, *sides, second,
    )


def solution(mesh):
    return jax.shard_map(
        body,
        mesh=mesh,
        in_specs=(
            P("lev", None, "tile"),
            P("lev", None, "tile"),
            P("lev", None, "tile"),
            P("lev", None, "tile"),
            P("lev", None, "tile"),
            P(None, "tile"),
            P("tile", None, None),
            P("tile", None, None, None),
            P("tile", None, None, None, None),
            P("tile", None, None, None),
            P("tile", None, None, None),
            P("tile", None, None, None),
            P(),
        ),
        out_specs=P("lev", None, "tile"),
        check_vma=False,
    )
```

```python
import jax
import jax.numpy as jnp
from jax import lax
from jax.experimental import pallas as pl
from jax.experimental.pallas import tpu as pltpu
from jax.sharding import PartitionSpec as P

LANES = 128
ROWS = 768
BAND = 8
CAP = 256
OWNERS = 32
BLOCK = 24
CHUNK = 32
LATE_ACCS = 7
EARLY_ACCS = 6
STRIP = 32
UNROLL = 4
PARTS = 6
PART = ROWS // PARTS
PLANES = BAND + 1
LIMIT = 64 << 20
VMEM = pltpu.VMEM
SMEM = pltpu.SMEM
F32 = jnp.float32
BF16 = jnp.bfloat16


def lane_ids():
    return lax.broadcasted_iota(jnp.int32, (STRIP, LANES), 1)


def prepare(band, weight, counts, cell, frac, innovation, kind, level, out):
    z = band[0]
    ids = lax.broadcasted_iota(jnp.int32, (OWNERS, LANES), 1)
    for s in range(2):
        own = lax.broadcasted_iota(jnp.int32, (OWNERS, OWNERS), 0)
        other = lax.broadcasted_iota(jnp.int32, (OWNERS, OWNERS), 1)
        row = jnp.broadcast_to(counts[0, s : s + 1, :].astype(F32), (OWNERS, OWNERS))
        count = jnp.sum(jnp.where(own == other, row, 0.0), 1, keepdims=True)
        out[pl.ds(20 + s, OWNERS, stride=BLOCK), :] = jnp.broadcast_to(count, (OWNERS, LANES))
        for h in range(2):
            part = slice(h * LANES, (h + 1) * LANES)
            t = kind[0, s, :, part]
            at = cell[0, s, :, part]
            scale = jnp.where(t == 0, weight[0], jnp.where(t == 1, weight[1], weight[2]))
            live = (ids + h * LANES).astype(F32) < count
            residual = jnp.where(live, scale * innovation[0, s, :, part], 0.0)
            local = level[0, s, :, part] - z * BAND
            here = (t == 1) & (local >= 0) & (local < BAND)
            keep = (t == 0) | here | ((t == 2) & (z == 0))
            residual = jnp.where(keep, residual, 0.0)
            residual = jnp.where(t == 0, 0.25 * residual, residual)
            target = jnp.where(t == 0, BAND, jnp.where(here, local, 0))
            east = frac[0, s, :, 0, part]
            north = frac[0, s, :, 1, part]
            index = target * ROWS + lax.shift_right_logical(at, 7)
            column = lax.bitwise_and(at, LANES - 1)
            first = s * 8 + h * 4
            values = (column.astype(F32), east, residual * (1.0 - north), residual * north)
            for j, value in enumerate(values):
                out[pl.ds(first + j, OWNERS, stride=BLOCK), :] = value
            out[pl.ds(16 + s * 2 + h, OWNERS, stride=BLOCK), :] = index.astype(F32)
        out[pl.ds(22 + s, OWNERS, stride=BLOCK), :] = jnp.zeros((OWNERS, LANES), F32)


def make_pairs(select, pairs, block, half, at):
    parts = jnp.concatenate(three_parts(block) + [jnp.zeros_like(block)], 0)
    spread = lax.dot_general(
        parts.astype(BF16), select[half], (((0,), (0,)), ((), ())), preferred_element_type=F32
    )
    column, east, south, north = (
        spread[:, j * LANES : (j + 1) * LANES] for j in range(4)
    )
    lanes = lax.broadcasted_iota(jnp.int32, (LANES, LANES), 1).astype(F32)
    weight = jnp.maximum(0.0, 1.0 - jnp.abs((lanes - column) - east))
    pairs[pl.ds(at, LANES, stride=2), :] = weight * south
    pairs[pl.ds(at + 1, LANES, stride=2), :] = weight * north


def spread(s, far_places, slots, select, pairs, places, sem, accs, first_cleared, ready):
    fetch = pltpu.make_async_copy(far_places, places, sem)
    fetch.start()
    row = lax.broadcasted_iota(jnp.int32, (32, 4 * LANES), 0)
    group = lax.shift_right_logical(lax.broadcasted_iota(jnp.int32, (32, 4 * LANES), 1), 7)
    for h in range(2):
        hit = (lax.bitwise_and(row, 7) == group + 4 * h) & (row < 24)
        select[h] = jnp.where(hit, 1.0, 0.0).astype(BF16)
    share = PLANES * ROWS // OWNERS

    def west(o, _):
        for acc in accs[first_cleared:]:
            acc[pl.ds(pl.multiple_of(o * share, 8), share), :] = jnp.zeros((share, LANES), F32)
        block = slots[pl.ds(pl.multiple_of(o * BLOCK + s * 8, 8), 8), :]
        make_pairs(select, pairs, block, 0, o * 2 * CAP)
        return 0

    lax.fori_loop(0, OWNERS, west, 0, unroll=4)
    fetch.wait()

    def most(o, value):
        return jnp.maximum(value, places[o * 8 * LANES + (4 + s) * LANES])

    @pl.when(lax.fori_loop(0, OWNERS, most, jnp.int32(0), unroll=8) > LANES)
    def _():
        def east(o, _):
            block = slots[pl.ds(pl.multiple_of(o * BLOCK + s * 8, 8), 8), :]
            make_pairs(select, pairs, block, 1, o * 2 * CAP + 2 * LANES)
            return 0

        lax.fori_loop(0, OWNERS, east, 0, unroll=8)

    for copy in ready:
        copy.wait()

    def owner(o, _):
        count = places[o * 8 * LANES + (4 + s) * LANES]

        def add(first, size):
            at = o * 8 * LANES + s * CAP + first
            pair = o * 2 * CAP + 2 * first
            for j in range(size):
                acc = accs[j % len(accs)]
                r = places[at + j]
                acc[pl.ds(r, 2), :] = acc[pl.ds(r, 2), :] + pairs[pl.ds(pair + 2 * j, 2), :]

        def wide(c, _):
            add(c * 2 * CHUNK, 2 * CHUNK)
            return 0

        def narrow(c, _):
            add(c * CHUNK, CHUNK)
            return 0

        full = lax.div(count, 2 * CHUNK)
        lax.fori_loop(0, full, wide, 0)
        return lax.fori_loop(2 * full, lax.div(count + (CHUNK - 1), CHUNK), narrow, 0)

    lax.fori_loop(0, OWNERS, owner, 0)


def total_of(accs, plane, at):
    value = accs[0][pl.ds(plane * ROWS + at, STRIP), :]
    for acc in accs[1:]:
        value = value + acc[pl.ds(plane * ROWS + at, STRIP), :]
    return value


def edge_columns(into, lanes, k, value):
    rolled = pltpu.roll(value, 2 * k + 1, 1)
    return jnp.where((lanes == 2 * k) | (lanes == 2 * k + 1), rolled, into)


def send_edges(edges, at, turned, to_west, to_east, part):
    turned[...] = edges[pl.ds(at, LANES), :].T[0:16, :]
    to_west[:, part] = turned[pl.ds(1, BAND, stride=2), :]
    to_east[:, part] = turned[pl.ds(0, BAND, stride=2), :]


def rims(east, coriolis, vertical, land, out, columns):
    lanes = lane_ids()
    for r in range(0, LANES, STRIP):
        rows = slice(r, r + STRIP)
        value = jnp.zeros((STRIP, LANES), F32)
        total = jnp.zeros((STRIP, LANES), F32)
        for k in range(BAND):
            e = east[k, rows, :]
            c = coriolis[k, rows, :]
            value = edge_columns(value, lanes, k, jnp.where(lanes == 0, e - c, e + c))
            total = total + vertical[k, rows, :]
        out[rows, :] = value
        columns[rows, :] = total * land[rows, :].astype(F32)


def row_part(ref, c):
    return ref.at[:, pl.ds(c * PART, PART), :]


def late_kernel(
    far_places, slots, final, land, vertical, rim, masked, sums, to_west, to_east,
    select, pairs, places, edges, turned, v_s, o_s, sem, in_sem, out_sem, *accs,
):
    copies = [
        pltpu.make_async_copy(final.at[k], accs[0].at[pl.ds(k * ROWS, ROWS)], in_sem.at[k])
        for k in range(BAND)
    ]
    copies.append(pltpu.make_async_copy(vertical, v_s, in_sem.at[BAND]))
    for copy in copies:
        copy.start()
    accs[0][pl.ds(BAND * ROWS, ROWS), :] = jnp.zeros((ROWS, LANES), F32)
    spread(1, far_places, slots, select, pairs, places, sem, accs, 1, copies[:BAND])
    copies[BAND].wait()
    lanes = lane_ids()

    def one(i, _):
        at = pl.multiple_of(i * STRIP, STRIP)
        rows = pl.ds(at, STRIP)
        sea = land[rows, :].astype(F32)
        shared = total_of(accs, BAND, at)
        total = jnp.zeros((STRIP, LANES), F32)
        edge = jnp.zeros((STRIP, LANES), F32)
        for k in range(BAND):
            m = sea * (total_of(accs, k, at) + shared)
            o_s[k, rows, :] = m
            total = total + v_s[k, rows, :] * m
            edge = edge_columns(edge, lanes, k, m)
        sums[rows, :] = total
        edges[rows, :] = edge * rim[rows, :]
        return 0

    leaving = []
    for c in range(PARTS):
        lax.fori_loop(c * PART // STRIP, (c + 1) * PART // STRIP, one, 0, unroll=UNROLL)
        copy = pltpu.make_async_copy(row_part(o_s, c), row_part(masked, c), out_sem.at[c])
        copy.start()
        leaving.append(copy)
    for b in range(ROWS // LANES):
        part = slice(b * LANES, (b + 1) * LANES)
        send_edges(edges, b * LANES, turned, to_west, to_east, part)
    for copy in leaving:
        copy.wait()


def fetch_fields(sources, targets, sem):
    copies = []
    for c in range(PARTS):
        row = []
        for j, (source, target) in enumerate(zip(sources, targets)):
            copy = pltpu.make_async_copy(row_part(source, c), row_part(target, c), sem.at[c, j])
            copy.start()
            row.append(copy)
        copies.append(row)
    return copies


def rim_select(select):
    row = lax.broadcasted_iota(jnp.int32, (8 * BAND, BAND * LANES), 0)
    column = lax.broadcasted_iota(jnp.int32, (8 * BAND, BAND * LANES), 1)
    level = lax.shift_right_logical(column, 7)
    lane = lax.bitwise_and(column, LANES - 1)
    side = jnp.where(row < 3 * BAND, LANES - 1, 0)
    hit = (lax.bitwise_and(row, BAND - 1) == level) & (lane == side) & (row < 6 * BAND)
    select[...] = jnp.where(hit, 1.0, 0.0).astype(BF16)


def three_parts(value):
    high = value.astype(BF16).astype(F32)
    rest = value - high
    middle = rest.astype(BF16).astype(F32)
    return [high, middle, rest - middle]


def place_rims(from_east, from_west, select, placed):
    for b in range(placed.shape[0] // LANES):
        part = slice(b * LANES, (b + 1) * LANES)
        east, west = from_east[:, part], from_west[:, part]
        empty = jnp.zeros((2 * BAND, LANES), F32)
        parts = jnp.concatenate(three_parts(east) + three_parts(west) + [empty], 0)
        placed[part, :] = lax.dot_general(
            parts.astype(BF16), select[...], (((0,), (0,)), ((), ())), preferred_element_type=F32
        )


def stencil(copies, masked, east, north, coriolis, vertical, flow, made, prepare_rows, start, added,
            finish, out, out_sem):
    for k in range(BAND):
        flow[k, 0:8, :] = jnp.zeros((8, LANES), F32)
        flow[k, ROWS + 8 : ROWS + 16, :] = jnp.zeros((8, LANES), F32)

    def first(i, _):
        at = pl.multiple_of(i * STRIP, STRIP)
        prepare_rows(at)
        rows = pl.ds(at, STRIP)
        for k in range(BAND):
            value = north[k, rows, :] * masked[k, rows, :]
            flow[k, pl.ds(pl.multiple_of(at + 8, 8), STRIP), :] = value
        return 0

    lanes = lane_ids()

    def second(i, _):
        at = pl.multiple_of(i * STRIP, STRIP)
        rows = pl.ds(at, STRIP)
        below = start(at)
        total = jnp.zeros((STRIP, LANES), F32)
        for k in reversed(range(BAND)):
            m = masked[k, rows, :]
            e = east[k, rows, :] * m
            c = coriolis[k, rows, :] * m
            v = vertical[k, rows, :]
            below = below + v * m
            ahead = jnp.where(lanes == LANES - 1, 0.0, pltpu.roll(e - c, LANES - 1, 1))
            behind = jnp.where(lanes == 0, 0.0, pltpu.roll(e + c, 1, 1))
            across = (
                flow[k, pl.ds(at + 7, STRIP), :]
                + flow[k, pl.ds(at + 9, STRIP), :]
                - 2.0 * flow[k, pl.ds(pl.multiple_of(at + 8, 8), STRIP), :]
            )
            value = m + (ahead + behind - 2.0 * e) + across + below + added(k, at)
            made[k, rows, :] = value
            total = total + v * value
        finish(at, total)
        return 0

    leaving = []
    for c in range(PARTS + 1):
        if c < PARTS:
            for copy in copies[c]:
                copy.wait()
            lax.fori_loop(c * PART // STRIP, (c + 1) * PART // STRIP, first, 0, unroll=UNROLL)
        if c > 0:
            lax.fori_loop((c - 1) * PART // STRIP, c * PART // STRIP, second, 0, unroll=UNROLL)
            copy = pltpu.make_async_copy(
                row_part(made, c - 1), row_part(out, c - 1), out_sem.at[c - 1]
            )
            copy.start()
            leaving.append(copy)
    return leaving


def early_kernel(
    far_places, slots, land, from_east, from_west, masked, east, north, coriolis, vertical,
    out, sums,
    select, pairs, places, rim_picks, placed, m_s, e_s, n_s, c_s, v_s, flow, made,
    sem, in_sem, out_sem, *accs,
):
    copies = fetch_fields(
        (masked, east, north, coriolis, vertical), (m_s, e_s, n_s, c_s, v_s), in_sem
    )
    rim_select(rim_picks)
    place_rims(from_east, from_west, rim_picks, placed)
    spread(0, far_places, slots, select, pairs, places, sem, accs, 0, ())

    def start(at):
        return total_of(accs, BAND, at)

    def added(k, at):
        rows = pl.ds(at, STRIP)
        return total_of(accs, k, at) + placed[rows, k * LANES : (k + 1) * LANES]

    def finish(at, total):
        rows = pl.ds(at, STRIP)
        sums[rows, :] = total * land[rows, :].astype(F32)

    leaving = stencil(
        copies, m_s, e_s, n_s, c_s, v_s, flow, made, lambda at: None, start, added, finish, out, out_sem
    )
    for copy in leaving:
        copy.wait()


def middle_kernel(
    band, one_up, two_up, three_up, complete, land, rim,
    field, east, north, coriolis, vertical, out, to_west, to_east, onward,
    edges, turned, m_s, e_s, n_s, c_s, v_s, flow, made, in_sem, out_sem,
):
    sends = jnp.where(band[0] == 0, 0.0, 1.0)

    copies = fetch_fields(
        (field, east, north, coriolis, vertical), (m_s, e_s, n_s, c_s, v_s), in_sem
    )
    lanes = lane_ids()

    def prepare_rows(at):
        rows = pl.ds(at, STRIP)
        sea = land[rows, :].astype(F32)
        higher = one_up[rows, :] + two_up[rows, :] + three_up[rows, :]
        edge = jnp.zeros((STRIP, LANES), F32)
        for k in range(BAND):
            m = sea * (m_s[k, rows, :] + higher)
            m_s[k, rows, :] = m
            edge = edge_columns(edge, lanes, k, m)
        edges[rows, :] = edge * rim[rows, :]

    def start(at):
        rows = pl.ds(at, STRIP)
        onward[rows, :] = sends * complete[rows, :]
        return jnp.zeros((STRIP, LANES), F32)

    leaving = stencil(
        copies, m_s, e_s, n_s, c_s, v_s, flow, made, prepare_rows, start, lambda k, at: 0.0,
        lambda at, total: None, out, out_sem,
    )
    for b in range(ROWS // LANES):
        part = slice(b * LANES, (b + 1) * LANES)
        send_edges(edges, b * LANES, turned, to_west, to_east, part)
    for copy in leaving:
        copy.wait()


def last_kernel(
    band, near, rest, from_east, from_west, field, out, select, placed, f_s, o_s, in_sem, out_sem
):
    copies = []
    for c in range(PARTS):
        copy = pltpu.make_async_copy(row_part(field, c), row_part(f_s, c), in_sem.at[c])
        copy.start()
        copies.append(copy)
    rim_select(select)
    place_rims(from_east, from_west, select, placed)
    inner = jnp.where(band[0] == 3, 0.0, 1.0)

    def one(i, _):
        rows = pl.ds(pl.multiple_of(i * STRIP, STRIP), STRIP)
        higher = inner * near[rows, :] + rest[rows, :]
        for k in range(BAND):
            rim = placed[rows, k * LANES : (k + 1) * LANES]
            o_s[k, rows, :] = f_s[k, rows, :] + higher + rim
        return 0

    leaving = []
    for c in range(PARTS):
        copies[c].wait()
        lax.fori_loop(c * PART // STRIP, (c + 1) * PART // STRIP, one, 0, unroll=UNROLL)
        copy = pltpu.make_async_copy(row_part(o_s, c), row_part(out, c), out_sem.at[c])
        copy.start()
        leaving.append(copy)
    for copy in leaving:
        copy.wait()


def shape(*dims):
    return jax.ShapeDtypeStruct(dims, F32)


def vm(count):
    return [pl.BlockSpec(memory_space=VMEM)] * count


def sm(count):
    return [pl.BlockSpec(memory_space=SMEM)] * count


def far(count):
    return [pl.BlockSpec(memory_space=pl.ANY)] * count


def fields_by_rows(count):
    return [pl.BlockSpec((BAND, LANES, LANES), lambda i: (0, i, 0))] * count


def planes_by_rows(count):
    return [pl.BlockSpec((LANES, LANES), lambda i: (i, 0))] * count


def call(kernel, ins, outs, shapes, scratch, moved, *args, grid=()):
    many = len(outs) > 1
    return pl.pallas_call(
        kernel,
        grid=grid,
        in_specs=ins,
        out_specs=tuple(outs) if many else outs[0],
        out_shape=tuple(shapes) if many else shapes[0],
        scratch_shapes=scratch,
        compiler_params=pltpu.CompilerParams(vmem_limit_bytes=LIMIT),
        cost_estimate=pl.CostEstimate(flops=moved, bytes_accessed=moved, transcendentals=0),
    )(*args)


def by_core(part, first_core, second_core):
    bands = lax.axis_size("lev")
    pairs = [
        (tile * bands + source, tile * bands + target)
        for tile in range(lax.axis_size("tile"))
        for source, target in (second_core if tile % 2 else first_core)
    ]
    return lax.ppermute(part, ("tile", "lev"), pairs)


def from_deeper(part):
    return (
        lax.ppermute(part, "lev", [(3, 2), (2, 1), (1, 0)]),
        lax.ppermute(part, "lev", [(3, 1), (2, 0)]),
        lax.ppermute(part, "lev", [(3, 0)]),
    )


def step_one(part):
    return by_core(part, ((3, 2), (2, 3), (1, 0)), ((2, 1), (3, 0)))


def step_two(part):
    return by_core(part, ((2, 1), (3, 0)), ((0, 1), (1, 0), (3, 2)))


def from_sides(to_west, to_east):
    count = lax.axis_size("tile")
    return (
        lax.ppermute(to_west, "tile", [((i + 1) % count, i) for i in range(count)]),
        lax.ppermute(to_east, "tile", [(i, (i + 1) % count) for i in range(count)]),
    )


def body(
    final_adjoint,
    east_coef,
    north_coef,
    coriolis_coef,
    vertical_coef,
    land_sea,
    counts,
    obs_cell,
    obs_frac,
    innovation,
    obs_type,
    obs_level,
    type_weight,
):
    band = lax.axis_index("lev").astype(jnp.int32).reshape(1)
    field = shape(BAND, ROWS, LANES)
    plane = shape(ROWS, LANES)
    edge = shape(BAND, ROWS)
    strips = (ROWS // LANES,)
    dma = pltpu.SemaphoreType.DMA
    send = call(
        prepare, sm(2) + vm(6), vm(1), [shape(OWNERS * BLOCK, LANES)], [], 1 << 20,
        band, type_weight, counts, obs_cell, obs_frac, innovation, obs_type, obs_level,
    )
    arrived = lax.all_to_all(
        send.reshape(OWNERS, BLOCK, LANES), "tile", split_axis=0, concat_axis=0, tiled=True
    )
    rim, columns = call(
        rims, fields_by_rows(3) + planes_by_rows(1), planes_by_rows(2), [plane] * 2, [],
        10 << 20, east_coef, coriolis_coef, vertical_coef, land_sea, grid=strips,
    )
    places = arrived[:, 16:24, :].astype(jnp.int32).reshape(-1)
    slots = arrived.reshape(OWNERS * BLOCK, LANES)
    acc = VMEM((PLANES * ROWS + 8, LANES), F32)
    spread_scratch = [
        VMEM((2, 32, 4 * LANES), BF16),
        VMEM((OWNERS * CAP * 2, LANES), F32),
        SMEM((OWNERS * 8 * LANES,), jnp.int32),
    ]
    turned = [VMEM((2 * BAND, LANES), F32)]
    masked, sums, to_west, to_east = call(
        late_kernel, far(1) + vm(1) + far(1) + vm(1) + far(1) + vm(1), far(1) + vm(3),
        [field, plane, edge, edge],
        spread_scratch + [VMEM((ROWS, LANES), F32)] + turned + [VMEM((BAND, ROWS, LANES), F32)] * 2
        + [dma, dma((BAND + 1,)), dma((PARTS,))] + [acc] * LATE_ACCS,
        10 << 20,
        places, slots, final_adjoint, land_sea, vertical_coef, rim,
    )
    sides = from_sides(to_west, to_east)
    ups = from_deeper(sums)
    stored = VMEM((BAND, ROWS, LANES), F32)
    wide = VMEM((BAND, ROWS + 16, LANES), F32)
    stencil_scratch = [stored] * 5 + [wide, stored]
    stencil_sems = [dma((PARTS, 5)), dma((PARTS,))]
    rim_scratch = [VMEM((8 * BAND, BAND * LANES), BF16), VMEM((ROWS, BAND * LANES), F32)]
    first, later = call(
        early_kernel, far(1) + vm(4) + far(5), far(1) + vm(1), [field, plane],
        spread_scratch + rim_scratch + stencil_scratch + [dma] + stencil_sems
        + [acc] * EARLY_ACCS,
        40 << 20,
        places, slots, land_sea, *sides,
        masked, east_coef, north_coef, coriolis_coef, vertical_coef,
    )
    complete = later + columns * (ups[0] + ups[1] + ups[2])
    later_near = step_one(complete)
    second, to_west, to_east, onward = call(
        middle_kernel, sm(1) + vm(6) + far(5), far(1) + vm(3), [field, edge, edge, plane],
        [VMEM((ROWS, LANES), F32)] + turned + stencil_scratch + stencil_sems, 24 << 20,
        band, *ups, complete, land_sea, rim,
        first, east_coef, north_coef, coriolis_coef, vertical_coef,
    )
    later_rest = step_two(onward + later_near)
    sides = from_sides(to_west, to_east)
    return call(
        last_kernel, sm(1) + vm(4) + far(1), far(1), [field],
        rim_scratch + [stored] * 2 + [dma((PARTS,))] * 2, 8 << 20,
        band, later_near, later_rest, *sides, second,
    )


def solution(mesh):
    return jax.shard_map(
        body,
        mesh=mesh,
        in_specs=(
            P("lev", None, "tile"),
            P("lev", None, "tile"),
            P("lev", None, "tile"),
            P("lev", None, "tile"),
            P("lev", None, "tile"),
            P(None, "tile"),
            P("tile", None, None),
            P("tile", None, None, None),
            P("tile", None, None, None, None),
            P("tile", None, None, None),
            P("tile", None, None, None),
            P("tile", None, None, None),
            P(),
        ),
        out_specs=P("lev", None, "tile"),
        check_vma=False,
    )
```

```python
import jax
import jax.numpy as jnp
from jax import lax
from jax.experimental import pallas as pl
from jax.experimental.pallas import tpu as pltpu
from jax.sharding import PartitionSpec as P

LANES = 128
ROWS = 768
BAND = 8
CAP = 256
OWNERS = 32
BLOCK = 24
CHUNK = 32
LATE_ACCS = 7
EARLY_ACCS = 6
STRIP = 32
UNROLL = 4
PARTS = 6
PART = ROWS // PARTS
PLANES = BAND + 1
LIMIT = 63 << 20
VMEM = pltpu.VMEM
SMEM = pltpu.SMEM
F32 = jnp.float32
BF16 = jnp.bfloat16


def lane_ids():
    return lax.broadcasted_iota(jnp.int32, (STRIP, LANES), 1)


def prepare(band, weight, counts, cell, frac, innovation, kind, level, out):
    z = band[0]
    ids = lax.broadcasted_iota(jnp.int32, (OWNERS, LANES), 1)
    for s in range(2):
        own = lax.broadcasted_iota(jnp.int32, (OWNERS, OWNERS), 0)
        other = lax.broadcasted_iota(jnp.int32, (OWNERS, OWNERS), 1)
        row = jnp.broadcast_to(counts[0, s : s + 1, :].astype(F32), (OWNERS, OWNERS))
        count = jnp.sum(jnp.where(own == other, row, 0.0), 1, keepdims=True)
        out[pl.ds(20 + s, OWNERS, stride=BLOCK), :] = jnp.broadcast_to(count, (OWNERS, LANES))
        for h in range(2):
            part = slice(h * LANES, (h + 1) * LANES)
            t = kind[0, s, :, part]
            at = cell[0, s, :, part]
            scale = jnp.where(t == 0, weight[0], jnp.where(t == 1, weight[1], weight[2]))
            live = (ids + h * LANES).astype(F32) < count
            residual = jnp.where(live, scale * innovation[0, s, :, part], 0.0)
            local = level[0, s, :, part] - z * BAND
            here = (t == 1) & (local >= 0) & (local < BAND)
            keep = (t == 0) | here | ((t == 2) & (z == 0))
            residual = jnp.where(keep, residual, 0.0)
            residual = jnp.where(t == 0, 0.25 * residual, residual)
            target = jnp.where(t == 0, BAND, jnp.where(here, local, 0))
            east = frac[0, s, :, 0, part]
            north = frac[0, s, :, 1, part]
            index = target * ROWS + lax.shift_right_logical(at, 7)
            column = lax.bitwise_and(at, LANES - 1)
            first = s * 8 + h * 4
            values = (column.astype(F32), east, residual * (1.0 - north), residual * north)
            for j, value in enumerate(values):
                out[pl.ds(first + j, OWNERS, stride=BLOCK), :] = value
            out[pl.ds(16 + s * 2 + h, OWNERS, stride=BLOCK), :] = index.astype(F32)
        out[pl.ds(22 + s, OWNERS, stride=BLOCK), :] = jnp.zeros((OWNERS, LANES), F32)


def make_pairs(select, pairs, block, half, at):
    parts = jnp.concatenate(three_parts(block) + [jnp.zeros_like(block)], 0)
    spread = lax.dot_general(
        parts.astype(BF16), select[half], (((0,), (0,)), ((), ())), preferred_element_type=F32
    )
    column, east, south, north = (
        spread[:, j * LANES : (j + 1) * LANES] for j in range(4)
    )
    lanes = lax.broadcasted_iota(jnp.int32, (LANES, LANES), 1).astype(F32)
    weight = jnp.maximum(0.0, 1.0 - jnp.abs((lanes - column) - east))
    pairs[pl.ds(at, LANES, stride=2), :] = weight * south
    pairs[pl.ds(at + 1, LANES, stride=2), :] = weight * north


def spread(s, far_places, slots, select, pairs, places, sem, accs, first_cleared, ready):
    fetch = pltpu.make_async_copy(far_places, places, sem)
    fetch.start()
    row = lax.broadcasted_iota(jnp.int32, (32, 4 * LANES), 0)
    group = lax.shift_right_logical(lax.broadcasted_iota(jnp.int32, (32, 4 * LANES), 1), 7)
    for h in range(2):
        hit = (lax.bitwise_and(row, 7) == group + 4 * h) & (row < 24)
        select[h] = jnp.where(hit, 1.0, 0.0).astype(BF16)
    share = PLANES * ROWS // OWNERS

    def west(o, _):
        for acc in accs[first_cleared:]:
            acc[pl.ds(pl.multiple_of(o * share, 8), share), :] = jnp.zeros((share, LANES), F32)
        block = slots[pl.ds(pl.multiple_of(o * BLOCK + s * 8, 8), 8), :]
        make_pairs(select, pairs, block, 0, o * 2 * CAP)
        return 0

    lax.fori_loop(0, OWNERS, west, 0, unroll=4)
    fetch.wait()

    def most(o, value):
        return jnp.maximum(value, places[o * 8 * LANES + (4 + s) * LANES])

    @pl.when(lax.fori_loop(0, OWNERS, most, jnp.int32(0), unroll=8) > LANES)
    def _():
        def east(o, _):
            block = slots[pl.ds(pl.multiple_of(o * BLOCK + s * 8, 8), 8), :]
            make_pairs(select, pairs, block, 1, o * 2 * CAP + 2 * LANES)
            return 0

        lax.fori_loop(0, OWNERS, east, 0, unroll=8)

    for copy in ready:
        copy.wait()

    def owner(o, _):
        count = places[o * 8 * LANES + (4 + s) * LANES]

        def add(first, size):
            at = o * 8 * LANES + s * CAP + first
            pair = o * 2 * CAP + 2 * first
            for j in range(size):
                acc = accs[j % len(accs)]
                r = places[at + j]
                acc[pl.ds(r, 2), :] = acc[pl.ds(r, 2), :] + pairs[pl.ds(pair + 2 * j, 2), :]

        def wide(c, _):
            add(c * 2 * CHUNK, 2 * CHUNK)
            return 0

        def narrow(c, _):
            add(c * CHUNK, CHUNK)
            return 0

        full = lax.div(count, 2 * CHUNK)
        lax.fori_loop(0, full, wide, 0)
        return lax.fori_loop(2 * full, lax.div(count + (CHUNK - 1), CHUNK), narrow, 0)

    lax.fori_loop(0, OWNERS, owner, 0)


def total_of(accs, plane, at):
    value = accs[0][pl.ds(plane * ROWS + at, STRIP), :]
    for acc in accs[1:]:
        value = value + acc[pl.ds(plane * ROWS + at, STRIP), :]
    return value


def edge_columns(into, lanes, k, value):
    rolled = pltpu.roll(value, 2 * k + 1, 1)
    return jnp.where((lanes == 2 * k) | (lanes == 2 * k + 1), rolled, into)


def send_edges(edges, at, turned, to_west, to_east, part):
    turned[...] = edges[pl.ds(at, LANES), :].T[0:16, :]
    to_west[:, part] = turned[pl.ds(1, BAND, stride=2), :]
    to_east[:, part] = turned[pl.ds(0, BAND, stride=2), :]


def rims(east, coriolis, vertical, land, out, columns):
    lanes = lane_ids()
    for r in range(0, LANES, STRIP):
        rows = slice(r, r + STRIP)
        value = jnp.zeros((STRIP, LANES), F32)
        total = jnp.zeros((STRIP, LANES), F32)
        for k in range(BAND):
            e = east[k, rows, :]
            c = coriolis[k, rows, :]
            value = edge_columns(value, lanes, k, jnp.where(lanes == 0, e - c, e + c))
            total = total + vertical[k, rows, :]
        out[rows, :] = value
        columns[rows, :] = total * land[rows, :].astype(F32)


def row_part(ref, c):
    return ref.at[:, pl.ds(c * PART, PART), :]


def late_kernel(
    far_places, slots, final, land, vertical, rim, masked, sums, to_west, to_east,
    select, pairs, places, edges, turned, v_s, o_s, sem, in_sem, out_sem, *accs,
):
    copies = [
        pltpu.make_async_copy(final.at[k], accs[0].at[pl.ds(k * ROWS, ROWS)], in_sem.at[k])
        for k in range(BAND)
    ]
    copies.append(pltpu.make_async_copy(vertical, v_s, in_sem.at[BAND]))
    for copy in copies:
        copy.start()
    accs[0][pl.ds(BAND * ROWS, ROWS), :] = jnp.zeros((ROWS, LANES), F32)
    spread(1, far_places, slots, select, pairs, places, sem, accs, 1, copies[:BAND])
    copies[BAND].wait()
    lanes = lane_ids()

    def one(i, _):
        at = pl.multiple_of(i * STRIP, STRIP)
        rows = pl.ds(at, STRIP)
        sea = land[rows, :].astype(F32)
        shared = total_of(accs, BAND, at)
        total = jnp.zeros((STRIP, LANES), F32)
        edge = jnp.zeros((STRIP, LANES), F32)
        for k in range(BAND):
            m = sea * (total_of(accs, k, at) + shared)
            o_s[k, rows, :] = m
            total = total + v_s[k, rows, :] * m
            edge = edge_columns(edge, lanes, k, m)
        sums[rows, :] = total
        edges[rows, :] = edge * rim[rows, :]
        return 0

    leaving = []
    for c in range(PARTS):
        lax.fori_loop(c * PART // STRIP, (c + 1) * PART // STRIP, one, 0, unroll=UNROLL)
        copy = pltpu.make_async_copy(row_part(o_s, c), row_part(masked, c), out_sem.at[c])
        copy.start()
        leaving.append(copy)
    for b in range(ROWS // LANES):
        part = slice(b * LANES, (b + 1) * LANES)
        send_edges(edges, b * LANES, turned, to_west, to_east, part)
    for copy in leaving:
        copy.wait()


def fetch_fields(sources, targets, sem):
    copies = []
    for c in range(PARTS):
        row = []
        for j, (source, target) in enumerate(zip(sources, targets)):
            copy = pltpu.make_async_copy(row_part(source, c), row_part(target, c), sem.at[c, j])
            copy.start()
            row.append(copy)
        copies.append(row)
    return copies


def rim_select(select):
    row = lax.broadcasted_iota(jnp.int32, (8 * BAND, BAND * LANES), 0)
    column = lax.broadcasted_iota(jnp.int32, (8 * BAND, BAND * LANES), 1)
    level = lax.shift_right_logical(column, 7)
    lane = lax.bitwise_and(column, LANES - 1)
    side = jnp.where(row < 3 * BAND, LANES - 1, 0)
    hit = (lax.bitwise_and(row, BAND - 1) == level) & (lane == side) & (row < 6 * BAND)
    select[...] = jnp.where(hit, 1.0, 0.0).astype(BF16)


def three_parts(value):
    high = value.astype(BF16).astype(F32)
    rest = value - high
    middle = rest.astype(BF16).astype(F32)
    return [high, middle, rest - middle]


def place_rims(from_east, from_west, select, placed):
    for b in range(placed.shape[0] // LANES):
        part = slice(b * LANES, (b + 1) * LANES)
        east, west = from_east[:, part], from_west[:, part]
        empty = jnp.zeros((2 * BAND, LANES), F32)
        parts = jnp.concatenate(three_parts(east) + three_parts(west) + [empty], 0)
        placed[part, :] = lax.dot_general(
            parts.astype(BF16), select[...], (((0,), (0,)), ((), ())), preferred_element_type=F32
        )


def stencil(copies, masked, east, north, coriolis, vertical, flow, made, prepare_rows, start, added,
            finish, out, out_sem):
    for k in range(BAND):
        flow[k, 0:8, :] = jnp.zeros((8, LANES), F32)
        flow[k, ROWS + 8 : ROWS + 16, :] = jnp.zeros((8, LANES), F32)

    def first(i, _):
        at = pl.multiple_of(i * STRIP, STRIP)
        prepare_rows(at)
        rows = pl.ds(at, STRIP)
        for k in range(BAND):
            value = north[k, rows, :] * masked[k, rows, :]
            flow[k, pl.ds(pl.multiple_of(at + 8, 8), STRIP), :] = value
        return 0

    lanes = lane_ids()

    def second(i, _):
        at = pl.multiple_of(i * STRIP, STRIP)
        rows = pl.ds(at, STRIP)
        below = start(at)
        total = jnp.zeros((STRIP, LANES), F32)
        for k in reversed(range(BAND)):
            m = masked[k, rows, :]
            e = east[k, rows, :] * m
            c = coriolis[k, rows, :] * m
            v = vertical[k, rows, :]
            below = below + v * m
            ahead = jnp.where(lanes == LANES - 1, 0.0, pltpu.roll(e - c, LANES - 1, 1))
            behind = jnp.where(lanes == 0, 0.0, pltpu.roll(e + c, 1, 1))
            across = (
                flow[k, pl.ds(at + 7, STRIP), :]
                + flow[k, pl.ds(at + 9, STRIP), :]
                - 2.0 * flow[k, pl.ds(pl.multiple_of(at + 8, 8), STRIP), :]
            )
            value = m + (ahead + behind - 2.0 * e) + across + below + added(k, at)
            made[k, rows, :] = value
            total = total + v * value
        finish(at, total)
        return 0

    leaving = []
    for c in range(PARTS + 1):
        if c < PARTS:
            for copy in copies[c]:
                copy.wait()
            lax.fori_loop(c * PART // STRIP, (c + 1) * PART // STRIP, first, 0, unroll=UNROLL)
        if c > 0:
            lax.fori_loop((c - 1) * PART // STRIP, c * PART // STRIP, second, 0, unroll=UNROLL)
            copy = pltpu.make_async_copy(
                row_part(made, c - 1), row_part(out, c - 1), out_sem.at[c - 1]
            )
            copy.start()
            leaving.append(copy)
    return leaving


def early_kernel(
    far_places, slots, land, from_east, from_west, masked, east, north, coriolis, vertical,
    out, sums,
    select, pairs, places, rim_picks, placed, m_s, e_s, n_s, c_s, v_s, flow, made,
    sem, in_sem, out_sem, *accs,
):
    copies = fetch_fields(
        (masked, east, north, coriolis, vertical), (m_s, e_s, n_s, c_s, v_s), in_sem
    )
    rim_select(rim_picks)
    place_rims(from_east, from_west, rim_picks, placed)
    spread(0, far_places, slots, select, pairs, places, sem, accs, 0, ())

    def start(at):
        return total_of(accs, BAND, at)

    def added(k, at):
        rows = pl.ds(at, STRIP)
        return total_of(accs, k, at) + placed[rows, k * LANES : (k + 1) * LANES]

    def finish(at, total):
        rows = pl.ds(at, STRIP)
        sums[rows, :] = total * land[rows, :].astype(F32)

    leaving = stencil(
        copies, m_s, e_s, n_s, c_s, v_s, flow, made, lambda at: None, start, added, finish, out, out_sem
    )
    for copy in leaving:
        copy.wait()


def middle_kernel(
    band, one_up, two_up, three_up, complete, land, rim,
    field, east, north, coriolis, vertical, out, to_west, to_east, onward,
    edges, turned, m_s, e_s, n_s, c_s, v_s, flow, made, in_sem, out_sem,
):
    sends = jnp.where(band[0] == 0, 0.0, 1.0)

    copies = fetch_fields(
        (field, east, north, coriolis, vertical), (m_s, e_s, n_s, c_s, v_s), in_sem
    )
    lanes = lane_ids()

    def prepare_rows(at):
        rows = pl.ds(at, STRIP)
        sea = land[rows, :].astype(F32)
        higher = one_up[rows, :] + two_up[rows, :] + three_up[rows, :]
        edge = jnp.zeros((STRIP, LANES), F32)
        for k in range(BAND):
            m = sea * (m_s[k, rows, :] + higher)
            m_s[k, rows, :] = m
            edge = edge_columns(edge, lanes, k, m)
        edges[rows, :] = edge * rim[rows, :]

    def start(at):
        rows = pl.ds(at, STRIP)
        onward[rows, :] = sends * complete[rows, :]
        return jnp.zeros((STRIP, LANES), F32)

    leaving = stencil(
        copies, m_s, e_s, n_s, c_s, v_s, flow, made, prepare_rows, start, lambda k, at: 0.0,
        lambda at, total: None, out, out_sem,
    )
    for b in range(ROWS // LANES):
        part = slice(b * LANES, (b + 1) * LANES)
        send_edges(edges, b * LANES, turned, to_west, to_east, part)
    for copy in leaving:
        copy.wait()


def last_kernel(
    band, near, rest, from_east, from_west, field, out, select, placed, f_s, o_s, in_sem, out_sem
):
    copies = []
    for c in range(PARTS):
        copy = pltpu.make_async_copy(row_part(field, c), row_part(f_s, c), in_sem.at[c])
        copy.start()
        copies.append(copy)
    rim_select(select)
    place_rims(from_east, from_west, select, placed)
    inner = jnp.where(band[0] == 3, 0.0, 1.0)

    def one(i, _):
        rows = pl.ds(pl.multiple_of(i * STRIP, STRIP), STRIP)
        higher = inner * near[rows, :] + rest[rows, :]
        for k in range(BAND):
            rim = placed[rows, k * LANES : (k + 1) * LANES]
            o_s[k, rows, :] = f_s[k, rows, :] + higher + rim
        return 0

    leaving = []
    for c in range(PARTS):
        copies[c].wait()
        lax.fori_loop(c * PART // STRIP, (c + 1) * PART // STRIP, one, 0, unroll=UNROLL)
        copy = pltpu.make_async_copy(row_part(o_s, c), row_part(out, c), out_sem.at[c])
        copy.start()
        leaving.append(copy)
    for copy in leaving:
        copy.wait()


def shape(*dims):
    return jax.ShapeDtypeStruct(dims, F32)


def vm(count):
    return [pl.BlockSpec(memory_space=VMEM)] * count


def sm(count):
    return [pl.BlockSpec(memory_space=SMEM)] * count


def far(count):
    return [pl.BlockSpec(memory_space=pl.ANY)] * count


def fields_by_rows(count):
    return [pl.BlockSpec((BAND, LANES, LANES), lambda i: (0, i, 0))] * count


def planes_by_rows(count):
    return [pl.BlockSpec((LANES, LANES), lambda i: (i, 0))] * count


def call(kernel, ins, outs, shapes, scratch, moved, *args, grid=()):
    many = len(outs) > 1
    return pl.pallas_call(
        kernel,
        grid=grid,
        in_specs=ins,
        out_specs=tuple(outs) if many else outs[0],
        out_shape=tuple(shapes) if many else shapes[0],
        scratch_shapes=scratch,
        compiler_params=pltpu.CompilerParams(vmem_limit_bytes=LIMIT),
        cost_estimate=pl.CostEstimate(flops=moved, bytes_accessed=moved, transcendentals=0),
    )(*args)


def by_core(part, first_core, second_core):
    bands = lax.axis_size("lev")
    pairs = [
        (tile * bands + source, tile * bands + target)
        for tile in range(lax.axis_size("tile"))
        for source, target in (second_core if tile % 2 else first_core)
    ]
    return lax.ppermute(part, ("tile", "lev"), pairs)


def from_deeper(part):
    return (
        lax.ppermute(part, "lev", [(3, 2), (2, 1), (1, 0)]),
        lax.ppermute(part, "lev", [(3, 1), (2, 0)]),
        lax.ppermute(part, "lev", [(3, 0)]),
    )


def step_one(part):
    return by_core(part, ((3, 2), (2, 3), (1, 0)), ((2, 1), (3, 0)))


def step_two(part):
    return by_core(part, ((2, 1), (3, 0)), ((0, 1), (1, 0), (3, 2)))


def from_sides(to_west, to_east):
    count = lax.axis_size("tile")
    return (
        lax.ppermute(to_west, "tile", [((i + 1) % count, i) for i in range(count)]),
        lax.ppermute(to_east, "tile", [(i, (i + 1) % count) for i in range(count)]),
    )


def body(
    final_adjoint,
    east_coef,
    north_coef,
    coriolis_coef,
    vertical_coef,
    land_sea,
    counts,
    obs_cell,
    obs_frac,
    innovation,
    obs_type,
    obs_level,
    type_weight,
):
    band = lax.axis_index("lev").astype(jnp.int32).reshape(1)
    field = shape(BAND, ROWS, LANES)
    plane = shape(ROWS, LANES)
    edge = shape(BAND, ROWS)
    strips = (ROWS // LANES,)
    dma = pltpu.SemaphoreType.DMA
    send = call(
        prepare, sm(2) + vm(6), vm(1), [shape(OWNERS * BLOCK, LANES)], [], 1 << 20,
        band, type_weight, counts, obs_cell, obs_frac, innovation, obs_type, obs_level,
    )
    arrived = lax.all_to_all(
        send.reshape(OWNERS, BLOCK, LANES), "tile", split_axis=0, concat_axis=0, tiled=True
    )
    rim, columns = call(
        rims, fields_by_rows(3) + planes_by_rows(1), planes_by_rows(2), [plane] * 2, [],
        10 << 20, east_coef, coriolis_coef, vertical_coef, land_sea, grid=strips,
    )
    places = arrived[:, 16:24, :].astype(jnp.int32).reshape(-1)
    slots = arrived.reshape(OWNERS * BLOCK, LANES)
    acc = VMEM((PLANES * ROWS + 8, LANES), F32)
    spread_scratch = [
        VMEM((2, 32, 4 * LANES), BF16),
        VMEM((OWNERS * CAP * 2, LANES), F32),
        SMEM((OWNERS * 8 * LANES,), jnp.int32),
    ]
    turned = [VMEM((2 * BAND, LANES), F32)]
    masked, sums, to_west, to_east = call(
        late_kernel, far(1) + vm(1) + far(1) + vm(1) + far(1) + vm(1), far(1) + vm(3),
        [field, plane, edge, edge],
        spread_scratch + [VMEM((ROWS, LANES), F32)] + turned + [VMEM((BAND, ROWS, LANES), F32)] * 2
        + [dma, dma((BAND + 1,)), dma((PARTS,))] + [acc] * LATE_ACCS,
        10 << 20,
        places, slots, final_adjoint, land_sea, vertical_coef, rim,
    )
    sides = from_sides(to_west, to_east)
    ups = from_deeper(sums)
    stored = VMEM((BAND, ROWS, LANES), F32)
    wide = VMEM((BAND, ROWS + 16, LANES), F32)
    stencil_scratch = [stored] * 5 + [wide, stored]
    stencil_sems = [dma((PARTS, 5)), dma((PARTS,))]
    rim_scratch = [VMEM((8 * BAND, BAND * LANES), BF16), VMEM((ROWS, BAND * LANES), F32)]
    first, later = call(
        early_kernel, far(1) + vm(4) + far(5), far(1) + vm(1), [field, plane],
        spread_scratch + rim_scratch + stencil_scratch + [dma] + stencil_sems
        + [acc] * EARLY_ACCS,
        40 << 20,
        places, slots, land_sea, *sides,
        masked, east_coef, north_coef, coriolis_coef, vertical_coef,
    )
    complete = later + columns * (ups[0] + ups[1] + ups[2])
    later_near = step_one(complete)
    second, to_west, to_east, onward = call(
        middle_kernel, sm(1) + vm(6) + far(5), far(1) + vm(3), [field, edge, edge, plane],
        [VMEM((ROWS, LANES), F32)] + turned + stencil_scratch + stencil_sems, 24 << 20,
        band, *ups, complete, land_sea, rim,
        first, east_coef, north_coef, coriolis_coef, vertical_coef,
    )
    later_rest = step_two(onward + later_near)
    sides = from_sides(to_west, to_east)
    return call(
        last_kernel, sm(1) + vm(4) + far(1), far(1), [field],
        rim_scratch + [stored] * 2 + [dma((PARTS,))] * 2, 8 << 20,
        band, later_near, later_rest, *sides, second,
    )


def solution(mesh):
    return jax.shard_map(
        body,
        mesh=mesh,
        in_specs=(
            P("lev", None, "tile"),
            P("lev", None, "tile"),
            P("lev", None, "tile"),
            P("lev", None, "tile"),
            P("lev", None, "tile"),
            P(None, "tile"),
            P("tile", None, None),
            P("tile", None, None, None),
            P("tile", None, None, None, None),
            P("tile", None, None, None),
            P("tile", None, None, None),
            P("tile", None, None, None),
            P(),
        ),
        out_specs=P("lev", None, "tile"),
        check_vma=False,
    )
```
